32 devices in a mesh: dp: 2 (over x), ctx: 4 (over y, core), seq: 4 (over z).
Axes of the slice: x: 2, y: 2, z: 4, core: 2. Of those that a mesh axis runs over, the one named last changes fastest.
Arguments:
- inputs: bfloat16 [4, 1024, 2304], P('dp', ('ctx', 'seq')), may hold values from -6 to 6
- positions: int32 [4, 1024], P('dp', 'ctx'), may hold values from 0 to 1023, as said below
- query_weight: bfloat16 [2304, 2048], P(('dp', 'ctx'), 'seq'), may hold values from -0.25 to 0.25
- key_weight: bfloat16 [2304, 1024], P(('dp', 'ctx', 'seq')), may hold values from -0.25 to 0.25
- value_weight: bfloat16 [2304, 1024], P(('dp', 'ctx', 'seq')), may hold values from -0.125 to 0.125
- output_weight: bfloat16 [2048, 2304], P('seq', ('dp', 'ctx')), may hold values from -0.125 to 0.125
- gate_weight: bfloat16 [2304, 9216], P(('dp', 'ctx'), 'seq'), may hold values from -0.125 to 0.125
- up_weight: bfloat16 [2304, 9216], P(('dp', 'ctx'), 'seq'), may hold values from -0.125 to 0.125
- down_weight: bfloat16 [9216, 2304], P('seq', ('dp', 'ctx')), may hold values from -0.0625 to 0.0625
- pre_attn_gain: bfloat16 [2304], P(('dp', 'ctx')), may hold values from 0.099609375 to 1.8984375
- post_attn_gain: bfloat16 [2304], P(('dp', 'ctx')), may hold values from 0.099609375 to 1.8984375
- pre_ffn_gain: bfloat16 [2304], P(('dp', 'ctx')), may hold values from 0.099609375 to 1.8984375
- post_ffn_gain: bfloat16 [2304], P(('dp', 'ctx')), may hold values from 0.099609375 to 1.8984375
- cotangent: bfloat16 [4, 1024, 2304], P('dp', ('ctx', 'seq')), may hold values from -6 to 6
Outputs:
- layer_output: bfloat16 [4, 1024, 2304], P('dp', ('ctx', 'seq'))
- input_grad: bfloat16 [4, 1024, 2304], P('dp', ('ctx', 'seq'))
- grad_query: float32 [2304, 2048], P(('dp', 'ctx'), 'seq')
- grad_key: float32 [2304, 1024], P(('dp', 'ctx', 'seq'))
- grad_value: float32 [2304, 1024], P(('dp', 'ctx', 'seq'))
- grad_output: float32 [2048, 2304], P('seq', ('dp', 'ctx'))
- grad_gate: float32 [2304, 9216], P(('dp', 'ctx'), 'seq')
- grad_up: float32 [2304, 9216], P(('dp', 'ctx'), 'seq')
- grad_down: float32 [9216, 2304], P('seq', ('dp', 'ctx'))
- grad_pre_attn: float32 [2304], P(('dp', 'ctx', 'seq'))
- grad_post_attn: float32 [2304], P(('dp', 'ctx', 'seq'))
- grad_pre_ffn: float32 [2304], P(('dp', 'ctx', 'seq'))
- grad_post_ffn: float32 [2304], P(('dp', 'ctx', 'seq'))
The draws below stay inside these ranges and needn't reach their ends.
Inputs may be any that keep to these rules, and one draw needn't show every extreme that they name: Within each sequence positions count 0, 1, 2, ... and restart at 0 where a new document begins; a sequence holds 1 to 4 documents and the first sequence is a single document.
All inputs are finite; a program needn't handle non-finite values.
Results may differ from the reference program's by a relative error of at most 0.023.
The reference program's roundings to bfloat16 on the way count: a program that leaves them out, or rounds other values in their place, can miss the bound.
Values may be sent and summed in bfloat16 or wider, within the bound.
No kernel may reach another device: no remote copies, remote signals or barrier semaphores. Data moves between devices by JAX's collectives and lax.ppermute only.
A program may use at most 256 MiB of HBM per device.

```python
import math
import jax
import jax.numpy as jnp
from jax import lax

MODEL_WIDTH = 2304
QUERY_HEAD_COUNT = 8
KEY_VALUE_HEADS = 4
HEAD_SIZE = 256
FF = 9216
SEQS = 4
LEN = 1024
QW = 2048
KW = 1024


def draw_positions(key, part):
    cuts = jax.random.randint(key, (SEQS, 3), 1, LEN)
    leading = jnp.arange(SEQS)[:, None] == 0
    cuts = jnp.where(leading, 0, cuts)
    index = jnp.arange(LEN)
    starts = jnp.max(jnp.where(cuts[:, :, None] <= index[None, None, :], cuts[:, :, None], 0), axis=1)
    return (index[None, :] - starts).astype(jnp.int32)


def steps_of(stream_key, extent, cuts, low, top_value):
    level = 1.0
    for axis_at, parts in cuts:
        heights = jax.random.uniform(jax.random.fold_in(jax.random.fold_in(stream_key, 6), axis_at), (parts,), jnp.float32, low / len(cuts), top_value / len(cuts))
        level = level * jnp.repeat(jnp.exp(heights), extent[axis_at] // parts).reshape((-1,) + (1,) * (len(extent) - 1 - axis_at))
    return level


def normal_values(stream_key, extent, width, limit, shards=(), kind=jnp.bfloat16):
    values = jax.random.normal(stream_key, extent, jnp.float32) * width
    if len(shards) > 0:
        values = steps_of(stream_key, extent, shards, -0.22, 0.18) * values
    return jnp.clip(values, min=-limit, max=limit).astype(kind)


def setup_inputs(seed: int = 0) -> dict:
    streams_of = jax.random.split(jax.random.key(seed), 15)
    return {
        "inputs": normal_values(streams_of[0], (SEQS, LEN, MODEL_WIDTH), 1.0, 6.0, ((0, 2), (1, 16))),
        "positions": draw_positions(jax.random.fold_in(streams_of[14], 71), 0),
        "query_weight": normal_values(streams_of[2], (MODEL_WIDTH, QW), (MODEL_WIDTH // 4) ** -0.5, 0.25, ((0, 8), (1, 4))),
        "key_weight": normal_values(streams_of[3], (MODEL_WIDTH, KW), (MODEL_WIDTH // 4) ** -0.5, 0.25, ((0, 32),)),
        "value_weight": normal_values(streams_of[4], (MODEL_WIDTH, KW), MODEL_WIDTH ** -0.5, 0.125, ((0, 32),)),
        "output_weight": normal_values(streams_of[5], (QW, MODEL_WIDTH), QW ** -0.5, 0.125, ((0, 4), (1, 8))),
        "gate_weight": normal_values(streams_of[6], (MODEL_WIDTH, FF), MODEL_WIDTH ** -0.5, 0.125, ((0, 8), (1, 4))),
        "up_weight": normal_values(streams_of[7], (MODEL_WIDTH, FF), MODEL_WIDTH ** -0.5, 0.125, ((0, 8), (1, 4))),
        "down_weight": normal_values(streams_of[8], (FF, MODEL_WIDTH), FF ** -0.5, 0.0625, ((0, 4), (1, 8))),
        "pre_attn_gain": jnp.clip(1.0 + 0.18 * jax.random.normal(streams_of[9], (MODEL_WIDTH,), jnp.float32), 0.099609375, 1.8984375).astype(jnp.bfloat16),
        "post_attn_gain": jnp.clip(1.0 + 0.18 * jax.random.normal(streams_of[10], (MODEL_WIDTH,), jnp.float32), 0.099609375, 1.8984375).astype(jnp.bfloat16),
        "pre_ffn_gain": jnp.clip(1.0 + 0.18 * jax.random.normal(streams_of[11], (MODEL_WIDTH,), jnp.float32), 0.099609375, 1.8984375).astype(jnp.bfloat16),
        "post_ffn_gain": jnp.clip(1.0 + 0.18 * jax.random.normal(streams_of[12], (MODEL_WIDTH,), jnp.float32), 0.099609375, 1.8984375).astype(jnp.bfloat16),
        "cotangent": normal_values(streams_of[13], (SEQS, LEN, MODEL_WIDTH), 1.0, 6.0, ((0, 2), (1, 16))),
    }


EPS = 1e-06
CAP = 50.0
BASE = 10000.0

@jax.custom_vjp
def low(v):
    return lax.optimization_barrier(v.astype(jnp.bfloat16)).astype(jnp.float32)

@jax.custom_vjp
def low_back(v):
    return v

def low_keep(v):
    return (low(v), None)

def low_pass(kept, grad):
    return (grad,)

def back_keep(v):
    return (v, None)

def back_low(kept, grad):
    return (low(grad),)
low.defvjp(low_keep, low_pass)
low_back.defvjp(back_keep, back_low)

def matmul(left, right):
    return jnp.dot(left, right, precision=lax.Precision.HIGHEST, preferred_element_type=jnp.float32)

def norm_gain(vector, gain):
    return vector * lax.rsqrt(lax.optimization_barrier(jnp.mean(vector * vector, axis=-1, keepdims=True)) + EPS) * gain

def rotate(vector, seq_pos):
    half = HEAD_SIZE // 2
    freq = BASE ** (-jnp.arange(half, dtype=jnp.float32) * 2.0 / HEAD_SIZE)
    angle = seq_pos.astype(jnp.float32)[:, None] * freq[None, :]
    cosine = jnp.cos(angle)[:, None, :]
    sine = jnp.sin(angle)[:, None, :]
    lower = vector[..., :half]
    upper = vector[..., half:]
    return jnp.concatenate([lower * cosine - upper * sine, upper * cosine + lower * sine], axis=-1)

def attend_block(query_rows, offset, key_rows, value_rows, seq_pos):
    row_count = query_rows.shape[0]
    scores = jnp.einsum('qhd,khd->hqk', query_rows, key_rows, precision=lax.Precision.HIGHEST) * HEAD_SIZE ** (-0.5)
    scores = low_back(scores)
    capped = CAP * jnp.tanh(scores / CAP)
    query_idx = offset + jnp.arange(row_count, dtype=jnp.int32)
    key_idx = jnp.arange(key_rows.shape[0], dtype=jnp.int32)
    query_pos = lax.dynamic_slice_in_dim(seq_pos, offset, row_count)
    visible = (key_idx[None, :] <= query_idx[:, None]) & (key_idx[None, :] >= (query_idx - query_pos)[:, None])
    masked = jnp.where(visible[None], capped, -1e+30)
    row_max = lax.optimization_barrier(jnp.max(masked, axis=-1, keepdims=True))
    exponent = jnp.exp(masked - row_max)
    probability = low(exponent / lax.optimization_barrier(jnp.sum(exponent, axis=-1, keepdims=True)))
    return jnp.einsum('hqk,khd->qhd', probability, value_rows, precision=lax.Precision.HIGHEST)

def layer_seq(seq_input, seq_pos, weights):
    w_query, key_matrix, value_matrix, w_output, w_gate, w_up, w_down, g_one, g_two, g_three, g_four = weights
    key_value_group = QUERY_HEAD_COUNT // KEY_VALUE_HEADS
    key_broadcast = jnp.repeat(key_matrix.reshape(MODEL_WIDTH, KEY_VALUE_HEADS, HEAD_SIZE), key_value_group, axis=1).reshape(MODEL_WIDTH, QUERY_HEAD_COUNT * HEAD_SIZE)
    value_broadcast = jnp.repeat(value_matrix.reshape(MODEL_WIDTH, KEY_VALUE_HEADS, HEAD_SIZE), key_value_group, axis=1).reshape(MODEL_WIDTH, QUERY_HEAD_COUNT * HEAD_SIZE)
    normed_one = low(norm_gain(seq_input, g_one))
    queries = low_back(low(rotate(low_back(matmul(normed_one, w_query)).reshape(LEN, QUERY_HEAD_COUNT, HEAD_SIZE), seq_pos)))
    key_rows = low_back(low(rotate(low_back(matmul(normed_one, key_broadcast)).reshape(LEN, QUERY_HEAD_COUNT, HEAD_SIZE), seq_pos)))
    value_rows = low_back(low(matmul(normed_one, value_broadcast))).reshape(LEN, QUERY_HEAD_COUNT, HEAD_SIZE)
    block_rows = math.gcd(LEN, 512)
    count = LEN // block_rows
    blocks = queries.reshape(count, block_rows, QUERY_HEAD_COUNT, HEAD_SIZE)
    starts = jnp.arange(count, dtype=jnp.int32) * block_rows
    attend = jax.checkpoint(lambda pieces: attend_block(pieces[0], pieces[1], key_rows, value_rows, seq_pos))
    attended = lax.map(attend, (blocks, starts)).reshape(LEN, QUERY_HEAD_COUNT * HEAD_SIZE)
    attended = low_back(low(attended))
    project = low_back(matmul(attended, w_output))
    middle = seq_input + norm_gain(project, g_two)
    normed_two = low(norm_gain(middle, g_three))
    gate = low_back(matmul(normed_two, w_gate))
    upper = low_back(matmul(normed_two, w_up))
    hidden = low(jax.nn.gelu(gate, approximate=True) * upper)
    feed = low_back(matmul(hidden, w_down))
    return middle + norm_gain(feed, g_four)

def reference(inputs, positions, query_weight, key_weight, value_weight, output_weight, gate_weight, up_weight, down_weight, pre_attn_gain, post_attn_gain, pre_ffn_gain, post_ffn_gain, cotangent):
    params = tuple((w.astype(jnp.float32) for w in (query_weight, key_weight, value_weight, output_weight, gate_weight, up_weight, down_weight, pre_attn_gain, post_attn_gain, pre_ffn_gain, post_ffn_gain)))
    checked = jax.checkpoint(layer_seq)

    def forward(whole, *weights_in):

        def step(carry, pieces):
            return (carry, checked(pieces[0], pieces[1], weights_in))
        unused, outputs = lax.scan(step, jnp.zeros((), jnp.float32), (whole, positions))
        return outputs
    result, pull = jax.vjp(forward, inputs.astype(jnp.float32), *params)
    grads = pull(cotangent.astype(jnp.float32))
    return (result.astype(jnp.bfloat16), grads[0].astype(jnp.bfloat16), grads[1], grads[2], grads[3], grads[4], grads[5], grads[6], grads[7], grads[8], grads[9], grads[10], grads[11])
```

```python
import math

import jax
import jax.numpy as jnp
from jax import lax
from jax.sharding import PartitionSpec as P

QUERY_HEAD_COUNT = 8
KEY_VALUE_HEADS = 4
HEAD_SIZE = 256


EPS = 1e-06
CAP = 50.0
BASE = 10000.0


def norm_gain(vector, gain):
    return vector * lax.rsqrt(jnp.mean(vector * vector, axis=-1, keepdims=True) + EPS) * gain


def geglu(gate_in, up_in):
    return jax.nn.gelu(gate_in, approximate=True) * up_in


def rounded(value):
    return lax.optimization_barrier(value.astype(jnp.bfloat16)).astype(jnp.float32)


def angle_tables(block_pos):
    half = HEAD_SIZE // 2
    freq = BASE ** (-jnp.arange(half, dtype=jnp.float32) * 2.0 / HEAD_SIZE)
    angle = block_pos.astype(jnp.float32)[..., None] * freq
    return (jnp.cos(angle)[:, :, None, :], jnp.sin(angle)[:, :, None, :])


def turn(vector, cosine, sine):
    half = HEAD_SIZE // 2
    lower = vector[..., :half]
    upper = vector[..., half:]
    return jnp.concatenate([lower * cosine - upper * sine, upper * cosine + lower * sine], axis=-1)


def turn_back(grad, cosine, sine):
    half = HEAD_SIZE // 2
    lower = grad[..., :half]
    upper = grad[..., half:]
    return jnp.concatenate([lower * cosine + upper * sine, upper * cosine - lower * sine], axis=-1)


def load_attention(
    query_weight, key_weight, value_weight, output_weight, gain_table, key_value_begin, kv_cols
):
    key_full, value_full = (
        lax.all_gather(key_weight, ("dp", "ctx", "seq"), axis=0, tiled=True),
        lax.all_gather(value_weight, ("dp", "ctx", "seq"), axis=0, tiled=True),
    )
    key_part = lax.dynamic_slice_in_dim(key_full, key_value_begin, kv_cols, 1)
    value_part = lax.dynamic_slice_in_dim(value_full, key_value_begin, kv_cols, 1)
    w_query, w_output, gain_full = (
        lax.all_gather(query_weight, ("dp", "ctx"), axis=0, tiled=True),
        lax.all_gather(output_weight, ("dp", "ctx"), axis=1, tiled=True),
        lax.all_gather(gain_table, ("dp", "ctx"), axis=0, tiled=True),
    )
    return (w_query, key_part, value_part, w_output, gain_full)


def load_ffn(w_gate, w_up, w_down):
    return (
        lax.all_gather(w_gate, ("dp", "ctx"), axis=0, tiled=True),
        lax.all_gather(w_up, ("dp", "ctx"), axis=0, tiled=True),
        lax.all_gather(w_down, ("dp", "ctx"), axis=1, tiled=True),
    )


def full_output(output_part):
    return lax.all_gather(output_part, "seq", axis=0, tiled=True)


def block_rows(local_rows):
    return lax.all_gather(local_rows, "seq", axis=1, tiled=True)


def row_total(partial_rows):
    return lax.psum_scatter(
        partial_rows.astype(jnp.bfloat16), "seq", scatter_dimension=1, tiled=True
    ).astype(jnp.float32)


def visible_mask(first_row, row_count, key_count, query_pos):
    query_idx = first_row + jnp.arange(row_count, dtype=jnp.int32)
    key_idx = jnp.arange(key_count, dtype=jnp.int32)
    return (key_idx[None, :] <= query_idx[:, None]) & (
        key_idx[None, :] >= (query_idx - query_pos)[:, None]
    )


def scores_of(queries, key_rows, first_row, query_pos):
    row_count = queries.shape[0]
    head_count = queries.shape[1] // HEAD_SIZE
    query_heads = queries.reshape(row_count, head_count, HEAD_SIZE)
    key_heads = key_rows.reshape(key_rows.shape[0], head_count, HEAD_SIZE)
    scores = jnp.einsum(
        "qhd,khd->hqk", query_heads, key_heads, preferred_element_type=jnp.float32
    ) * HEAD_SIZE ** (-0.5)
    bent = jnp.tanh(scores / CAP)
    visible = visible_mask(first_row, row_count, key_rows.shape[0], query_pos)
    masked = jnp.where(visible[None], CAP * bent, -1e30)
    return (query_heads, key_heads, bent, masked)


def attend_forward(queries, key_rows, value_rows, query_pos, first_row):
    query_heads, key_heads, bent, masked = scores_of(queries, key_rows, first_row, query_pos)
    head_count = query_heads.shape[1]
    value_heads = value_rows.reshape(value_rows.shape[0], head_count, HEAD_SIZE)
    row_max = jnp.max(masked, axis=-1, keepdims=True)
    exponent = jnp.exp(masked - row_max)
    row_sum = jnp.sum(exponent, axis=-1, keepdims=True)
    probability = (exponent / row_sum).astype(jnp.bfloat16)
    log_total = (row_max + jnp.log(row_sum))[..., 0]
    result = jnp.einsum(
        "hqk,khd->qhd", probability, value_heads, preferred_element_type=jnp.float32
    )
    return (
        result.astype(jnp.bfloat16).reshape(queries.shape[0], head_count * HEAD_SIZE),
        log_total,
    )


def attend_backward(queries, key_rows, value_rows, query_pos, first_row, log_total, grad_rows):
    query_heads, key_heads, bent, masked = scores_of(queries, key_rows, first_row, query_pos)
    head_count = query_heads.shape[1]
    value_heads = value_rows.reshape(value_rows.shape[0], head_count, HEAD_SIZE)
    grad_heads = grad_rows.reshape(queries.shape[0], head_count, HEAD_SIZE)
    probability = jnp.exp(masked - log_total[..., None])
    prob_low = probability.astype(jnp.bfloat16)
    grad_value = jnp.einsum(
        "hqk,qhd->khd", prob_low, grad_heads, preferred_element_type=jnp.float32
    )
    grad_prob = jnp.einsum(
        "qhd,khd->hqk", grad_heads, value_heads, preferred_element_type=jnp.float32
    )
    delta = jnp.sum(probability * grad_prob, axis=-1, keepdims=True)
    grad_scores = (probability * (grad_prob - delta) * (1.0 - bent * bent)).astype(jnp.bfloat16)
    grad_query = jnp.einsum(
        "hqk,khd->qhd", grad_scores, key_heads, preferred_element_type=jnp.float32
    ) * HEAD_SIZE ** (-0.5)
    grad_key = jnp.einsum(
        "hqk,qhd->khd", grad_scores, query_heads, preferred_element_type=jnp.float32
    ) * HEAD_SIZE ** (-0.5)
    key_count = key_rows.shape[0]
    return (
        grad_query.reshape(queries.shape[0], head_count * HEAD_SIZE),
        grad_key.reshape(key_count, head_count * HEAD_SIZE),
        grad_value.reshape(key_count, head_count * HEAD_SIZE),
    )


def general_local(
    inputs,
    positions,
    query_weight,
    key_weight,
    value_weight,
    output_weight,
    gate_weight,
    up_weight,
    down_weight,
    pre_attn_gain,
    post_attn_gain,
    pre_ffn_gain,
    post_ffn_gain,
    cotangent,
):
    seqs, tokens, width = inputs.shape
    block_len = positions.shape[1]
    full_len = block_len * lax.axis_size("ctx")
    offset = lax.axis_index("ctx") * block_len
    head_count = QUERY_HEAD_COUNT // lax.axis_size("seq")
    key_value_group = QUERY_HEAD_COUNT // KEY_VALUE_HEADS
    kv_heads = max(head_count // key_value_group, 1)
    kv_cols = kv_heads * HEAD_SIZE
    repeat_by = head_count // kv_heads
    head_cols = head_count * HEAD_SIZE
    key_value_begin = lax.axis_index("seq") * head_count // key_value_group * HEAD_SIZE
    cosine, sine = angle_tables(positions)
    gain_table = jnp.stack([pre_attn_gain, post_attn_gain, pre_ffn_gain, post_ffn_gain], axis=1)
    fwd_attn = load_attention(
        query_weight, key_weight, value_weight, output_weight, gain_table, key_value_begin, kv_cols
    )
    fwd_ffn = load_ffn(gate_weight, up_weight, down_weight)
    w_query, key_matrix, value_matrix, w_output, gain_full = fwd_attn
    w_gate, w_up, w_down = fwd_ffn
    gain_float = gain_full.astype(jnp.float32)
    gain_one = gain_float[:, 0]
    gain_two = gain_float[:, 1]
    gain_three = gain_float[:, 2]
    gain_four = gain_float[:, 3]
    x_float = inputs.astype(jnp.float32)
    normed_one = norm_gain(x_float, gain_one).astype(jnp.bfloat16)
    block_one = block_rows(normed_one)
    query_raw = jnp.einsum("srd,de->sre", block_one, w_query, preferred_element_type=jnp.float32)
    key_raw = jnp.einsum("srd,de->sre", block_one, key_matrix, preferred_element_type=jnp.float32)
    value_raw = jnp.einsum(
        "srd,de->sre", block_one, value_matrix, preferred_element_type=jnp.float32
    )
    query_rot = (
        turn(query_raw.reshape(seqs, block_len, head_count, HEAD_SIZE), cosine, sine)
        .astype(jnp.bfloat16)
        .reshape(seqs, block_len, head_cols)
    )
    key_rot = (
        turn(key_raw.reshape(seqs, block_len, kv_heads, HEAD_SIZE), cosine, sine)
        .astype(jnp.bfloat16)
        .reshape(seqs, block_len, kv_cols)
    )
    key_all, value_all = (
        lax.all_gather(key_rot, "ctx", axis=1, tiled=True),
        lax.all_gather(value_raw.astype(jnp.bfloat16), "ctx", axis=1, tiled=True),
    )
    key_broadcast = jnp.repeat(
        key_all.reshape(seqs, full_len, kv_heads, HEAD_SIZE), repeat_by, axis=2
    ).reshape(seqs, full_len, head_cols)
    value_broadcast = jnp.repeat(
        value_all.reshape(seqs, full_len, kv_heads, HEAD_SIZE), repeat_by, axis=2
    ).reshape(seqs, full_len, head_cols)
    query_block = math.gcd(block_len, 512)
    block_count = block_len // query_block
    item_count = seqs * block_count
    item_index = jnp.arange(item_count, dtype=jnp.int32)
    block_starts = offset + item_index % block_count * query_block
    seq_owner = item_index // block_count

    def forward_item(pieces):
        queries, query_pos, first_row, seq_id = pieces
        key_rows = lax.dynamic_index_in_dim(key_broadcast, seq_id, 0, keepdims=False)
        value_rows = lax.dynamic_index_in_dim(value_broadcast, seq_id, 0, keepdims=False)
        return attend_forward(queries, key_rows, value_rows, query_pos, first_row)

    head_items, log_total = lax.map(forward_item, (query_rot, positions, block_starts, seq_owner))
    out_full = full_output(w_output)
    heads_tok = lax.all_to_all(head_items, "seq", split_axis=1, concat_axis=2, tiled=True)
    project = jnp.einsum("ste,ed->std", heads_tok, out_full, preferred_element_type=jnp.float32)
    middle = x_float + norm_gain(project, gain_two)
    normed_two = norm_gain(middle, gain_three).astype(jnp.bfloat16)
    ffn_input = block_rows(normed_two)
    gate = jnp.einsum("srd,df->srf", ffn_input, w_gate, preferred_element_type=jnp.float32)
    upper = jnp.einsum("srd,df->srf", ffn_input, w_up, preferred_element_type=jnp.float32)
    hidden = geglu(gate, upper).astype(jnp.bfloat16)
    feed = row_total(jnp.einsum("srf,fd->srd", hidden, w_down, preferred_element_type=jnp.float32))
    layer_output = (middle + norm_gain(feed, gain_four)).astype(jnp.bfloat16)
    back_attn = load_attention(
        query_weight, key_weight, value_weight, output_weight, gain_table, key_value_begin, kv_cols
    )
    back_ffn = load_ffn(gate_weight, up_weight, down_weight)
    bq_weight, bk_weight, bv_weight, bo_weight = (
        back_attn[0],
        back_attn[1],
        back_attn[2],
        back_attn[3],
    )
    bgate_weight, bup_weight, bdown_weight = back_ffn
    grad_top = cotangent.astype(jnp.float32)
    unused, pull_four = jax.vjp(norm_gain, feed, gain_four)
    grad_feed, grad_g_four = pull_four(grad_top)
    grad_feed_rows = block_rows(grad_feed.astype(jnp.bfloat16))
    grad_hidden = jnp.einsum(
        "srd,fd->srf", grad_feed_rows, bdown_weight, preferred_element_type=jnp.float32
    )
    grad_down_part = jnp.einsum(
        "srf,srd->fd", hidden, grad_feed_rows, preferred_element_type=jnp.float32
    )
    unused, pull_act = jax.vjp(geglu, gate, upper)
    grad_gate_act, grad_up_act = pull_act(grad_hidden)
    grad_gate_act = grad_gate_act.astype(jnp.bfloat16)
    grad_up_act = grad_up_act.astype(jnp.bfloat16)
    grad_rows_part = jnp.einsum(
        "srf,df->srd", grad_gate_act, bgate_weight, preferred_element_type=jnp.float32
    ) + jnp.einsum("srf,df->srd", grad_up_act, bup_weight, preferred_element_type=jnp.float32)
    grad_gate_part = jnp.einsum(
        "srd,srf->df", ffn_input, grad_gate_act, preferred_element_type=jnp.float32
    )
    grad_up_part = jnp.einsum(
        "srd,srf->df", ffn_input, grad_up_act, preferred_element_type=jnp.float32
    )
    ffn_grads = (
        lax.psum_scatter(
            grad_gate_part.astype(jnp.bfloat16), ("dp", "ctx"), scatter_dimension=0, tiled=True
        ).astype(jnp.float32),
        lax.psum_scatter(
            grad_up_part.astype(jnp.bfloat16), ("dp", "ctx"), scatter_dimension=0, tiled=True
        ).astype(jnp.float32),
        lax.psum_scatter(
            grad_down_part.astype(jnp.bfloat16), ("dp", "ctx"), scatter_dimension=1, tiled=True
        ).astype(jnp.float32),
    )
    grad_normed_two = row_total(grad_rows_part)
    unused, pull_three = jax.vjp(norm_gain, middle, gain_three)
    grad_mid_norm, grad_g_three = pull_three(grad_normed_two)
    grad_middle = grad_top + grad_mid_norm
    unused, pull_two = jax.vjp(norm_gain, project, gain_two)
    grad_project, grad_g_two = pull_two(grad_middle)
    grad_project = grad_project.astype(jnp.bfloat16)
    out_back = full_output(bo_weight)
    grad_heads_tok = jnp.einsum(
        "std,ed->ste", grad_project, out_back, preferred_element_type=jnp.float32
    ).astype(jnp.bfloat16)
    grad_output_part = lax.psum_scatter(
        jnp.einsum(
            "ste,std->ed", heads_tok, grad_project, preferred_element_type=jnp.float32
        ).astype(jnp.bfloat16),
        "seq",
        scatter_dimension=0,
        tiled=True,
    )
    grad_heads = lax.all_to_all(grad_heads_tok, "seq", split_axis=2, concat_axis=1, tiled=True)

    def backward_item(carry, pieces):
        key_acc, value_acc = carry
        queries, query_pos, first_row, seq_id, log_part, grad_part = pieces
        key_rows = lax.dynamic_index_in_dim(key_broadcast, seq_id, 0, keepdims=False)
        value_rows = lax.dynamic_index_in_dim(value_broadcast, seq_id, 0, keepdims=False)
        grad_query, grad_key, grad_value = attend_backward(
            queries, key_rows, value_rows, query_pos, first_row, log_part, grad_part
        )
        key_acc = lax.dynamic_update_index_in_dim(
            key_acc,
            lax.dynamic_index_in_dim(key_acc, seq_id, 0, keepdims=False) + grad_key,
            seq_id,
            0,
        )
        value_acc = lax.dynamic_update_index_in_dim(
            value_acc,
            lax.dynamic_index_in_dim(value_acc, seq_id, 0, keepdims=False) + grad_value,
            seq_id,
            0,
        )
        return ((key_acc, value_acc), grad_query)

    empty = jnp.zeros((seqs, full_len, head_cols), jnp.float32)
    (key_terms, value_terms), grad_query_items = lax.scan(
        backward_item,
        (empty, empty),
        (query_rot, positions, block_starts, seq_owner, log_total, grad_heads),
    )
    key_sums, value_sums = (
        lax.psum_scatter(
            key_terms.astype(jnp.bfloat16), "ctx", scatter_dimension=1, tiled=True
        ).astype(jnp.float32),
        lax.psum_scatter(
            value_terms.astype(jnp.bfloat16), "ctx", scatter_dimension=1, tiled=True
        ).astype(jnp.float32),
    )
    grad_query_rot = rounded(grad_query_items.reshape(seqs, block_len, head_count, HEAD_SIZE))
    grad_query_raw = (
        turn_back(grad_query_rot, cosine, sine)
        .astype(jnp.bfloat16)
        .reshape(seqs, block_len, head_cols)
    )
    grad_key_rot = rounded(key_sums.reshape(seqs, block_len, head_count, HEAD_SIZE))
    grad_key_raw = (
        turn_back(grad_key_rot, cosine, sine)
        .astype(jnp.bfloat16)
        .reshape(seqs, block_len, head_cols)
    )
    grad_value_raw = value_sums.astype(jnp.bfloat16)
    key_expand = jnp.repeat(
        bk_weight.reshape(width, kv_heads, HEAD_SIZE), repeat_by, axis=1
    ).reshape(width, head_cols)
    value_expand = jnp.repeat(
        bv_weight.reshape(width, kv_heads, HEAD_SIZE), repeat_by, axis=1
    ).reshape(width, head_cols)
    grad_block_one = jnp.einsum(
        "sre,de->srd", grad_query_raw, bq_weight, preferred_element_type=jnp.float32
    )
    grad_block_one = grad_block_one + jnp.einsum(
        "sre,de->srd", grad_key_raw, key_expand, preferred_element_type=jnp.float32
    )
    grad_block_one = grad_block_one + jnp.einsum(
        "sre,de->srd", grad_value_raw, value_expand, preferred_element_type=jnp.float32
    )
    grad_normed_one = row_total(grad_block_one)
    grad_query_part = jnp.einsum(
        "srd,sre->de", block_one, grad_query_raw, preferred_element_type=jnp.float32
    )
    grad_key_wide = jnp.einsum(
        "srd,sre->de", block_one, grad_key_raw, preferred_element_type=jnp.float32
    )
    grad_value_wide = jnp.einsum(
        "srd,sre->de", block_one, grad_value_raw, preferred_element_type=jnp.float32
    )
    grad_key_part = jnp.sum(
        grad_key_wide.reshape(width, kv_heads, repeat_by, HEAD_SIZE), axis=2
    ).reshape(width, kv_cols)
    grad_value_part = jnp.sum(
        grad_value_wide.reshape(width, kv_heads, repeat_by, HEAD_SIZE), axis=2
    ).reshape(width, kv_cols)
    unused, pull_one = jax.vjp(norm_gain, x_float, gain_one)
    grad_input_norm, grad_g_one = pull_one(grad_normed_one)
    input_grad = (grad_middle + grad_input_norm).astype(jnp.bfloat16)
    gain_grads = jnp.stack([grad_g_one, grad_g_two, grad_g_three, grad_g_four], axis=1)
    attention_gradients = (
        lax.psum_scatter(
            grad_query_part.astype(jnp.bfloat16), ("dp", "ctx"), scatter_dimension=0, tiled=True
        ).astype(jnp.float32),
        lax.psum_scatter(grad_output_part, ("dp", "ctx"), scatter_dimension=1, tiled=True).astype(
            jnp.float32
        ),
    )
    key_spread = lax.dynamic_update_slice_in_dim(
        jnp.zeros((width, KEY_VALUE_HEADS * HEAD_SIZE), jnp.float32),
        grad_key_part,
        key_value_begin,
        1,
    )
    value_spread = lax.dynamic_update_slice_in_dim(
        jnp.zeros((width, KEY_VALUE_HEADS * HEAD_SIZE), jnp.float32),
        grad_value_part,
        key_value_begin,
        1,
    )
    kv_sums = (
        lax.psum_scatter(key_spread, ("dp", "ctx", "seq"), scatter_dimension=0, tiled=True),
        lax.psum_scatter(value_spread, ("dp", "ctx", "seq"), scatter_dimension=0, tiled=True),
        lax.psum_scatter(gain_grads, ("dp", "ctx", "seq"), scatter_dimension=0, tiled=True),
    )
    gain_out = kv_sums[2]
    return (
        layer_output,
        input_grad,
        attention_gradients[0],
        kv_sums[0],
        kv_sums[1],
        attention_gradients[1],
        ffn_grads[0],
        ffn_grads[1],
        ffn_grads[2],
        gain_out[:, 0],
        gain_out[:, 1],
        gain_out[:, 2],
        gain_out[:, 3],
    )


def flip(value, axis):
    return lax.ppermute(value, axis, [(0, 1), (1, 0)])


def ordered(index, own, other, axis=0):
    return jnp.where(
        index == 0, jnp.stack([own, other], axis=axis), jnp.stack([other, own], axis=axis)
    )


def pick(value, index, axis=0):
    return lax.dynamic_index_in_dim(value, index, axis, keepdims=False)


def trade_sequences(value):
    cy = lax.axis_index("cy")
    return ordered(cy, pick(value, cy), flip(pick(value, 1 - cy), "cy"))


def gather_weight(local_rows):
    x, y, c = lax.axis_index("dp"), lax.axis_index("cy"), lax.axis_index("core")
    own = pick(local_rows, c, 1)
    got = flip(pick(local_rows, 1 - c, 1), "core")
    first = jnp.where(c == 0, own, got)
    second = jnp.where(c == 0, got, own)
    first_y = flip(first, "cy")
    second_x = flip(second, "dp")
    first_pair = ordered(y, first, first_y)
    second_pair = ordered(x, second, second_x)
    first_x = flip(first_pair, "dp")
    second_y = flip(second_pair, "cy")
    first_all = ordered(x, first_pair, first_x)
    second_all = ordered(y, second_pair, second_y, axis=1)
    return jnp.stack([first_all, second_all], axis=2).reshape(-1, own.shape[-1])


def scatter_weight_grad(grad):
    x, y, c = lax.axis_index("dp"), lax.axis_index("cy"), lax.axis_index("core")
    cols = grad.shape[-1]
    parts = grad.reshape(2, 2, 2, -1, cols)
    first, second = parts[:, :, 0], parts[:, :, 1]
    first_x = flip(pick(first, 1 - x), "dp")
    second_y = flip(pick(second, 1 - y, 1), "cy")
    first_sum = (pick(first, x).astype(jnp.float32) + first_x.astype(jnp.float32)).astype(
        jnp.bfloat16
    )
    second_sum = (pick(second, y, 1).astype(jnp.float32) + second_y.astype(jnp.float32)).astype(
        jnp.bfloat16
    )
    first_y = flip(pick(first_sum, 1 - y), "cy")
    second_x = flip(pick(second_sum, 1 - x), "dp")
    first_total = pick(first_sum, y).astype(jnp.float32) + first_y.astype(jnp.float32)
    second_total = pick(second_sum, x).astype(jnp.float32) + second_x.astype(jnp.float32)
    keep = jnp.where(c == 0, first_total, second_total)
    got = flip(jnp.where(c == 0, second_total, first_total).astype(jnp.bfloat16), "core")
    return ordered(c, keep, got.astype(jnp.float32), axis=1)


def gather_rows(local_rows):
    width = local_rows.shape[-1]
    return lax.all_gather(local_rows, ("core", "seq"), axis=1, tiled=True).reshape(-1, width)


def scatter_rows(partial_rows):
    c = lax.axis_index("core")
    parts = partial_rows.astype(jnp.bfloat16).reshape(2, 2, -1, partial_rows.shape[-1])
    got = flip(pick(parts, 1 - c, 1), "core")
    both = pick(parts, c, 1).astype(jnp.float32) + got.astype(jnp.float32)
    return lax.psum_scatter(
        both.astype(jnp.bfloat16), "seq", scatter_dimension=1, tiled=True
    ).astype(jnp.float32)


def dot(left, right, dims):
    return lax.dot_general(left, right, ((dims[:1], dims[1:]), ((), ())), preferred_element_type=jnp.float32)


def head_scores(queries, keys, visible):
    bent = jnp.tanh(dot(queries, keys, (1, 1)) * (HEAD_SIZE ** (-0.5) / CAP))
    return bent, jnp.where(visible, CAP * bent, -1e30)


def head_local(
    inputs,
    positions,
    query_weight,
    key_weight,
    value_weight,
    output_weight,
    gate_weight,
    up_weight,
    down_weight,
    pre_attn_gain,
    post_attn_gain,
    pre_ffn_gain,
    post_ffn_gain,
    cotangent,
):
    width = inputs.shape[-1]
    c, cy = lax.axis_index("core"), lax.axis_index("cy")
    low = jnp.bfloat16
    rows_own = query_weight.shape[0]
    kv_stack = jnp.stack([key_weight, value_weight], axis=1).reshape(-1, 2, KEY_VALUE_HEADS, HEAD_SIZE)
    kv_rows = lax.all_to_all(
        kv_stack.transpose(2, 0, 1, 3), "seq", split_axis=0, concat_axis=0, tiled=True
    ).reshape(rows_own, 2, HEAD_SIZE)
    attn_share = jnp.concatenate(
        [
            query_weight.reshape(rows_own, 2, HEAD_SIZE),
            kv_rows,
            output_weight.T.reshape(rows_own, 2, HEAD_SIZE),
        ],
        axis=2,
    )
    ffn_cols = gate_weight.shape[1] // 2
    gate_up_share = jnp.concatenate(
        [gate_weight.reshape(rows_own, 2, ffn_cols), up_weight.reshape(rows_own, 2, ffn_cols)],
        axis=2,
    )
    down_share = down_weight.T.reshape(rows_own, 2, ffn_cols)
    gain_table = jnp.stack([pre_attn_gain, post_attn_gain, pre_ffn_gain, post_ffn_gain], axis=0)
    gain_full = lax.all_gather(gain_table, ("dp", "cy", "core"), axis=1, tiled=True).astype(jnp.float32)
    gain_one, gain_two, gain_three, gain_four = gain_full[0], gain_full[1], gain_full[2], gain_full[3]

    x_float = trade_sequences(inputs).astype(jnp.float32)
    grad_top = trade_sequences(cotangent).astype(jnp.float32)
    seq_pos = lax.all_gather(positions, ("cy", "core"), axis=1, tiled=True)
    seq_pos = pick(seq_pos, cy)
    half = HEAD_SIZE // 2
    freq = BASE ** (-jnp.arange(half, dtype=jnp.float32) * 2.0 / HEAD_SIZE)
    angle = seq_pos.astype(jnp.float32)[:, None] * freq
    cosine, sine = jnp.cos(angle), jnp.sin(angle)
    kv_cosine = jnp.where(c == 0, cosine, 1.0)
    kv_sine = jnp.where(c == 0, sine, 0.0)

    attn_weight = gather_weight(attn_share)
    in_weight = attn_weight[:, : 2 * HEAD_SIZE]
    out_weight = attn_weight[:, 2 * HEAD_SIZE :]
    gate_up_share, down_share, attn_weight_late = lax.optimization_barrier(
        (gate_up_share, down_share, attn_weight[:8])
    )
    gate_up_weight = gather_weight(gate_up_share)
    down_back = gather_weight(down_share)

    block_one = gather_rows(norm_gain(x_float, gain_one).astype(low))
    raw = dot(block_one, in_weight, (1, 0))
    queries = turn(raw[:, :HEAD_SIZE], cosine, sine).astype(low)
    kv_own = turn(raw[:, HEAD_SIZE:], kv_cosine, kv_sine).astype(low)
    kv_other = flip(kv_own, "core")
    keys = jnp.where(c == 0, kv_own, kv_other)
    values = jnp.where(c == 0, kv_other, kv_own)
    token = jnp.arange(seq_pos.shape[0], dtype=jnp.int32)
    visible = (token[None, :] <= token[:, None]) & (token[None, :] >= (token - seq_pos)[:, None])
    bent, masked = head_scores(queries, keys, visible)
    row_max = jnp.max(masked, axis=-1, keepdims=True)
    exponent = jnp.exp(masked - row_max)
    row_sum = jnp.sum(exponent, axis=-1, keepdims=True)
    heads = dot((exponent / row_sum).astype(low), values, (1, 0)).astype(low)
    log_total = row_max + jnp.log(row_sum)

    project = scatter_rows(dot(heads, out_weight, (1, 1)))
    middle = x_float + norm_gain(project, gain_two)
    block_two = gather_rows(norm_gain(middle, gain_three).astype(low))
    gate_up = dot(block_two, gate_up_weight, (1, 0))
    gate, upper = gate_up[:, :ffn_cols], gate_up[:, ffn_cols:]
    hidden = geglu(gate, upper).astype(low)
    feed = scatter_rows(dot(hidden, down_back, (1, 1)))
    layer_output = trade_sequences((middle + norm_gain(feed, gain_four)).astype(low))

    unused, pull_four = jax.vjp(norm_gain, feed, gain_four)
    grad_feed, grad_g_four = pull_four(grad_top)
    grad_feed_rows = gather_rows(grad_feed.astype(low))
    grad_hidden = dot(grad_feed_rows, down_back, (1, 0))
    unused, pull_act = jax.vjp(geglu, gate, upper)
    grad_gate_act, grad_up_act = pull_act(grad_hidden)
    grad_gate_up = jnp.concatenate([grad_gate_act.astype(low), grad_up_act.astype(low)], axis=1)
    grad_normed_two = scatter_rows(dot(grad_gate_up, gate_up_weight, (1, 1)))
    grad_down = scatter_weight_grad(dot(grad_feed_rows, hidden, (0, 0)).astype(low))
    grad_gu = scatter_weight_grad(dot(block_two, grad_gate_up, (0, 0)).astype(low))

    unused, pull_three = jax.vjp(norm_gain, middle, gain_three)
    grad_mid_norm, grad_g_three = pull_three(grad_normed_two)
    grad_middle = grad_top + grad_mid_norm
    unused, pull_two = jax.vjp(norm_gain, project, gain_two)
    grad_project, grad_g_two = pull_two(grad_middle)
    grad_project_rows = gather_rows(grad_project.astype(low))
    grad_heads = dot(grad_project_rows, out_weight, (1, 0)).astype(low)
    grad_output_part = dot(grad_project_rows, heads, (0, 0)).astype(low)

    bent, masked = head_scores(queries, keys, visible)
    probability = jnp.exp(masked - log_total)
    grad_value = dot(probability.astype(low), grad_heads, (0, 0)).astype(low)
    grad_prob = dot(grad_heads, values, (1, 1))
    delta = jnp.sum(probability * grad_prob, axis=-1, keepdims=True)
    grad_scores = (probability * (grad_prob - delta) * (1.0 - bent * bent)).astype(low)
    scale = HEAD_SIZE ** (-0.5)
    grad_query_rot = rounded(dot(grad_scores, keys, (1, 0)) * scale)
    grad_key_rot = rounded(dot(grad_scores, queries, (0, 0)) * scale)
    grad_query_raw = turn_back(grad_query_rot, cosine, sine).astype(low)
    grad_key_raw = turn_back(grad_key_rot, cosine, sine).astype(low)
    kv_grad_own = jnp.where(c == 0, grad_key_raw, grad_value)
    kv_grad_got = flip(jnp.where(c == 0, grad_value, grad_key_raw), "core")
    kv_grad = (kv_grad_own.astype(jnp.float32) + kv_grad_got.astype(jnp.float32)).astype(low)
    grad_in = jnp.concatenate([grad_query_raw, kv_grad], axis=1)
    grad_normed_one = scatter_rows(dot(grad_in, in_weight, (1, 1)))
    grad_in_part = dot(block_one, grad_in, (0, 0)).astype(low)
    attn_grads = scatter_weight_grad(jnp.concatenate([grad_in_part, grad_output_part], axis=1))

    unused, pull_one = jax.vjp(norm_gain, x_float, gain_one)
    grad_input_norm, grad_g_one = pull_one(grad_normed_one)
    input_grad = trade_sequences((grad_middle + grad_input_norm).astype(low))
    gain_grads = jnp.stack([grad_g_one, grad_g_two, grad_g_three, grad_g_four], axis=0)
    everyone = ("dp", "cy", "core", "seq")
    device_count = lax.axis_size(everyone)
    gain_out = jnp.sum(
        lax.all_to_all(
            gain_grads.reshape(4, device_count, -1).transpose(1, 0, 2),
            everyone,
            split_axis=0,
            concat_axis=0,
            tiled=True,
        ),
        axis=0,
    )
    grad_query_out = attn_grads[:, :, :HEAD_SIZE].reshape(rows_own, 2 * HEAD_SIZE)
    grad_output_out = attn_grads[:, :, 2 * HEAD_SIZE :].reshape(rows_own, 2 * HEAD_SIZE).T
    kv_back = lax.all_to_all(
        attn_grads[:, :, HEAD_SIZE : 2 * HEAD_SIZE].astype(low), "seq", split_axis=0, concat_axis=0, tiled=True
    ).reshape(KEY_VALUE_HEADS, -1, 2, HEAD_SIZE).transpose(2, 1, 0, 3).reshape(2, -1, KEY_VALUE_HEADS * HEAD_SIZE).astype(jnp.float32)
    return (
        layer_output,
        input_grad,
        grad_query_out,
        kv_back[0],
        kv_back[1],
        grad_output_out,
        grad_gu[:, :, :ffn_cols].reshape(rows_own, 2 * ffn_cols),
        grad_gu[:, :, ffn_cols:].reshape(rows_own, 2 * ffn_cols),
        grad_down.reshape(rows_own, 2 * ffn_cols).T,
        gain_out[0],
        gain_out[1],
        gain_out[2],
        gain_out[3],
    )


def one_head_each(mesh):
    sizes = mesh.shape
    return (
        sizes["dp"] == 2
        and sizes["ctx"] == 4
        and sizes["seq"] == KEY_VALUE_HEADS
        and QUERY_HEAD_COUNT == 2 * KEY_VALUE_HEADS
    )


def solution(mesh):
    if one_head_each(mesh):
        body, ctx = head_local, ("cy", "core")
        grid = jax.sharding.Mesh(
            mesh.devices.reshape(mesh.shape["dp"], -1, 2, mesh.shape["seq"]),
            ("dp", "cy", "core", "seq"),
        )
    else:
        body, ctx, grid = general_local, ("ctx",), mesh
    owners, everyone = ("dp", *ctx), ("dp", *ctx, "seq")
    rows = P("dp", (*ctx, "seq"), None)
    tall, flat, wide = P(owners, "seq"), P(everyone, None), P("seq", owners)
    gains = (P(owners),) * 4
    return jax.shard_map(
        body,
        mesh=grid,
        in_specs=(rows, P("dp", ctx), tall, flat, flat, wide, tall, tall, wide, *gains, rows),
        out_specs=(rows, rows, tall, flat, flat, wide, tall, tall, wide, *((P(everyone),) * 4)),
        check_vma=False,
    )
```

```python
import functools
import math

import jax
import jax.numpy as jnp
from jax import lax
from jax.experimental import pallas as pl
from jax.experimental.pallas import tpu as pltpu
from jax.sharding import PartitionSpec as P

QUERY_HEAD_COUNT = 8
KEY_VALUE_HEADS = 4
HEAD_SIZE = 256


EPS = 1e-06
CAP = 50.0
BASE = 10000.0


def norm_gain(vector, gain):
    return vector * lax.rsqrt(jnp.mean(vector * vector, axis=-1, keepdims=True) + EPS) * gain


def geglu(gate_in, up_in):
    return jax.nn.gelu(gate_in, approximate=True) * up_in


def rounded(value):
    return lax.optimization_barrier(value.astype(jnp.bfloat16)).astype(jnp.float32)


def angle_tables(block_pos):
    half = HEAD_SIZE // 2
    freq = BASE ** (-jnp.arange(half, dtype=jnp.float32) * 2.0 / HEAD_SIZE)
    angle = block_pos.astype(jnp.float32)[..., None] * freq
    return (jnp.cos(angle)[:, :, None, :], jnp.sin(angle)[:, :, None, :])


def turn(vector, cosine, sine):
    half = HEAD_SIZE // 2
    lower = vector[..., :half]
    upper = vector[..., half:]
    return jnp.concatenate([lower * cosine - upper * sine, upper * cosine + lower * sine], axis=-1)


def turn_back(grad, cosine, sine):
    half = HEAD_SIZE // 2
    lower = grad[..., :half]
    upper = grad[..., half:]
    return jnp.concatenate([lower * cosine + upper * sine, upper * cosine - lower * sine], axis=-1)


def load_attention(
    query_weight, key_weight, value_weight, output_weight, gain_table, key_value_begin, kv_cols
):
    key_full, value_full = (
        lax.all_gather(key_weight, ("dp", "ctx", "seq"), axis=0, tiled=True),
        lax.all_gather(value_weight, ("dp", "ctx", "seq"), axis=0, tiled=True),
    )
    key_part = lax.dynamic_slice_in_dim(key_full, key_value_begin, kv_cols, 1)
    value_part = lax.dynamic_slice_in_dim(value_full, key_value_begin, kv_cols, 1)
    w_query, w_output, gain_full = (
        lax.all_gather(query_weight, ("dp", "ctx"), axis=0, tiled=True),
        lax.all_gather(output_weight, ("dp", "ctx"), axis=1, tiled=True),
        lax.all_gather(gain_table, ("dp", "ctx"), axis=0, tiled=True),
    )
    return (w_query, key_part, value_part, w_output, gain_full)


def load_ffn(w_gate, w_up, w_down):
    return (
        lax.all_gather(w_gate, ("dp", "ctx"), axis=0, tiled=True),
        lax.all_gather(w_up, ("dp", "ctx"), axis=0, tiled=True),
        lax.all_gather(w_down, ("dp", "ctx"), axis=1, tiled=True),
    )


def full_output(output_part):
    return lax.all_gather(output_part, "seq", axis=0, tiled=True)


def block_rows(local_rows):
    return lax.all_gather(local_rows, "seq", axis=1, tiled=True)


def row_total(partial_rows):
    return lax.psum_scatter(
        partial_rows.astype(jnp.bfloat16), "seq", scatter_dimension=1, tiled=True
    ).astype(jnp.float32)


def visible_mask(first_row, row_count, key_count, query_pos):
    query_idx = first_row + jnp.arange(row_count, dtype=jnp.int32)
    key_idx = jnp.arange(key_count, dtype=jnp.int32)
    return (key_idx[None, :] <= query_idx[:, None]) & (
        key_idx[None, :] >= (query_idx - query_pos)[:, None]
    )


def scores_of(queries, key_rows, first_row, query_pos):
    row_count = queries.shape[0]
    head_count = queries.shape[1] // HEAD_SIZE
    query_heads = queries.reshape(row_count, head_count, HEAD_SIZE)
    key_heads = key_rows.reshape(key_rows.shape[0], head_count, HEAD_SIZE)
    scores = jnp.einsum(
        "qhd,khd->hqk", query_heads, key_heads, preferred_element_type=jnp.float32
    ) * HEAD_SIZE ** (-0.5)
    bent = jnp.tanh(scores / CAP)
    visible = visible_mask(first_row, row_count, key_rows.shape[0], query_pos)
    masked = jnp.where(visible[None], CAP * bent, -1e30)
    return (query_heads, key_heads, bent, masked)


def attend_forward(queries, key_rows, value_rows, query_pos, first_row):
    query_heads, key_heads, bent, masked = scores_of(queries, key_rows, first_row, query_pos)
    head_count = query_heads.shape[1]
    value_heads = value_rows.reshape(value_rows.shape[0], head_count, HEAD_SIZE)
    row_max = jnp.max(masked, axis=-1, keepdims=True)
    exponent = jnp.exp(masked - row_max)
    row_sum = jnp.sum(exponent, axis=-1, keepdims=True)
    probability = (exponent / row_sum).astype(jnp.bfloat16)
    log_total = (row_max + jnp.log(row_sum))[..., 0]
    result = jnp.einsum(
        "hqk,khd->qhd", probability, value_heads, preferred_element_type=jnp.float32
    )
    return (
        result.astype(jnp.bfloat16).reshape(queries.shape[0], head_count * HEAD_SIZE),
        log_total,
    )


def attend_backward(queries, key_rows, value_rows, query_pos, first_row, log_total, grad_rows):
    query_heads, key_heads, bent, masked = scores_of(queries, key_rows, first_row, query_pos)
    head_count = query_heads.shape[1]
    value_heads = value_rows.reshape(value_rows.shape[0], head_count, HEAD_SIZE)
    grad_heads = grad_rows.reshape(queries.shape[0], head_count, HEAD_SIZE)
    probability = jnp.exp(masked - log_total[..., None])
    prob_low = probability.astype(jnp.bfloat16)
    grad_value = jnp.einsum(
        "hqk,qhd->khd", prob_low, grad_heads, preferred_element_type=jnp.float32
    )
    grad_prob = jnp.einsum(
        "qhd,khd->hqk", grad_heads, value_heads, preferred_element_type=jnp.float32
    )
    delta = jnp.sum(probability * grad_prob, axis=-1, keepdims=True)
    grad_scores = (probability * (grad_prob - delta) * (1.0 - bent * bent)).astype(jnp.bfloat16)
    grad_query = jnp.einsum(
        "hqk,khd->qhd", grad_scores, key_heads, preferred_element_type=jnp.float32
    ) * HEAD_SIZE ** (-0.5)
    grad_key = jnp.einsum(
        "hqk,qhd->khd", grad_scores, query_heads, preferred_element_type=jnp.float32
    ) * HEAD_SIZE ** (-0.5)
    key_count = key_rows.shape[0]
    return (
        grad_query.reshape(queries.shape[0], head_count * HEAD_SIZE),
        grad_key.reshape(key_count, head_count * HEAD_SIZE),
        grad_value.reshape(key_count, head_count * HEAD_SIZE),
    )


def general_local(
    inputs,
    positions,
    query_weight,
    key_weight,
    value_weight,
    output_weight,
    gate_weight,
    up_weight,
    down_weight,
    pre_attn_gain,
    post_attn_gain,
    pre_ffn_gain,
    post_ffn_gain,
    cotangent,
):
    seqs, tokens, width = inputs.shape
    block_len = positions.shape[1]
    full_len = block_len * lax.axis_size("ctx")
    offset = lax.axis_index("ctx") * block_len
    head_count = QUERY_HEAD_COUNT // lax.axis_size("seq")
    key_value_group = QUERY_HEAD_COUNT // KEY_VALUE_HEADS
    kv_heads = max(head_count // key_value_group, 1)
    kv_cols = kv_heads * HEAD_SIZE
    repeat_by = head_count // kv_heads
    head_cols = head_count * HEAD_SIZE
    key_value_begin = lax.axis_index("seq") * head_count // key_value_group * HEAD_SIZE
    cosine, sine = angle_tables(positions)
    gain_table = jnp.stack([pre_attn_gain, post_attn_gain, pre_ffn_gain, post_ffn_gain], axis=1)
    fwd_attn = load_attention(
        query_weight, key_weight, value_weight, output_weight, gain_table, key_value_begin, kv_cols
    )
    fwd_ffn = load_ffn(gate_weight, up_weight, down_weight)
    w_query, key_matrix, value_matrix, w_output, gain_full = fwd_attn
    w_gate, w_up, w_down = fwd_ffn
    gain_float = gain_full.astype(jnp.float32)
    gain_one = gain_float[:, 0]
    gain_two = gain_float[:, 1]
    gain_three = gain_float[:, 2]
    gain_four = gain_float[:, 3]
    x_float = inputs.astype(jnp.float32)
    normed_one = norm_gain(x_float, gain_one).astype(jnp.bfloat16)
    block_one = block_rows(normed_one)
    query_raw = jnp.einsum("srd,de->sre", block_one, w_query, preferred_element_type=jnp.float32)
    key_raw = jnp.einsum("srd,de->sre", block_one, key_matrix, preferred_element_type=jnp.float32)
    value_raw = jnp.einsum(
        "srd,de->sre", block_one, value_matrix, preferred_element_type=jnp.float32
    )
    query_rot = (
        turn(query_raw.reshape(seqs, block_len, head_count, HEAD_SIZE), cosine, sine)
        .astype(jnp.bfloat16)
        .reshape(seqs, block_len, head_cols)
    )
    key_rot = (
        turn(key_raw.reshape(seqs, block_len, kv_heads, HEAD_SIZE), cosine, sine)
        .astype(jnp.bfloat16)
        .reshape(seqs, block_len, kv_cols)
    )
    key_all, value_all = (
        lax.all_gather(key_rot, "ctx", axis=1, tiled=True),
        lax.all_gather(value_raw.astype(jnp.bfloat16), "ctx", axis=1, tiled=True),
    )
    key_broadcast = jnp.repeat(
        key_all.reshape(seqs, full_len, kv_heads, HEAD_SIZE), repeat_by, axis=2
    ).reshape(seqs, full_len, head_cols)
    value_broadcast = jnp.repeat(
        value_all.reshape(seqs, full_len, kv_heads, HEAD_SIZE), repeat_by, axis=2
    ).reshape(seqs, full_len, head_cols)
    query_block = math.gcd(block_len, 512)
    block_count = block_len // query_block
    item_count = seqs * block_count
    item_index = jnp.arange(item_count, dtype=jnp.int32)
    block_starts = offset + item_index % block_count * query_block
    seq_owner = item_index // block_count

    def forward_item(pieces):
        queries, query_pos, first_row, seq_id = pieces
        key_rows = lax.dynamic_index_in_dim(key_broadcast, seq_id, 0, keepdims=False)
        value_rows = lax.dynamic_index_in_dim(value_broadcast, seq_id, 0, keepdims=False)
        return attend_forward(queries, key_rows, value_rows, query_pos, first_row)

    head_items, log_total = lax.map(forward_item, (query_rot, positions, block_starts, seq_owner))
    out_full = full_output(w_output)
    heads_tok = lax.all_to_all(head_items, "seq", split_axis=1, concat_axis=2, tiled=True)
    project = jnp.einsum("ste,ed->std", heads_tok, out_full, preferred_element_type=jnp.float32)
    middle = x_float + norm_gain(project, gain_two)
    normed_two = norm_gain(middle, gain_three).astype(jnp.bfloat16)
    ffn_input = block_rows(normed_two)
    gate = jnp.einsum("srd,df->srf", ffn_input, w_gate, preferred_element_type=jnp.float32)
    upper = jnp.einsum("srd,df->srf", ffn_input, w_up, preferred_element_type=jnp.float32)
    hidden = geglu(gate, upper).astype(jnp.bfloat16)
    feed = row_total(jnp.einsum("srf,fd->srd", hidden, w_down, preferred_element_type=jnp.float32))
    layer_output = (middle + norm_gain(feed, gain_four)).astype(jnp.bfloat16)
    back_attn = load_attention(
        query_weight, key_weight, value_weight, output_weight, gain_table, key_value_begin, kv_cols
    )
    back_ffn = load_ffn(gate_weight, up_weight, down_weight)
    bq_weight, bk_weight, bv_weight, bo_weight = (
        back_attn[0],
        back_attn[1],
        back_attn[2],
        back_attn[3],
    )
    bgate_weight, bup_weight, bdown_weight = back_ffn
    grad_top = cotangent.astype(jnp.float32)
    unused, pull_four = jax.vjp(norm_gain, feed, gain_four)
    grad_feed, grad_g_four = pull_four(grad_top)
    grad_feed_rows = block_rows(grad_feed.astype(jnp.bfloat16))
    grad_hidden = jnp.einsum(
        "srd,fd->srf", grad_feed_rows, bdown_weight, preferred_element_type=jnp.float32
    )
    grad_down_part = jnp.einsum(
        "srf,srd->fd", hidden, grad_feed_rows, preferred_element_type=jnp.float32
    )
    unused, pull_act = jax.vjp(geglu, gate, upper)
    grad_gate_act, grad_up_act = pull_act(grad_hidden)
    grad_gate_act = grad_gate_act.astype(jnp.bfloat16)
    grad_up_act = grad_up_act.astype(jnp.bfloat16)
    grad_rows_part = jnp.einsum(
        "srf,df->srd", grad_gate_act, bgate_weight, preferred_element_type=jnp.float32
    ) + jnp.einsum("srf,df->srd", grad_up_act, bup_weight, preferred_element_type=jnp.float32)
    grad_gate_part = jnp.einsum(
        "srd,srf->df", ffn_input, grad_gate_act, preferred_element_type=jnp.float32
    )
    grad_up_part = jnp.einsum(
        "srd,srf->df", ffn_input, grad_up_act, preferred_element_type=jnp.float32
    )
    ffn_grads = (
        lax.psum_scatter(
            grad_gate_part.astype(jnp.bfloat16), ("dp", "ctx"), scatter_dimension=0, tiled=True
        ).astype(jnp.float32),
        lax.psum_scatter(
            grad_up_part.astype(jnp.bfloat16), ("dp", "ctx"), scatter_dimension=0, tiled=True
        ).astype(jnp.float32),
        lax.psum_scatter(
            grad_down_part.astype(jnp.bfloat16), ("dp", "ctx"), scatter_dimension=1, tiled=True
        ).astype(jnp.float32),
    )
    grad_normed_two = row_total(grad_rows_part)
    unused, pull_three = jax.vjp(norm_gain, middle, gain_three)
    grad_mid_norm, grad_g_three = pull_three(grad_normed_two)
    grad_middle = grad_top + grad_mid_norm
    unused, pull_two = jax.vjp(norm_gain, project, gain_two)
    grad_project, grad_g_two = pull_two(grad_middle)
    grad_project = grad_project.astype(jnp.bfloat16)
    out_back = full_output(bo_weight)
    grad_heads_tok = jnp.einsum(
        "std,ed->ste", grad_project, out_back, preferred_element_type=jnp.float32
    ).astype(jnp.bfloat16)
    grad_output_part = lax.psum_scatter(
        jnp.einsum(
            "ste,std->ed", heads_tok, grad_project, preferred_element_type=jnp.float32
        ).astype(jnp.bfloat16),
        "seq",
        scatter_dimension=0,
        tiled=True,
    )
    grad_heads = lax.all_to_all(grad_heads_tok, "seq", split_axis=2, concat_axis=1, tiled=True)

    def backward_item(carry, pieces):
        key_acc, value_acc = carry
        queries, query_pos, first_row, seq_id, log_part, grad_part = pieces
        key_rows = lax.dynamic_index_in_dim(key_broadcast, seq_id, 0, keepdims=False)
        value_rows = lax.dynamic_index_in_dim(value_broadcast, seq_id, 0, keepdims=False)
        grad_query, grad_key, grad_value = attend_backward(
            queries, key_rows, value_rows, query_pos, first_row, log_part, grad_part
        )
        key_acc = lax.dynamic_update_index_in_dim(
            key_acc,
            lax.dynamic_index_in_dim(key_acc, seq_id, 0, keepdims=False) + grad_key,
            seq_id,
            0,
        )
        value_acc = lax.dynamic_update_index_in_dim(
            value_acc,
            lax.dynamic_index_in_dim(value_acc, seq_id, 0, keepdims=False) + grad_value,
            seq_id,
            0,
        )
        return ((key_acc, value_acc), grad_query)

    empty = jnp.zeros((seqs, full_len, head_cols), jnp.float32)
    (key_terms, value_terms), grad_query_items = lax.scan(
        backward_item,
        (empty, empty),
        (query_rot, positions, block_starts, seq_owner, log_total, grad_heads),
    )
    key_sums, value_sums = (
        lax.psum_scatter(
            key_terms.astype(jnp.bfloat16), "ctx", scatter_dimension=1, tiled=True
        ).astype(jnp.float32),
        lax.psum_scatter(
            value_terms.astype(jnp.bfloat16), "ctx", scatter_dimension=1, tiled=True
        ).astype(jnp.float32),
    )
    grad_query_rot = rounded(grad_query_items.reshape(seqs, block_len, head_count, HEAD_SIZE))
    grad_query_raw = (
        turn_back(grad_query_rot, cosine, sine)
        .astype(jnp.bfloat16)
        .reshape(seqs, block_len, head_cols)
    )
    grad_key_rot = rounded(key_sums.reshape(seqs, block_len, head_count, HEAD_SIZE))
    grad_key_raw = (
        turn_back(grad_key_rot, cosine, sine)
        .astype(jnp.bfloat16)
        .reshape(seqs, block_len, head_cols)
    )
    grad_value_raw = value_sums.astype(jnp.bfloat16)
    key_expand = jnp.repeat(
        bk_weight.reshape(width, kv_heads, HEAD_SIZE), repeat_by, axis=1
    ).reshape(width, head_cols)
    value_expand = jnp.repeat(
        bv_weight.reshape(width, kv_heads, HEAD_SIZE), repeat_by, axis=1
    ).reshape(width, head_cols)
    grad_block_one = jnp.einsum(
        "sre,de->srd", grad_query_raw, bq_weight, preferred_element_type=jnp.float32
    )
    grad_block_one = grad_block_one + jnp.einsum(
        "sre,de->srd", grad_key_raw, key_expand, preferred_element_type=jnp.float32
    )
    grad_block_one = grad_block_one + jnp.einsum(
        "sre,de->srd", grad_value_raw, value_expand, preferred_element_type=jnp.float32
    )
    grad_normed_one = row_total(grad_block_one)
    grad_query_part = jnp.einsum(
        "srd,sre->de", block_one, grad_query_raw, preferred_element_type=jnp.float32
    )
    grad_key_wide = jnp.einsum(
        "srd,sre->de", block_one, grad_key_raw, preferred_element_type=jnp.float32
    )
    grad_value_wide = jnp.einsum(
        "srd,sre->de", block_one, grad_value_raw, preferred_element_type=jnp.float32
    )
    grad_key_part = jnp.sum(
        grad_key_wide.reshape(width, kv_heads, repeat_by, HEAD_SIZE), axis=2
    ).reshape(width, kv_cols)
    grad_value_part = jnp.sum(
        grad_value_wide.reshape(width, kv_heads, repeat_by, HEAD_SIZE), axis=2
    ).reshape(width, kv_cols)
    unused, pull_one = jax.vjp(norm_gain, x_float, gain_one)
    grad_input_norm, grad_g_one = pull_one(grad_normed_one)
    input_grad = (grad_middle + grad_input_norm).astype(jnp.bfloat16)
    gain_grads = jnp.stack([grad_g_one, grad_g_two, grad_g_three, grad_g_four], axis=1)
    attention_gradients = (
        lax.psum_scatter(
            grad_query_part.astype(jnp.bfloat16), ("dp", "ctx"), scatter_dimension=0, tiled=True
        ).astype(jnp.float32),
        lax.psum_scatter(grad_output_part, ("dp", "ctx"), scatter_dimension=1, tiled=True).astype(
            jnp.float32
        ),
    )
    key_spread = lax.dynamic_update_slice_in_dim(
        jnp.zeros((width, KEY_VALUE_HEADS * HEAD_SIZE), jnp.float32),
        grad_key_part,
        key_value_begin,
        1,
    )
    value_spread = lax.dynamic_update_slice_in_dim(
        jnp.zeros((width, KEY_VALUE_HEADS * HEAD_SIZE), jnp.float32),
        grad_value_part,
        key_value_begin,
        1,
    )
    kv_sums = (
        lax.psum_scatter(key_spread, ("dp", "ctx", "seq"), scatter_dimension=0, tiled=True),
        lax.psum_scatter(value_spread, ("dp", "ctx", "seq"), scatter_dimension=0, tiled=True),
        lax.psum_scatter(gain_grads, ("dp", "ctx", "seq"), scatter_dimension=0, tiled=True),
    )
    gain_out = kv_sums[2]
    return (
        layer_output,
        input_grad,
        attention_gradients[0],
        kv_sums[0],
        kv_sums[1],
        attention_gradients[1],
        ffn_grads[0],
        ffn_grads[1],
        ffn_grads[2],
        gain_out[:, 0],
        gain_out[:, 1],
        gain_out[:, 2],
        gain_out[:, 3],
    )


def flip(value, axis):
    return lax.ppermute(value, axis, [(0, 1), (1, 0)])


def ordered(index, own, other, axis=0):
    return jnp.where(
        index == 0, jnp.stack([own, other], axis=axis), jnp.stack([other, own], axis=axis)
    )


def pick(value, index, axis=0):
    return lax.dynamic_index_in_dim(value, index, axis, keepdims=False)


def after(value, *earlier):
    return lax.optimization_barrier((value, *earlier))[0]


def total(kept, *got):
    value = kept.astype(jnp.float32)
    for more in got:
        value = value + more.astype(jnp.float32)
    return value


def trade_sequences(value):
    cy = lax.axis_index("cy")
    return ordered(cy, pick(value, cy), flip(pick(value, 1 - cy), "cy"))


def core_columns(matrices, core):
    parts = []
    for matrix in matrices:
        cols = matrix.shape[1] // 2
        parts.append(lax.dynamic_slice_in_dim(matrix, core * cols, cols, 1))
    return jnp.concatenate(parts, axis=1) if len(parts) > 1 else parts[0]


def start_gather(matrices):
    c = lax.axis_index("core")
    got = flip(core_columns(matrices, 1 - c), "core")
    rows = ordered(c, core_columns(matrices, c), got)
    return rows, flip(rows, "cy"), flip(rows, "dp")


def next_gather(rows, rows_y, rows_x):
    return rows, rows_y, rows_x, flip(rows_y[0], "dp"), flip(rows_x[1], "cy")


def place_kernel(splits, *refs):
    sources, outs = refs[:5], refs[5 : 5 + len(splits)]
    held, sem_in, sem_out = refs[5 + len(splits) : -2], refs[-2], refs[-1]
    x, y = lax.axis_index("dp"), lax.axis_index("cy")
    loads = [
        pltpu.make_async_copy(source, buffer, sem_in.at[i])
        for i, (source, buffer) in enumerate(zip(sources, held))
    ]
    for load in loads:
        load.start()
    stores = []
    for i, (load, buffer) in enumerate(zip(loads, held)):
        load.wait()
        begin = 0
        for out, cols in zip(outs, splits):
            at = pl.ds(begin, cols)
            target = (
                out.at[x, y],
                out.at[x, 1 - y],
                out.at[1 - x, y],
                out.at[1 - x, 1 - y, 0],
                out.at[1 - x, 1 - y, 1],
            )[i]
            piece = buffer.at[:, :, at] if i < 3 else buffer.at[:, at]
            stores.append(pltpu.make_async_copy(piece, target, sem_out.at[len(stores)]))
            stores[-1].start()
            begin += cols
    for store in stores:
        store.wait()


def end_gather(begun, splits):
    rows = begun[0]
    size = 8 * rows.shape[1] * rows.shape[2] * rows.dtype.itemsize
    anywhere = pl.BlockSpec(memory_space=pl.ANY)
    outs = pl.pallas_call(
        functools.partial(place_kernel, splits),
        out_shape=[
            jax.ShapeDtypeStruct((2, 2, 2, rows.shape[1], cols), rows.dtype) for cols in splits
        ],
        in_specs=[anywhere] * 5,
        out_specs=[anywhere] * len(splits),
        scratch_shapes=[pltpu.VMEM(piece.shape, piece.dtype) for piece in begun]
        + [pltpu.SemaphoreType.DMA((5,)), pltpu.SemaphoreType.DMA((5 * len(splits),))],
        compiler_params=pltpu.CompilerParams(vmem_limit_bytes=size + (2 << 20)),
        cost_estimate=pl.CostEstimate(flops=0, bytes_accessed=2 * size, transcendentals=0),
        name="place_rows",
    )(*begun)
    return [out.reshape(-1, out.shape[-1]) for out in outs]


def start_scatter(grad):
    x, y = lax.axis_index("dp"), lax.axis_index("cy")
    parts = grad.reshape(2, 2, 2, -1, grad.shape[-1])
    far = pick(pick(parts, 1 - x), 1 - y)
    return parts, flip(far[0], "dp"), flip(far[1], "cy")


def next_scatter(parts, far_first, far_second):
    x, y = lax.axis_index("dp"), lax.axis_index("cy")
    low = parts.dtype
    by_y, by_x = pick(pick(parts, x), 1 - y), pick(pick(parts, 1 - x), y)
    by_y = jnp.stack([total(by_y[0], far_first).astype(low), by_y[1]])
    by_x = jnp.stack([by_x[0], total(by_x[1], far_second).astype(low)])
    return pick(pick(parts, x), y), flip(by_y, "cy"), flip(by_x, "dp")


def end_scatter(own, from_y, from_x):
    c = lax.axis_index("core")
    sums = total(own, from_y, from_x)
    keep = pick(sums, c)
    got = flip(pick(sums, 1 - c).astype(jnp.bfloat16), "core").astype(jnp.float32)
    return jnp.where(c == 0, keep, got), jnp.where(c == 0, got, keep)


def gather_rows(local_rows):
    width = local_rows.shape[-1]
    return lax.all_gather(local_rows, ("core", "seq"), axis=1, tiled=True).reshape(-1, width)


def core_rows(left, right, dims):
    c = lax.axis_index("core")
    parts = left.reshape(2, 2, -1, left.shape[-1])

    def rows_of(core):
        rows = dot(pick(parts, core, 1).reshape(-1, left.shape[-1]), right, dims)
        return rows.astype(jnp.bfloat16).reshape(2, -1, rows.shape[-1])

    away = rows_of(1 - c)
    got = flip(away, "core")
    kept = lax.optimization_barrier(rows_of(c))
    return total(kept, got).astype(jnp.bfloat16)


def scatter_rows(core_sums):
    return lax.psum_scatter(core_sums, "seq", scatter_dimension=1, tiled=True).astype(jnp.float32)


def dot(left, right, dims):
    return lax.dot_general(
        left, right, ((dims[:1], dims[1:]), ((), ())), preferred_element_type=jnp.float32
    )


def head_scores(queries, keys, visible):
    bent = jnp.tanh(dot(queries, keys, (1, 1)) * (HEAD_SIZE ** (-0.5) / CAP))
    return bent, jnp.where(visible, CAP * bent, -1e30)


def head_local(
    inputs,
    positions,
    query_weight,
    key_weight,
    value_weight,
    output_weight,
    gate_weight,
    up_weight,
    down_weight,
    pre_attn_gain,
    post_attn_gain,
    pre_ffn_gain,
    post_ffn_gain,
    cotangent,
):
    c, cy = lax.axis_index("core"), lax.axis_index("cy")
    low = jnp.bfloat16
    rows_own = query_weight.shape[0]
    ffn_cols = gate_weight.shape[1] // 2

    x_local = trade_sequences(inputs)
    block_x = gather_rows(x_local)
    x_float = x_local.astype(jnp.float32)
    kv_stack = jnp.stack([key_weight, value_weight], axis=1)
    kv_stack = kv_stack.reshape(-1, 2, KEY_VALUE_HEADS, HEAD_SIZE).transpose(2, 0, 1, 3)
    kv_rows = lax.all_to_all(kv_stack, "seq", split_axis=0, concat_axis=0, tiled=True)
    gain_table = jnp.stack([pre_attn_gain, post_attn_gain, pre_ffn_gain, post_ffn_gain], axis=0)
    gain_full = lax.all_gather(gain_table, ("dp", "cy", "core"), axis=1, tiled=True)
    kv_rows = after(kv_rows.reshape(rows_own, 2 * HEAD_SIZE), gain_full)
    gain_one, gain_two, gain_three, gain_four = gain_full.astype(jnp.float32)

    pos_own = trade_sequences(positions)
    seq_pos = ordered(c, pos_own, flip(pos_own, "core"), axis=1).reshape(-1)
    half = HEAD_SIZE // 2
    freq = BASE ** (-jnp.arange(half, dtype=jnp.float32) * 2.0 / HEAD_SIZE)
    angle = seq_pos.astype(jnp.float32)[:, None] * freq
    cosine, sine = jnp.cos(angle), jnp.sin(angle)
    kv_cosine = jnp.where(c == 0, cosine, 1.0)
    kv_sine = jnp.where(c == 0, sine, 0.0)

    attn_begun = next_gather(*start_gather([query_weight, kv_rows, output_weight.T]))
    in_weight, out_weight = end_gather(attn_begun, (2 * HEAD_SIZE, HEAD_SIZE))
    down_begun = start_gather([after(down_weight.T, attn_begun)])
    gate_up_begun = start_gather(after([gate_weight, up_weight], attn_begun))
    cotangent = after(cotangent, attn_begun)
    grad_top = trade_sequences(cotangent)

    block_one = norm_gain(block_x.astype(jnp.float32), gain_one).astype(low)
    raw = dot(block_one, in_weight, (1, 0))
    queries = turn(raw[:, :HEAD_SIZE], cosine, sine).astype(low)
    kv_own = turn(raw[:, HEAD_SIZE:], kv_cosine, kv_sine).astype(low)
    kv_other = flip(kv_own, "core")
    keys = jnp.where(c == 0, kv_own, kv_other)
    values = jnp.where(c == 0, kv_other, kv_own)
    token = jnp.arange(seq_pos.shape[0], dtype=jnp.int32)
    visible = (token[None, :] <= token[:, None]) & (token[None, :] >= (token - seq_pos)[:, None])
    bent, masked = head_scores(queries, keys, visible)
    row_max = jnp.max(masked, axis=-1, keepdims=True)
    exponent = jnp.exp(masked - row_max)
    row_sum = jnp.sum(exponent, axis=-1, keepdims=True)
    heads = dot((exponent / row_sum).astype(low), values, (1, 0)).astype(low)
    log_total = row_max + jnp.log(row_sum)
    heads = after(heads, grad_top, down_begun)
    grad_top = grad_top.astype(jnp.float32)

    project_core = core_rows(heads, out_weight, (1, 1))
    project = scatter_rows(project_core)
    middle = x_float + norm_gain(project, gain_two)
    normed_two = norm_gain(middle, gain_three).astype(low)
    normed_two = after(normed_two, gate_up_begun)
    gate_up_begun = next_gather(*after(gate_up_begun, normed_two))
    down_begun = next_gather(*after(down_begun, normed_two))
    block_two = gather_rows(normed_two)
    (gate_up_weight,) = end_gather(gate_up_begun, (2 * ffn_cols,))
    (down_back,) = end_gather(down_begun, (ffn_cols,))
    gate_up = dot(block_two, gate_up_weight, (1, 0))
    gate, upper = gate_up[:, :ffn_cols], gate_up[:, ffn_cols:]
    hidden = geglu(gate, upper).astype(low)
    feed = scatter_rows(core_rows(hidden, down_back, (1, 1)))
    unused, pull_four = jax.vjp(norm_gain, feed, gain_four)
    grad_feed, grad_g_four = pull_four(grad_top)
    grad_feed = grad_feed.astype(low)
    layer_output = after((middle + norm_gain(feed, gain_four)).astype(low), grad_feed)
    layer_output = trade_sequences(layer_output)

    grad_feed_rows = after(gather_rows(grad_feed), layer_output)
    grad_hidden = dot(grad_feed_rows, down_back, (1, 0))
    unused, pull_act = jax.vjp(geglu, gate, upper)
    grad_gate_act, grad_up_act = pull_act(grad_hidden)
    grad_gate_up = jnp.concatenate([grad_gate_act.astype(low), grad_up_act.astype(low)], axis=1)
    normed_two_core = core_rows(grad_gate_up, gate_up_weight, (1, 1))
    grad_normed_two = scatter_rows(normed_two_core)
    hidden, block_two = after((hidden, block_two), normed_two_core)
    grad_down_begun = start_scatter(dot(grad_feed_rows, hidden, (0, 0)).astype(low))
    grad_gu_begun = start_scatter(dot(block_two, grad_gate_up, (0, 0)).astype(low))

    unused, pull_three = jax.vjp(norm_gain, middle, gain_three)
    grad_mid_norm, grad_g_three = pull_three(grad_normed_two)
    grad_middle = grad_top + grad_mid_norm
    unused, pull_two = jax.vjp(norm_gain, project, gain_two)
    grad_project, grad_g_two = pull_two(grad_middle)
    grad_project = grad_project.astype(low)
    grad_down_begun = next_scatter(*after(grad_down_begun, grad_project))
    grad_gu_begun = next_scatter(*after(grad_gu_begun, grad_project))
    grad_project_rows = gather_rows(grad_project)
    grad_heads = dot(grad_project_rows, out_weight, (1, 0)).astype(low)

    bent, masked = head_scores(queries, keys, visible)
    probability = jnp.exp(masked - log_total)
    grad_value = dot(probability.astype(low), grad_heads, (0, 0)).astype(low)
    grad_prob = dot(grad_heads, values, (1, 1))
    delta = jnp.sum(probability * grad_prob, axis=-1, keepdims=True)
    grad_scores = (probability * (grad_prob - delta) * (1.0 - bent * bent)).astype(low)
    scale = HEAD_SIZE ** (-0.5)
    grad_query_rot = rounded(dot(grad_scores, keys, (1, 0)) * scale)
    grad_key_rot = rounded(dot(grad_scores, queries, (0, 0)) * scale)
    grad_query_raw = turn_back(grad_query_rot, cosine, sine).astype(low)
    grad_key_raw = turn_back(grad_key_rot, cosine, sine).astype(low)
    kv_grad_own = jnp.where(c == 0, grad_key_raw, grad_value)
    kv_grad_got = flip(jnp.where(c == 0, grad_value, grad_key_raw), "core")
    grad_in = jnp.concatenate([grad_query_raw, total(kv_grad_own, kv_grad_got).astype(low)], axis=1)
    normed_one_core = core_rows(grad_in, in_weight, (1, 1))
    grad_normed_one = scatter_rows(normed_one_core)
    block_one, heads = after((block_one, heads), normed_one_core)
    grad_in_part = dot(block_one, grad_in, (0, 0)).astype(low)
    grad_output_part = dot(grad_project_rows, heads, (0, 0)).astype(low)
    attn_grad_begun = start_scatter(jnp.concatenate([grad_in_part, grad_output_part], axis=1))
    attn_grad_begun = next_scatter(*attn_grad_begun)
    grad_down = end_scatter(*after(grad_down_begun, normed_one_core))
    grad_gu = end_scatter(*after(grad_gu_begun, normed_one_core))
    attn_grads = end_scatter(*attn_grad_begun)

    unused, pull_one = jax.vjp(norm_gain, x_float, gain_one)
    grad_input_norm, grad_g_one = pull_one(grad_normed_one)
    input_grad = trade_sequences((grad_middle + grad_input_norm).astype(low))
    gain_grads = jnp.stack([grad_g_one, grad_g_two, grad_g_three, grad_g_four], axis=0)
    everyone = ("dp", "cy", "core", "seq")
    gain_parts = gain_grads.reshape(4, lax.axis_size(everyone), -1).transpose(1, 0, 2)
    gain_out = jnp.sum(
        lax.all_to_all(gain_parts, everyone, split_axis=0, concat_axis=0, tiled=True), axis=0
    )

    def whole(pair, begin, cols):
        return jnp.concatenate([part[:, begin : begin + cols] for part in pair], axis=1)

    kv_back = whole(attn_grads, HEAD_SIZE, HEAD_SIZE).astype(low)
    kv_back = lax.all_to_all(kv_back, "seq", split_axis=0, concat_axis=0, tiled=True)
    kv_back = kv_back.reshape(KEY_VALUE_HEADS, -1, 2, HEAD_SIZE).transpose(2, 1, 0, 3)
    kv_back = kv_back.reshape(2, -1, KEY_VALUE_HEADS * HEAD_SIZE).astype(jnp.float32)
    return (
        layer_output,
        input_grad,
        whole(attn_grads, 0, HEAD_SIZE),
        kv_back[0],
        kv_back[1],
        whole(attn_grads, 2 * HEAD_SIZE, HEAD_SIZE).T,
        whole(grad_gu, 0, ffn_cols),
        whole(grad_gu, ffn_cols, ffn_cols),
        whole(grad_down, 0, ffn_cols).T,
        gain_out[0],
        gain_out[1],
        gain_out[2],
        gain_out[3],
    )


def one_head_each(mesh):
    sizes = mesh.shape
    return (
        sizes["dp"] == 2
        and sizes["ctx"] == 4
        and sizes["seq"] == KEY_VALUE_HEADS
        and QUERY_HEAD_COUNT == 2 * KEY_VALUE_HEADS
    )


def solution(mesh):
    if one_head_each(mesh):
        body, ctx = head_local, ("cy", "core")
        grid = jax.sharding.Mesh(
            mesh.devices.reshape(mesh.shape["dp"], -1, 2, mesh.shape["seq"]),
            ("dp", "cy", "core", "seq"),
        )
    else:
        body, ctx, grid = general_local, ("ctx",), mesh
    owners, everyone = ("dp", *ctx), ("dp", *ctx, "seq")
    rows = P("dp", (*ctx, "seq"), None)
    tall, flat, wide = P(owners, "seq"), P(everyone, None), P("seq", owners)
    gains = (P(owners),) * 4
    return jax.shard_map(
        body,
        mesh=grid,
        in_specs=(rows, P("dp", ctx), tall, flat, flat, wide, tall, tall, wide, *gains, rows),
        out_specs=(rows, rows, tall, flat, flat, wide, tall, tall, wide, *((P(everyone),) * 4)),
        check_vma=False,
    )
```

```python
import functools
import math

import jax
import jax.numpy as jnp
from jax import lax
from jax.experimental import pallas as pl
from jax.experimental.pallas import tpu as pltpu
from jax.sharding import PartitionSpec as P

QUERY_HEAD_COUNT = 8
KEY_VALUE_HEADS = 4
HEAD_SIZE = 256


EPS = 1e-06
CAP = 50.0
BASE = 10000.0


def norm_gain(vector, gain):
    return vector * lax.rsqrt(jnp.mean(vector * vector, axis=-1, keepdims=True) + EPS) * gain


def geglu(gate_in, up_in):
    return jax.nn.gelu(gate_in, approximate=True) * up_in


def rounded(value):
    return lax.optimization_barrier(value.astype(jnp.bfloat16)).astype(jnp.float32)


def angle_tables(block_pos):
    half = HEAD_SIZE // 2
    freq = BASE ** (-jnp.arange(half, dtype=jnp.float32) * 2.0 / HEAD_SIZE)
    angle = block_pos.astype(jnp.float32)[..., None] * freq
    return (jnp.cos(angle)[:, :, None, :], jnp.sin(angle)[:, :, None, :])


def turn(vector, cosine, sine):
    half = HEAD_SIZE // 2
    lower = vector[..., :half]
    upper = vector[..., half:]
    return jnp.concatenate([lower * cosine - upper * sine, upper * cosine + lower * sine], axis=-1)


def turn_back(grad, cosine, sine):
    half = HEAD_SIZE // 2
    lower = grad[..., :half]
    upper = grad[..., half:]
    return jnp.concatenate([lower * cosine + upper * sine, upper * cosine - lower * sine], axis=-1)


def load_attention(
    query_weight, key_weight, value_weight, output_weight, gain_table, key_value_begin, kv_cols
):
    key_full, value_full = (
        lax.all_gather(key_weight, ("dp", "ctx", "seq"), axis=0, tiled=True),
        lax.all_gather(value_weight, ("dp", "ctx", "seq"), axis=0, tiled=True),
    )
    key_part = lax.dynamic_slice_in_dim(key_full, key_value_begin, kv_cols, 1)
    value_part = lax.dynamic_slice_in_dim(value_full, key_value_begin, kv_cols, 1)
    w_query, w_output, gain_full = (
        lax.all_gather(query_weight, ("dp", "ctx"), axis=0, tiled=True),
        lax.all_gather(output_weight, ("dp", "ctx"), axis=1, tiled=True),
        lax.all_gather(gain_table, ("dp", "ctx"), axis=0, tiled=True),
    )
    return (w_query, key_part, value_part, w_output, gain_full)


def load_ffn(w_gate, w_up, w_down):
    return (
        lax.all_gather(w_gate, ("dp", "ctx"), axis=0, tiled=True),
        lax.all_gather(w_up, ("dp", "ctx"), axis=0, tiled=True),
        lax.all_gather(w_down, ("dp", "ctx"), axis=1, tiled=True),
    )


def full_output(output_part):
    return lax.all_gather(output_part, "seq", axis=0, tiled=True)


def block_rows(local_rows):
    return lax.all_gather(local_rows, "seq", axis=1, tiled=True)


def row_total(partial_rows):
    return lax.psum_scatter(
        partial_rows.astype(jnp.bfloat16), "seq", scatter_dimension=1, tiled=True
    ).astype(jnp.float32)


def visible_mask(first_row, row_count, key_count, query_pos):
    query_idx = first_row + jnp.arange(row_count, dtype=jnp.int32)
    key_idx = jnp.arange(key_count, dtype=jnp.int32)
    return (key_idx[None, :] <= query_idx[:, None]) & (
        key_idx[None, :] >= (query_idx - query_pos)[:, None]
    )


def scores_of(queries, key_rows, first_row, query_pos):
    row_count = queries.shape[0]
    head_count = queries.shape[1] // HEAD_SIZE
    query_heads = queries.reshape(row_count, head_count, HEAD_SIZE)
    key_heads = key_rows.reshape(key_rows.shape[0], head_count, HEAD_SIZE)
    scores = jnp.einsum(
        "qhd,khd->hqk", query_heads, key_heads, preferred_element_type=jnp.float32
    ) * HEAD_SIZE ** (-0.5)
    bent = jnp.tanh(scores / CAP)
    visible = visible_mask(first_row, row_count, key_rows.shape[0], query_pos)
    masked = jnp.where(visible[None], CAP * bent, -1e30)
    return (query_heads, key_heads, bent, masked)


def attend_forward(queries, key_rows, value_rows, query_pos, first_row):
    query_heads, key_heads, bent, masked = scores_of(queries, key_rows, first_row, query_pos)
    head_count = query_heads.shape[1]
    value_heads = value_rows.reshape(value_rows.shape[0], head_count, HEAD_SIZE)
    row_max = jnp.max(masked, axis=-1, keepdims=True)
    exponent = jnp.exp(masked - row_max)
    row_sum = jnp.sum(exponent, axis=-1, keepdims=True)
    probability = (exponent / row_sum).astype(jnp.bfloat16)
    log_total = (row_max + jnp.log(row_sum))[..., 0]
    result = jnp.einsum(
        "hqk,khd->qhd", probability, value_heads, preferred_element_type=jnp.float32
    )
    return (
        result.astype(jnp.bfloat16).reshape(queries.shape[0], head_count * HEAD_SIZE),
        log_total,
    )


def attend_backward(queries, key_rows, value_rows, query_pos, first_row, log_total, grad_rows):
    query_heads, key_heads, bent, masked = scores_of(queries, key_rows, first_row, query_pos)
    head_count = query_heads.shape[1]
    value_heads = value_rows.reshape(value_rows.shape[0], head_count, HEAD_SIZE)
    grad_heads = grad_rows.reshape(queries.shape[0], head_count, HEAD_SIZE)
    probability = jnp.exp(masked - log_total[..., None])
    prob_low = probability.astype(jnp.bfloat16)
    grad_value = jnp.einsum(
        "hqk,qhd->khd", prob_low, grad_heads, preferred_element_type=jnp.float32
    )
    grad_prob = jnp.einsum(
        "qhd,khd->hqk", grad_heads, value_heads, preferred_element_type=jnp.float32
    )
    delta = jnp.sum(probability * grad_prob, axis=-1, keepdims=True)
    grad_scores = (probability * (grad_prob - delta) * (1.0 - bent * bent)).astype(jnp.bfloat16)
    grad_query = jnp.einsum(
        "hqk,khd->qhd", grad_scores, key_heads, preferred_element_type=jnp.float32
    ) * HEAD_SIZE ** (-0.5)
    grad_key = jnp.einsum(
        "hqk,qhd->khd", grad_scores, query_heads, preferred_element_type=jnp.float32
    ) * HEAD_SIZE ** (-0.5)
    key_count = key_rows.shape[0]
    return (
        grad_query.reshape(queries.shape[0], head_count * HEAD_SIZE),
        grad_key.reshape(key_count, head_count * HEAD_SIZE),
        grad_value.reshape(key_count, head_count * HEAD_SIZE),
    )


def general_local(
    inputs,
    positions,
    query_weight,
    key_weight,
    value_weight,
    output_weight,
    gate_weight,
    up_weight,
    down_weight,
    pre_attn_gain,
    post_attn_gain,
    pre_ffn_gain,
    post_ffn_gain,
    cotangent,
):
    seqs, tokens, width = inputs.shape
    block_len = positions.shape[1]
    full_len = block_len * lax.axis_size("ctx")
    offset = lax.axis_index("ctx") * block_len
    head_count = QUERY_HEAD_COUNT // lax.axis_size("seq")
    key_value_group = QUERY_HEAD_COUNT // KEY_VALUE_HEADS
    kv_heads = max(head_count // key_value_group, 1)
    kv_cols = kv_heads * HEAD_SIZE
    repeat_by = head_count // kv_heads
    head_cols = head_count * HEAD_SIZE
    key_value_begin = lax.axis_index("seq") * head_count // key_value_group * HEAD_SIZE
    cosine, sine = angle_tables(positions)
    gain_table = jnp.stack([pre_attn_gain, post_attn_gain, pre_ffn_gain, post_ffn_gain], axis=1)
    fwd_attn = load_attention(
        query_weight, key_weight, value_weight, output_weight, gain_table, key_value_begin, kv_cols
    )
    fwd_ffn = load_ffn(gate_weight, up_weight, down_weight)
    w_query, key_matrix, value_matrix, w_output, gain_full = fwd_attn
    w_gate, w_up, w_down = fwd_ffn
    gain_float = gain_full.astype(jnp.float32)
    gain_one = gain_float[:, 0]
    gain_two = gain_float[:, 1]
    gain_three = gain_float[:, 2]
    gain_four = gain_float[:, 3]
    x_float = inputs.astype(jnp.float32)
    normed_one = norm_gain(x_float, gain_one).astype(jnp.bfloat16)
    block_one = block_rows(normed_one)
    query_raw = jnp.einsum("srd,de->sre", block_one, w_query, preferred_element_type=jnp.float32)
    key_raw = jnp.einsum("srd,de->sre", block_one, key_matrix, preferred_element_type=jnp.float32)
    value_raw = jnp.einsum(
        "srd,de->sre", block_one, value_matrix, preferred_element_type=jnp.float32
    )
    query_rot = (
        turn(query_raw.reshape(seqs, block_len, head_count, HEAD_SIZE), cosine, sine)
        .astype(jnp.bfloat16)
        .reshape(seqs, block_len, head_cols)
    )
    key_rot = (
        turn(key_raw.reshape(seqs, block_len, kv_heads, HEAD_SIZE), cosine, sine)
        .astype(jnp.bfloat16)
        .reshape(seqs, block_len, kv_cols)
    )
    key_all, value_all = (
        lax.all_gather(key_rot, "ctx", axis=1, tiled=True),
        lax.all_gather(value_raw.astype(jnp.bfloat16), "ctx", axis=1, tiled=True),
    )
    key_broadcast = jnp.repeat(
        key_all.reshape(seqs, full_len, kv_heads, HEAD_SIZE), repeat_by, axis=2
    ).reshape(seqs, full_len, head_cols)
    value_broadcast = jnp.repeat(
        value_all.reshape(seqs, full_len, kv_heads, HEAD_SIZE), repeat_by, axis=2
    ).reshape(seqs, full_len, head_cols)
    query_block = math.gcd(block_len, 512)
    block_count = block_len // query_block
    item_count = seqs * block_count
    item_index = jnp.arange(item_count, dtype=jnp.int32)
    block_starts = offset + item_index % block_count * query_block
    seq_owner = item_index // block_count

    def forward_item(pieces):
        queries, query_pos, first_row, seq_id = pieces
        key_rows = lax.dynamic_index_in_dim(key_broadcast, seq_id, 0, keepdims=False)
        value_rows = lax.dynamic_index_in_dim(value_broadcast, seq_id, 0, keepdims=False)
        return attend_forward(queries, key_rows, value_rows, query_pos, first_row)

    head_items, log_total = lax.map(forward_item, (query_rot, positions, block_starts, seq_owner))
    out_full = full_output(w_output)
    heads_tok = lax.all_to_all(head_items, "seq", split_axis=1, concat_axis=2, tiled=True)
    project = jnp.einsum("ste,ed->std", heads_tok, out_full, preferred_element_type=jnp.float32)
    middle = x_float + norm_gain(project, gain_two)
    normed_two = norm_gain(middle, gain_three).astype(jnp.bfloat16)
    ffn_input = block_rows(normed_two)
    gate = jnp.einsum("srd,df->srf", ffn_input, w_gate, preferred_element_type=jnp.float32)
    upper = jnp.einsum("srd,df->srf", ffn_input, w_up, preferred_element_type=jnp.float32)
    hidden = geglu(gate, upper).astype(jnp.bfloat16)
    feed = row_total(jnp.einsum("srf,fd->srd", hidden, w_down, preferred_element_type=jnp.float32))
    layer_output = (middle + norm_gain(feed, gain_four)).astype(jnp.bfloat16)
    back_attn = load_attention(
        query_weight, key_weight, value_weight, output_weight, gain_table, key_value_begin, kv_cols
    )
    back_ffn = load_ffn(gate_weight, up_weight, down_weight)
    bq_weight, bk_weight, bv_weight, bo_weight = (
        back_attn[0],
        back_attn[1],
        back_attn[2],
        back_attn[3],
    )
    bgate_weight, bup_weight, bdown_weight = back_ffn
    grad_top = cotangent.astype(jnp.float32)
    unused, pull_four = jax.vjp(norm_gain, feed, gain_four)
    grad_feed, grad_g_four = pull_four(grad_top)
    grad_feed_rows = block_rows(grad_feed.astype(jnp.bfloat16))
    grad_hidden = jnp.einsum(
        "srd,fd->srf", grad_feed_rows, bdown_weight, preferred_element_type=jnp.float32
    )
    grad_down_part = jnp.einsum(
        "srf,srd->fd", hidden, grad_feed_rows, preferred_element_type=jnp.float32
    )
    unused, pull_act = jax.vjp(geglu, gate, upper)
    grad_gate_act, grad_up_act = pull_act(grad_hidden)
    grad_gate_act = grad_gate_act.astype(jnp.bfloat16)
    grad_up_act = grad_up_act.astype(jnp.bfloat16)
    grad_rows_part = jnp.einsum(
        "srf,df->srd", grad_gate_act, bgate_weight, preferred_element_type=jnp.float32
    ) + jnp.einsum("srf,df->srd", grad_up_act, bup_weight, preferred_element_type=jnp.float32)
    grad_gate_part = jnp.einsum(
        "srd,srf->df", ffn_input, grad_gate_act, preferred_element_type=jnp.float32
    )
    grad_up_part = jnp.einsum(
        "srd,srf->df", ffn_input, grad_up_act, preferred_element_type=jnp.float32
    )
    ffn_grads = (
        lax.psum_scatter(
            grad_gate_part.astype(jnp.bfloat16), ("dp", "ctx"), scatter_dimension=0, tiled=True
        ).astype(jnp.float32),
        lax.psum_scatter(
            grad_up_part.astype(jnp.bfloat16), ("dp", "ctx"), scatter_dimension=0, tiled=True
        ).astype(jnp.float32),
        lax.psum_scatter(
            grad_down_part.astype(jnp.bfloat16), ("dp", "ctx"), scatter_dimension=1, tiled=True
        ).astype(jnp.float32),
    )
    grad_normed_two = row_total(grad_rows_part)
    unused, pull_three = jax.vjp(norm_gain, middle, gain_three)
    grad_mid_norm, grad_g_three = pull_three(grad_normed_two)
    grad_middle = grad_top + grad_mid_norm
    unused, pull_two = jax.vjp(norm_gain, project, gain_two)
    grad_project, grad_g_two = pull_two(grad_middle)
    grad_project = grad_project.astype(jnp.bfloat16)
    out_back = full_output(bo_weight)
    grad_heads_tok = jnp.einsum(
        "std,ed->ste", grad_project, out_back, preferred_element_type=jnp.float32
    ).astype(jnp.bfloat16)
    grad_output_part = lax.psum_scatter(
        jnp.einsum(
            "ste,std->ed", heads_tok, grad_project, preferred_element_type=jnp.float32
        ).astype(jnp.bfloat16),
        "seq",
        scatter_dimension=0,
        tiled=True,
    )
    grad_heads = lax.all_to_all(grad_heads_tok, "seq", split_axis=2, concat_axis=1, tiled=True)

    def backward_item(carry, pieces):
        key_acc, value_acc = carry
        queries, query_pos, first_row, seq_id, log_part, grad_part = pieces
        key_rows = lax.dynamic_index_in_dim(key_broadcast, seq_id, 0, keepdims=False)
        value_rows = lax.dynamic_index_in_dim(value_broadcast, seq_id, 0, keepdims=False)
        grad_query, grad_key, grad_value = attend_backward(
            queries, key_rows, value_rows, query_pos, first_row, log_part, grad_part
        )
        key_acc = lax.dynamic_update_index_in_dim(
            key_acc,
            lax.dynamic_index_in_dim(key_acc, seq_id, 0, keepdims=False) + grad_key,
            seq_id,
            0,
        )
        value_acc = lax.dynamic_update_index_in_dim(
            value_acc,
            lax.dynamic_index_in_dim(value_acc, seq_id, 0, keepdims=False) + grad_value,
            seq_id,
            0,
        )
        return ((key_acc, value_acc), grad_query)

    empty = jnp.zeros((seqs, full_len, head_cols), jnp.float32)
    (key_terms, value_terms), grad_query_items = lax.scan(
        backward_item,
        (empty, empty),
        (query_rot, positions, block_starts, seq_owner, log_total, grad_heads),
    )
    key_sums, value_sums = (
        lax.psum_scatter(
            key_terms.astype(jnp.bfloat16), "ctx", scatter_dimension=1, tiled=True
        ).astype(jnp.float32),
        lax.psum_scatter(
            value_terms.astype(jnp.bfloat16), "ctx", scatter_dimension=1, tiled=True
        ).astype(jnp.float32),
    )
    grad_query_rot = rounded(grad_query_items.reshape(seqs, block_len, head_count, HEAD_SIZE))
    grad_query_raw = (
        turn_back(grad_query_rot, cosine, sine)
        .astype(jnp.bfloat16)
        .reshape(seqs, block_len, head_cols)
    )
    grad_key_rot = rounded(key_sums.reshape(seqs, block_len, head_count, HEAD_SIZE))
    grad_key_raw = (
        turn_back(grad_key_rot, cosine, sine)
        .astype(jnp.bfloat16)
        .reshape(seqs, block_len, head_cols)
    )
    grad_value_raw = value_sums.astype(jnp.bfloat16)
    key_expand = jnp.repeat(
        bk_weight.reshape(width, kv_heads, HEAD_SIZE), repeat_by, axis=1
    ).reshape(width, head_cols)
    value_expand = jnp.repeat(
        bv_weight.reshape(width, kv_heads, HEAD_SIZE), repeat_by, axis=1
    ).reshape(width, head_cols)
    grad_block_one = jnp.einsum(
        "sre,de->srd", grad_query_raw, bq_weight, preferred_element_type=jnp.float32
    )
    grad_block_one = grad_block_one + jnp.einsum(
        "sre,de->srd", grad_key_raw, key_expand, preferred_element_type=jnp.float32
    )
    grad_block_one = grad_block_one + jnp.einsum(
        "sre,de->srd", grad_value_raw, value_expand, preferred_element_type=jnp.float32
    )
    grad_normed_one = row_total(grad_block_one)
    grad_query_part = jnp.einsum(
        "srd,sre->de", block_one, grad_query_raw, preferred_element_type=jnp.float32
    )
    grad_key_wide = jnp.einsum(
        "srd,sre->de", block_one, grad_key_raw, preferred_element_type=jnp.float32
    )
    grad_value_wide = jnp.einsum(
        "srd,sre->de", block_one, grad_value_raw, preferred_element_type=jnp.float32
    )
    grad_key_part = jnp.sum(
        grad_key_wide.reshape(width, kv_heads, repeat_by, HEAD_SIZE), axis=2
    ).reshape(width, kv_cols)
    grad_value_part = jnp.sum(
        grad_value_wide.reshape(width, kv_heads, repeat_by, HEAD_SIZE), axis=2
    ).reshape(width, kv_cols)
    unused, pull_one = jax.vjp(norm_gain, x_float, gain_one)
    grad_input_norm, grad_g_one = pull_one(grad_normed_one)
    input_grad = (grad_middle + grad_input_norm).astype(jnp.bfloat16)
    gain_grads = jnp.stack([grad_g_one, grad_g_two, grad_g_three, grad_g_four], axis=1)
    attention_gradients = (
        lax.psum_scatter(
            grad_query_part.astype(jnp.bfloat16), ("dp", "ctx"), scatter_dimension=0, tiled=True
        ).astype(jnp.float32),
        lax.psum_scatter(grad_output_part, ("dp", "ctx"), scatter_dimension=1, tiled=True).astype(
            jnp.float32
        ),
    )
    key_spread = lax.dynamic_update_slice_in_dim(
        jnp.zeros((width, KEY_VALUE_HEADS * HEAD_SIZE), jnp.float32),
        grad_key_part,
        key_value_begin,
        1,
    )
    value_spread = lax.dynamic_update_slice_in_dim(
        jnp.zeros((width, KEY_VALUE_HEADS * HEAD_SIZE), jnp.float32),
        grad_value_part,
        key_value_begin,
        1,
    )
    kv_sums = (
        lax.psum_scatter(key_spread, ("dp", "ctx", "seq"), scatter_dimension=0, tiled=True),
        lax.psum_scatter(value_spread, ("dp", "ctx", "seq"), scatter_dimension=0, tiled=True),
        lax.psum_scatter(gain_grads, ("dp", "ctx", "seq"), scatter_dimension=0, tiled=True),
    )
    gain_out = kv_sums[2]
    return (
        layer_output,
        input_grad,
        attention_gradients[0],
        kv_sums[0],
        kv_sums[1],
        attention_gradients[1],
        ffn_grads[0],
        ffn_grads[1],
        ffn_grads[2],
        gain_out[:, 0],
        gain_out[:, 1],
        gain_out[:, 2],
        gain_out[:, 3],
    )


def flip(value, axis):
    return lax.ppermute(value, axis, [(0, 1), (1, 0)])


def ordered(index, own, other, axis=0):
    return jnp.where(
        index == 0, jnp.stack([own, other], axis=axis), jnp.stack([other, own], axis=axis)
    )


def pick(value, index, axis=0):
    return lax.dynamic_index_in_dim(value, index, axis, keepdims=False)


def after(value, *earlier):
    return lax.optimization_barrier((value, *earlier))[0]


def total(kept, *got):
    value = kept.astype(jnp.float32)
    for more in got:
        value = value + more.astype(jnp.float32)
    return value


def trade_sequences(value):
    cy = lax.axis_index("cy")
    return ordered(cy, pick(value, cy), flip(pick(value, 1 - cy), "cy"))


def core_columns(matrices, core):
    parts = []
    for matrix, begin, width in matrices:
        at = core * (matrix.shape[1] // 2) + begin
        parts.append(lax.dynamic_slice_in_dim(matrix, at, width, 1))
    return jnp.concatenate(parts, axis=1) if len(parts) > 1 else parts[0]


def start_gather(*matrices):
    c = lax.axis_index("core")
    got = flip(core_columns(matrices, 1 - c), "core")
    rows = ordered(c, core_columns(matrices, c), got)
    return rows, flip(rows, "cy"), flip(rows, "dp")


def next_gather(rows, rows_y, rows_x):
    return rows, rows_y, rows_x, flip(rows_y[0], "dp"), flip(rows_x[1], "cy")


def place_kernel(moves, count, *refs):
    sources, outs = refs[:count], refs[count : len(refs) - count - 2]
    held, sem_in, sem_out = refs[-count - 2 : -2], refs[-2], refs[-1]
    x, y = lax.axis_index("dp"), lax.axis_index("cy")
    loads = [
        pltpu.make_async_copy(source, buffer, sem_in.at[i])
        for i, (source, buffer) in enumerate(zip(sources, held))
    ]
    for load in loads:
        load.start()
    stores = []
    for i, (load, buffer) in enumerate(zip(loads, held)):
        load.wait()
        for out, begin, to, cols in moves[i // 5]:
            out, to = outs[out], pl.ds(to, cols)
            target = (
                out.at[x, y, :, :, to],
                out.at[x, 1 - y, :, :, to],
                out.at[1 - x, y, :, :, to],
                out.at[1 - x, 1 - y, 0, :, to],
                out.at[1 - x, 1 - y, 1, :, to],
            )[i % 5]
            at = pl.ds(begin, cols)
            piece = buffer.at[:, :, at] if i % 5 < 3 else buffer.at[:, at]
            stores.append(pltpu.make_async_copy(piece, target, sem_out.at[len(stores)]))
            stores[-1].start()
    for store in stores:
        store.wait()


def end_gather(gathers, moves, widths):
    pieces = [piece for begun in gathers for piece in begun]
    rows, low = pieces[0].shape[1], pieces[0].dtype
    size = 8 * rows * sum(widths) * low.itemsize
    anywhere = pl.BlockSpec(memory_space=pl.ANY)
    stores = 5 * sum(len(some) for some in moves)
    outs = pl.pallas_call(
        functools.partial(place_kernel, moves, len(pieces)),
        out_shape=[jax.ShapeDtypeStruct((2, 2, 2, rows, width), low) for width in widths],
        in_specs=[anywhere] * len(pieces),
        out_specs=[anywhere] * len(widths),
        scratch_shapes=[pltpu.VMEM(piece.shape, low) for piece in pieces]
        + [pltpu.SemaphoreType.DMA((len(pieces),)), pltpu.SemaphoreType.DMA((stores,))],
        compiler_params=pltpu.CompilerParams(vmem_limit_bytes=size + (2 << 20)),
        cost_estimate=pl.CostEstimate(flops=0, bytes_accessed=2 * size, transcendentals=0),
        name="place_rows",
    )(*pieces)
    return [out.reshape(-1, out.shape[-1]) for out in outs]


def start_scatter(grad):
    x, y = lax.axis_index("dp"), lax.axis_index("cy")
    parts = grad.reshape(2, 2, 2, -1, grad.shape[-1])
    return parts, pick(parts, 1 - x)[:, 0], pick(parts, 1 - y, 1)[:, 1]


def send_scatter(parts, by_x, by_y):
    return parts, flip(by_x, "dp"), flip(by_y, "cy")


def next_scatter(parts, from_x, from_y):
    x, y = lax.axis_index("dp"), lax.axis_index("cy")
    by_y = total(pick(pick(parts, x), 1 - y)[0], pick(from_x, 1 - y)).astype(parts.dtype)
    by_x = total(pick(pick(parts, 1 - x), y)[1], pick(from_y, 1 - x)).astype(parts.dtype)
    return parts, from_x, from_y, flip(by_y, "cy"), flip(by_x, "dp")


def end_scatter(parts, from_x, from_y, last_y, last_x):
    x, y, c = lax.axis_index("dp"), lax.axis_index("cy"), lax.axis_index("core")
    own = pick(pick(parts, x), y)
    first = total(own[0], pick(from_x, y), last_y)
    second = total(own[1], pick(from_y, x), last_x)
    keep = jnp.where(c == 0, first, second)
    away = jnp.where(c == 0, second, first).astype(jnp.bfloat16)
    got = flip(away, "core").astype(jnp.float32)
    return jnp.where(c == 0, keep, got), jnp.where(c == 0, got, keep)


def gather_gains(table):
    table = ordered(lax.axis_index("core"), table, flip(table, "core"), axis=1)
    table = ordered(lax.axis_index("cy"), table, flip(table, "cy"), axis=1)
    table = ordered(lax.axis_index("dp"), table, flip(table, "dp"), axis=1)
    return table.reshape(table.shape[0], -1)


def exchange_seq(parts):
    z, size = lax.axis_index("seq"), lax.axis_size("seq")
    got = [pick(parts, z)]
    for step in range(1, size):
        ring = [(i, (i + step) % size) for i in range(size)]
        got.insert(0, lax.ppermute(pick(parts, lax.rem(z + step, size)), "seq", ring))
    got = jnp.stack(got + got[:-1])
    return lax.dynamic_slice_in_dim(got, size - 1 - z, size, 0)


def shift(value, step):
    size = lax.axis_size("seq")
    return lax.ppermute(value, "seq", [(i, (i + step) % size) for i in range(size)])


def gather_rows(local_rows):
    size = lax.axis_size("seq")
    got = {step: shift(local_rows, step) for step in (2, 1, 3)}
    pieces = [local_rows] + [got[size - ahead] for ahead in range(1, size)]
    return jnp.concatenate(pieces + [flip(piece, "core") for piece in pieces])


def gather_first(local_rows):
    c, z, size = lax.axis_index("core"), lax.axis_index("seq"), lax.axis_size("seq")
    whole = lax.all_gather(local_rows, ("core", "seq"), axis=0)
    order = [(core, ahead) for core in (c, 1 - c) for ahead in range(size)]
    return jnp.concatenate([pick(whole, core * size + lax.rem(z + i, size)) for core, i in order])


def row_tokens(rows, length):
    c, z, size = lax.axis_index("core"), lax.axis_index("seq"), lax.axis_size("seq")
    shape = (2, size, 2, rows // 2)
    core = jnp.where(lax.broadcasted_iota(jnp.int32, shape, 0) == 0, c, 1 - c)
    owner = lax.rem(z + lax.broadcasted_iota(jnp.int32, shape, 1), size)
    begin = lax.broadcasted_iota(jnp.int32, shape, 2) * (length // 2)
    row = lax.broadcasted_iota(jnp.int32, shape, 3)
    return (begin + (core * size + owner) * (rows // 2) + row).reshape(-1)


def row_order(values):
    c, z, size = lax.axis_index("core"), lax.axis_index("seq"), lax.axis_size("seq")
    parts = values.reshape(2, 2, size, -1).transpose(1, 2, 0, 3)
    parts = jnp.stack([pick(parts, c), pick(parts, 1 - c)])
    parts = jnp.concatenate([parts, parts], axis=1)
    return lax.dynamic_slice_in_dim(parts, z, size, 1).reshape(-1)


def core_swap(value):
    half = value.shape[0] // 2
    got = flip(value, "core")
    return jnp.concatenate([got[half:], got[:half]])


def core_rows(left, right, dims):
    half = left.shape[0] // 2
    got = flip(dot(left[half:], right, dims).astype(jnp.bfloat16), "core")
    kept = lax.optimization_barrier(dot(left[:half], right, dims).astype(jnp.bfloat16))
    return total(kept, got).astype(jnp.bfloat16)


def core_sums(partial_rows):
    half = partial_rows.shape[0] // 2
    return total(partial_rows[:half], flip(partial_rows[half:], "core")).astype(jnp.bfloat16)


def scatter_rows(sums):
    size = lax.axis_size("seq")
    parts = sums.reshape(size, -1, sums.shape[-1])
    got = [shift(parts[step], step) for step in (2, 1, 3)]
    return total(parts[0], *got)


def chip_rows(*matrices):
    c = lax.axis_index("core")
    got = flip(core_columns(matrices, 1 - c), "core")
    return ordered(c, core_columns(matrices, c), got)


def gather_chips(rows):
    whole = lax.all_gather(rows.reshape(-1, rows.shape[-1]), ("dp", "cy"), axis=0, tiled=True)
    return whole


def scatter_chips(grad):
    sums = lax.psum_scatter(grad, ("dp", "cy"), scatter_dimension=0, tiled=True)
    return sums.reshape(2, -1, sums.shape[-1])


def both_columns(sums):
    c = lax.axis_index("core")
    keep = pick(sums, c).astype(jnp.float32)
    got = flip(pick(sums, 1 - c), "core").astype(jnp.float32)
    return jnp.where(c == 0, keep, got), jnp.where(c == 0, got, keep)


def dot(left, right, dims):
    return lax.dot_general(
        left, right, ((dims[:1], dims[1:]), ((), ())), preferred_element_type=jnp.float32
    )


def head_scores(queries, keys, visible):
    bent = jnp.tanh(dot(queries, keys, (1, 1)) * (HEAD_SIZE ** (-0.5) / CAP))
    return bent, jnp.where(visible, CAP * bent, -1e30)


def head_local(
    inputs,
    positions,
    query_weight,
    key_weight,
    value_weight,
    output_weight,
    gate_weight,
    up_weight,
    down_weight,
    pre_attn_gain,
    post_attn_gain,
    pre_ffn_gain,
    post_ffn_gain,
    cotangent,
):
    c, cy = lax.axis_index("core"), lax.axis_index("cy")
    low = jnp.bfloat16
    rows_own = query_weight.shape[0]
    ffn_cols = gate_weight.shape[1] // 2

    kv_stack = jnp.stack([key_weight, value_weight], axis=1)
    kv_stack = kv_stack.reshape(-1, 2, KEY_VALUE_HEADS, HEAD_SIZE).transpose(2, 0, 1, 3)
    kv_rows = exchange_seq(kv_stack).reshape(rows_own, 2 * HEAD_SIZE)
    x_local = after(trade_sequences(inputs), kv_rows)
    own_shape = x_local.shape
    x_local = x_local.reshape(-1, x_local.shape[-1])
    block_x = gather_first(x_local)
    x_float = x_local.astype(jnp.float32)
    gain_table = jnp.stack([pre_attn_gain, post_attn_gain, pre_ffn_gain, post_ffn_gain], axis=0)
    gain_one, gain_two, gain_three, gain_four = gather_gains(gain_table).astype(jnp.float32)

    pos_own = trade_sequences(positions)
    seq_pos = ordered(c, pos_own, flip(pos_own, "core"), axis=1).reshape(-1)
    half = HEAD_SIZE // 2
    freq = BASE ** (-jnp.arange(half, dtype=jnp.float32) * 2.0 / HEAD_SIZE)
    token = row_tokens(x_local.shape[0], seq_pos.shape[0])
    seq_pos = row_order(seq_pos)
    angle = seq_pos.astype(jnp.float32)[:, None] * freq
    cosine, sine = jnp.cos(angle), jnp.sin(angle)
    kv_cosine = jnp.where(c == 0, cosine, 1.0)
    kv_sine = jnp.where(c == 0, sine, 0.0)

    attn_begun = next_gather(
        *start_gather(
            (query_weight, 0, HEAD_SIZE), (kv_rows, 0, HEAD_SIZE), (output_weight.T, 0, HEAD_SIZE)
        )
    )
    split = 2 * HEAD_SIZE
    in_weight, out_weight = end_gather(
        [attn_begun], [((0, 0, 0, split), (1, split, 0, HEAD_SIZE))], (split, HEAD_SIZE)
    )
    gate_up_rows = chip_rows((gate_weight, 0, ffn_cols), (up_weight, 0, ffn_cols))
    gate_up_weight = gather_chips(after(gate_up_rows, attn_begun[:3]))
    down_back = gather_chips(chip_rows((down_weight.T, 0, ffn_cols)))
    grad_top = trade_sequences(after(cotangent, attn_begun))

    block_one = norm_gain(block_x.astype(jnp.float32), gain_one).astype(low)
    raw = dot(block_one, in_weight, (1, 0))
    queries = turn(raw[:, :HEAD_SIZE], cosine, sine).astype(low)
    kv_own = turn(raw[:, HEAD_SIZE:], kv_cosine, kv_sine).astype(low)
    kv_other = core_swap(kv_own)
    keys = jnp.where(c == 0, kv_own, kv_other)
    values = jnp.where(c == 0, kv_other, kv_own)
    visible = (token[None, :] <= token[:, None]) & (token[None, :] >= (token - seq_pos)[:, None])
    bent, masked = head_scores(queries, keys, visible)
    row_max = jnp.max(masked, axis=-1, keepdims=True)
    exponent = jnp.exp(masked - row_max)
    row_sum = jnp.sum(exponent, axis=-1, keepdims=True)
    heads = dot((exponent / row_sum).astype(low), values, (1, 0)).astype(low)
    log_total = row_max + jnp.log(row_sum)
    heads = after(heads, grad_top)
    grad_top = grad_top.reshape(x_local.shape).astype(jnp.float32)

    project_core = core_rows(heads, out_weight, (1, 1))
    project = scatter_rows(project_core)
    middle = x_float + norm_gain(project, gain_two)
    normed_two = norm_gain(middle, gain_three).astype(low)
    block_two = gather_rows(normed_two)
    gate_up = dot(block_two, gate_up_weight, (1, 0))
    gate, upper = gate_up[:, :ffn_cols], gate_up[:, ffn_cols:]
    hidden = geglu(gate, upper).astype(low)
    feed = scatter_rows(core_rows(hidden, down_back, (1, 1)))
    unused, pull_four = jax.vjp(norm_gain, feed, gain_four)
    grad_feed, grad_g_four = pull_four(grad_top)
    grad_feed = grad_feed.astype(low)
    layer_output = after((middle + norm_gain(feed, gain_four)).astype(low), grad_feed)
    layer_output = trade_sequences(layer_output.reshape(own_shape))

    grad_feed_rows = after(gather_rows(grad_feed), layer_output)
    grad_hidden = dot(grad_feed_rows, down_back, (1, 0))
    unused, pull_act = jax.vjp(geglu, gate, upper)
    grad_gate_act, grad_up_act = pull_act(grad_hidden)
    grad_gate_up = jnp.concatenate([grad_gate_act.astype(low), grad_up_act.astype(low)], axis=1)
    normed_two_core = core_rows(grad_gate_up, gate_up_weight, (1, 1))
    grad_normed_two = scatter_rows(normed_two_core)
    late = after((hidden, block_two), normed_two_core)
    grad_down = dot(grad_feed_rows, late[0], (0, 0)).astype(low)
    grad_gu = dot(late[1], grad_gate_up, (0, 0)).astype(low)
    grad_normed_two = after(grad_normed_two, grad_down, grad_gu)
    grad_down, grad_gu = scatter_chips(grad_down), scatter_chips(grad_gu)

    unused, pull_three = jax.vjp(norm_gain, middle, gain_three)
    grad_mid_norm, grad_g_three = pull_three(grad_normed_two)
    grad_middle = grad_top + grad_mid_norm
    unused, pull_two = jax.vjp(norm_gain, project, gain_two)
    grad_project, grad_g_two = pull_two(grad_middle)
    grad_project = grad_project.astype(low)
    grad_project_rows = gather_rows(grad_project)
    grad_heads = dot(grad_project_rows, out_weight, (1, 0)).astype(low)

    bent, masked = head_scores(queries, keys, visible)
    probability = jnp.exp(masked - log_total)
    grad_value = dot(probability.astype(low), grad_heads, (0, 0)).astype(low)
    grad_prob = dot(grad_heads, values, (1, 1))
    delta = jnp.sum(probability * grad_prob, axis=-1, keepdims=True)
    grad_scores = (probability * (grad_prob - delta) * (1.0 - bent * bent)).astype(low)
    scale = HEAD_SIZE ** (-0.5)
    grad_query_rot = rounded(dot(grad_scores, keys, (1, 0)) * scale)
    grad_key_rot = rounded(dot(grad_scores, queries, (0, 0)) * scale)
    grad_query_raw = turn_back(grad_query_rot, cosine, sine).astype(low)
    grad_key_raw = turn_back(grad_key_rot, cosine, sine).astype(low)
    kv_grad_own = jnp.where(c == 0, grad_key_raw, grad_value)
    kv_grad_got = core_swap(jnp.where(c == 0, grad_value, grad_key_raw))
    grad_in = jnp.concatenate([grad_query_raw, total(kv_grad_own, kv_grad_got).astype(low)], axis=1)
    normed_one_part = dot(grad_in, in_weight, (1, 1)).astype(low)
    normed_one_core = core_sums(normed_one_part)
    grad_normed_one = scatter_rows(normed_one_core)
    block_one, heads = after((block_one, heads), normed_one_core)
    grad_in_part = dot(block_one, grad_in, (0, 0)).astype(low)
    grad_output_part = dot(grad_project_rows, heads, (0, 0)).astype(low)
    attn_grad_begun = start_scatter(jnp.concatenate([grad_in_part, grad_output_part], axis=1))
    attn_grad_begun = send_scatter(*attn_grad_begun)
    grad_normed_one = after(grad_normed_one, attn_grad_begun)
    attn_grad_begun = next_scatter(*attn_grad_begun)
    attn_grads = end_scatter(*attn_grad_begun)
    grad_down, grad_gu = after((grad_down, grad_gu), attn_grad_begun)
    grad_down, grad_gu = both_columns(grad_down), both_columns(grad_gu)

    block_x = after(block_x, attn_grad_begun[0]).astype(jnp.float32)
    unused, pull_gain = jax.vjp(lambda gain: norm_gain(block_x, gain), gain_one)
    (grad_g_one,) = pull_gain(normed_one_part.astype(jnp.float32))
    everyone = ("dp", "cy", "core", "seq")
    gain_grads = jnp.stack([grad_g_one, grad_g_two, grad_g_three, grad_g_four], axis=0)
    gain_grads = after(gain_grads, grad_normed_one)
    gain_parts = gain_grads.reshape(4, lax.axis_size(everyone), -1).transpose(1, 0, 2)
    gain_out = jnp.sum(
        lax.all_to_all(gain_parts, everyone, split_axis=0, concat_axis=0, tiled=True), axis=0
    )

    unused, pull_one = jax.vjp(lambda rows: norm_gain(rows, gain_one), x_float)
    (grad_input_norm,) = pull_one(grad_normed_one)
    input_grad = trade_sequences((grad_middle + grad_input_norm).astype(low).reshape(own_shape))

    def whole(pair, begin, cols):
        return jnp.concatenate([part[:, begin : begin + cols] for part in pair], axis=1)

    kv_back = whole(attn_grads, HEAD_SIZE, HEAD_SIZE).astype(low)
    kv_back = exchange_seq(kv_back.reshape(KEY_VALUE_HEADS, -1, 2 * HEAD_SIZE))
    kv_back = kv_back.reshape(KEY_VALUE_HEADS, -1, 2, HEAD_SIZE).transpose(2, 1, 0, 3)
    kv_back = kv_back.reshape(2, -1, KEY_VALUE_HEADS * HEAD_SIZE).astype(jnp.float32)
    return (
        layer_output,
        input_grad,
        whole(attn_grads, 0, HEAD_SIZE),
        kv_back[0],
        kv_back[1],
        whole(attn_grads, 2 * HEAD_SIZE, HEAD_SIZE).T,
        whole(grad_gu, 0, ffn_cols),
        whole(grad_gu, ffn_cols, ffn_cols),
        whole(grad_down, 0, ffn_cols).T,
        gain_out[0],
        gain_out[1],
        gain_out[2],
        gain_out[3],
    )


def one_head_each(mesh):
    sizes = mesh.shape
    return (
        sizes["dp"] == 2
        and sizes["ctx"] == 4
        and sizes["seq"] == KEY_VALUE_HEADS
        and QUERY_HEAD_COUNT == 2 * KEY_VALUE_HEADS
    )


def solution(mesh):
    if one_head_each(mesh):
        body, ctx = head_local, ("cy", "core")
        grid = jax.sharding.Mesh(
            mesh.devices.reshape(mesh.shape["dp"], -1, 2, mesh.shape["seq"]),
            ("dp", "cy", "core", "seq"),
        )
    else:
        body, ctx, grid = general_local, ("ctx",), mesh
    owners, everyone = ("dp", *ctx), ("dp", *ctx, "seq")
    rows = P("dp", (*ctx, "seq"), None)
    tall, flat, wide = P(owners, "seq"), P(everyone, None), P("seq", owners)
    gains = (P(owners),) * 4
    return jax.shard_map(
        body,
        mesh=grid,
        in_specs=(rows, P("dp", ctx), tall, flat, flat, wide, tall, tall, wide, *gains, rows),
        out_specs=(rows, rows, tall, flat, flat, wide, tall, tall, wide, *((P(everyone),) * 4)),
        check_vma=False,
    )
```

```python
import functools
import math

import jax
import jax.numpy as jnp
from jax import lax
from jax.experimental import pallas as pl
from jax.experimental.pallas import tpu as pltpu
from jax.sharding import PartitionSpec as P

QUERY_HEAD_COUNT = 8
KEY_VALUE_HEADS = 4
HEAD_SIZE = 256


EPS = 1e-06
CAP = 50.0
BASE = 10000.0


def norm_gain(vector, gain):
    return vector * lax.rsqrt(jnp.mean(vector * vector, axis=-1, keepdims=True) + EPS) * gain


def geglu(gate_in, up_in):
    return jax.nn.gelu(gate_in, approximate=True) * up_in


def rounded(value):
    return lax.optimization_barrier(value.astype(jnp.bfloat16)).astype(jnp.float32)


def angle_tables(block_pos):
    half = HEAD_SIZE // 2
    freq = BASE ** (-jnp.arange(half, dtype=jnp.float32) * 2.0 / HEAD_SIZE)
    angle = block_pos.astype(jnp.float32)[..., None] * freq
    return (jnp.cos(angle)[:, :, None, :], jnp.sin(angle)[:, :, None, :])


def turn(vector, cosine, sine):
    half = HEAD_SIZE // 2
    lower = vector[..., :half]
    upper = vector[..., half:]
    return jnp.concatenate([lower * cosine - upper * sine, upper * cosine + lower * sine], axis=-1)


def turn_back(grad, cosine, sine):
    half = HEAD_SIZE // 2
    lower = grad[..., :half]
    upper = grad[..., half:]
    return jnp.concatenate([lower * cosine + upper * sine, upper * cosine - lower * sine], axis=-1)


def load_attention(
    query_weight, key_weight, value_weight, output_weight, gain_table, key_value_begin, kv_cols
):
    key_full, value_full = (
        lax.all_gather(key_weight, ("dp", "ctx", "seq"), axis=0, tiled=True),
        lax.all_gather(value_weight, ("dp", "ctx", "seq"), axis=0, tiled=True),
    )
    key_part = lax.dynamic_slice_in_dim(key_full, key_value_begin, kv_cols, 1)
    value_part = lax.dynamic_slice_in_dim(value_full, key_value_begin, kv_cols, 1)
    w_query, w_output, gain_full = (
        lax.all_gather(query_weight, ("dp", "ctx"), axis=0, tiled=True),
        lax.all_gather(output_weight, ("dp", "ctx"), axis=1, tiled=True),
        lax.all_gather(gain_table, ("dp", "ctx"), axis=0, tiled=True),
    )
    return (w_query, key_part, value_part, w_output, gain_full)


def load_ffn(w_gate, w_up, w_down):
    return (
        lax.all_gather(w_gate, ("dp", "ctx"), axis=0, tiled=True),
        lax.all_gather(w_up, ("dp", "ctx"), axis=0, tiled=True),
        lax.all_gather(w_down, ("dp", "ctx"), axis=1, tiled=True),
    )


def full_output(output_part):
    return lax.all_gather(output_part, "seq", axis=0, tiled=True)


def block_rows(local_rows):
    return lax.all_gather(local_rows, "seq", axis=1, tiled=True)


def row_total(partial_rows):
    return lax.psum_scatter(
        partial_rows.astype(jnp.bfloat16), "seq", scatter_dimension=1, tiled=True
    ).astype(jnp.float32)


def visible_mask(first_row, row_count, key_count, query_pos):
    query_idx = first_row + jnp.arange(row_count, dtype=jnp.int32)
    key_idx = jnp.arange(key_count, dtype=jnp.int32)
    return (key_idx[None, :] <= query_idx[:, None]) & (
        key_idx[None, :] >= (query_idx - query_pos)[:, None]
    )


def scores_of(queries, key_rows, first_row, query_pos):
    row_count = queries.shape[0]
    head_count = queries.shape[1] // HEAD_SIZE
    query_heads = queries.reshape(row_count, head_count, HEAD_SIZE)
    key_heads = key_rows.reshape(key_rows.shape[0], head_count, HEAD_SIZE)
    scores = jnp.einsum(
        "qhd,khd->hqk", query_heads, key_heads, preferred_element_type=jnp.float32
    ) * HEAD_SIZE ** (-0.5)
    bent = jnp.tanh(scores / CAP)
    visible = visible_mask(first_row, row_count, key_rows.shape[0], query_pos)
    masked = jnp.where(visible[None], CAP * bent, -1e30)
    return (query_heads, key_heads, bent, masked)


def attend_forward(queries, key_rows, value_rows, query_pos, first_row):
    query_heads, key_heads, bent, masked = scores_of(queries, key_rows, first_row, query_pos)
    head_count = query_heads.shape[1]
    value_heads = value_rows.reshape(value_rows.shape[0], head_count, HEAD_SIZE)
    row_max = jnp.max(masked, axis=-1, keepdims=True)
    exponent = jnp.exp(masked - row_max)
    row_sum = jnp.sum(exponent, axis=-1, keepdims=True)
    probability = (exponent / row_sum).astype(jnp.bfloat16)
    log_total = (row_max + jnp.log(row_sum))[..., 0]
    result = jnp.einsum(
        "hqk,khd->qhd", probability, value_heads, preferred_element_type=jnp.float32
    )
    return (
        result.astype(jnp.bfloat16).reshape(queries.shape[0], head_count * HEAD_SIZE),
        log_total,
    )


def attend_backward(queries, key_rows, value_rows, query_pos, first_row, log_total, grad_rows):
    query_heads, key_heads, bent, masked = scores_of(queries, key_rows, first_row, query_pos)
    head_count = query_heads.shape[1]
    value_heads = value_rows.reshape(value_rows.shape[0], head_count, HEAD_SIZE)
    grad_heads = grad_rows.reshape(queries.shape[0], head_count, HEAD_SIZE)
    probability = jnp.exp(masked - log_total[..., None])
    prob_low = probability.astype(jnp.bfloat16)
    grad_value = jnp.einsum(
        "hqk,qhd->khd", prob_low, grad_heads, preferred_element_type=jnp.float32
    )
    grad_prob = jnp.einsum(
        "qhd,khd->hqk", grad_heads, value_heads, preferred_element_type=jnp.float32
    )
    delta = jnp.sum(probability * grad_prob, axis=-1, keepdims=True)
    grad_scores = (probability * (grad_prob - delta) * (1.0 - bent * bent)).astype(jnp.bfloat16)
    grad_query = jnp.einsum(
        "hqk,khd->qhd", grad_scores, key_heads, preferred_element_type=jnp.float32
    ) * HEAD_SIZE ** (-0.5)
    grad_key = jnp.einsum(
        "hqk,qhd->khd", grad_scores, query_heads, preferred_element_type=jnp.float32
    ) * HEAD_SIZE ** (-0.5)
    key_count = key_rows.shape[0]
    return (
        grad_query.reshape(queries.shape[0], head_count * HEAD_SIZE),
        grad_key.reshape(key_count, head_count * HEAD_SIZE),
        grad_value.reshape(key_count, head_count * HEAD_SIZE),
    )


def general_local(
    inputs,
    positions,
    query_weight,
    key_weight,
    value_weight,
    output_weight,
    gate_weight,
    up_weight,
    down_weight,
    pre_attn_gain,
    post_attn_gain,
    pre_ffn_gain,
    post_ffn_gain,
    cotangent,
):
    seqs, tokens, width = inputs.shape
    block_len = positions.shape[1]
    full_len = block_len * lax.axis_size("ctx")
    offset = lax.axis_index("ctx") * block_len
    head_count = QUERY_HEAD_COUNT // lax.axis_size("seq")
    key_value_group = QUERY_HEAD_COUNT // KEY_VALUE_HEADS
    kv_heads = max(head_count // key_value_group, 1)
    kv_cols = kv_heads * HEAD_SIZE
    repeat_by = head_count // kv_heads
    head_cols = head_count * HEAD_SIZE
    key_value_begin = lax.axis_index("seq") * head_count // key_value_group * HEAD_SIZE
    cosine, sine = angle_tables(positions)
    gain_table = jnp.stack([pre_attn_gain, post_attn_gain, pre_ffn_gain, post_ffn_gain], axis=1)
    fwd_attn = load_attention(
        query_weight, key_weight, value_weight, output_weight, gain_table, key_value_begin, kv_cols
    )
    fwd_ffn = load_ffn(gate_weight, up_weight, down_weight)
    w_query, key_matrix, value_matrix, w_output, gain_full = fwd_attn
    w_gate, w_up, w_down = fwd_ffn
    gain_float = gain_full.astype(jnp.float32)
    gain_one = gain_float[:, 0]
    gain_two = gain_float[:, 1]
    gain_three = gain_float[:, 2]
    gain_four = gain_float[:, 3]
    x_float = inputs.astype(jnp.float32)
    normed_one = norm_gain(x_float, gain_one).astype(jnp.bfloat16)
    block_one = block_rows(normed_one)
    query_raw = jnp.einsum("srd,de->sre", block_one, w_query, preferred_element_type=jnp.float32)
    key_raw = jnp.einsum("srd,de->sre", block_one, key_matrix, preferred_element_type=jnp.float32)
    value_raw = jnp.einsum(
        "srd,de->sre", block_one, value_matrix, preferred_element_type=jnp.float32
    )
    query_rot = (
        turn(query_raw.reshape(seqs, block_len, head_count, HEAD_SIZE), cosine, sine)
        .astype(jnp.bfloat16)
        .reshape(seqs, block_len, head_cols)
    )
    key_rot = (
        turn(key_raw.reshape(seqs, block_len, kv_heads, HEAD_SIZE), cosine, sine)
        .astype(jnp.bfloat16)
        .reshape(seqs, block_len, kv_cols)
    )
    key_all, value_all = (
        lax.all_gather(key_rot, "ctx", axis=1, tiled=True),
        lax.all_gather(value_raw.astype(jnp.bfloat16), "ctx", axis=1, tiled=True),
    )
    key_broadcast = jnp.repeat(
        key_all.reshape(seqs, full_len, kv_heads, HEAD_SIZE), repeat_by, axis=2
    ).reshape(seqs, full_len, head_cols)
    value_broadcast = jnp.repeat(
        value_all.reshape(seqs, full_len, kv_heads, HEAD_SIZE), repeat_by, axis=2
    ).reshape(seqs, full_len, head_cols)
    query_block = math.gcd(block_len, 512)
    block_count = block_len // query_block
    item_count = seqs * block_count
    item_index = jnp.arange(item_count, dtype=jnp.int32)
    block_starts = offset + item_index % block_count * query_block
    seq_owner = item_index // block_count

    def forward_item(pieces):
        queries, query_pos, first_row, seq_id = pieces
        key_rows = lax.dynamic_index_in_dim(key_broadcast, seq_id, 0, keepdims=False)
        value_rows = lax.dynamic_index_in_dim(value_broadcast, seq_id, 0, keepdims=False)
        return attend_forward(queries, key_rows, value_rows, query_pos, first_row)

    head_items, log_total = lax.map(forward_item, (query_rot, positions, block_starts, seq_owner))
    out_full = full_output(w_output)
    heads_tok = lax.all_to_all(head_items, "seq", split_axis=1, concat_axis=2, tiled=True)
    project = jnp.einsum("ste,ed->std", heads_tok, out_full, preferred_element_type=jnp.float32)
    middle = x_float + norm_gain(project, gain_two)
    normed_two = norm_gain(middle, gain_three).astype(jnp.bfloat16)
    ffn_input = block_rows(normed_two)
    gate = jnp.einsum("srd,df->srf", ffn_input, w_gate, preferred_element_type=jnp.float32)
    upper = jnp.einsum("srd,df->srf", ffn_input, w_up, preferred_element_type=jnp.float32)
    hidden = geglu(gate, upper).astype(jnp.bfloat16)
    feed = row_total(jnp.einsum("srf,fd->srd", hidden, w_down, preferred_element_type=jnp.float32))
    layer_output = (middle + norm_gain(feed, gain_four)).astype(jnp.bfloat16)
    back_attn = load_attention(
        query_weight, key_weight, value_weight, output_weight, gain_table, key_value_begin, kv_cols
    )
    back_ffn = load_ffn(gate_weight, up_weight, down_weight)
    bq_weight, bk_weight, bv_weight, bo_weight = (
        back_attn[0],
        back_attn[1],
        back_attn[2],
        back_attn[3],
    )
    bgate_weight, bup_weight, bdown_weight = back_ffn
    grad_top = cotangent.astype(jnp.float32)
    unused, pull_four = jax.vjp(norm_gain, feed, gain_four)
    grad_feed, grad_g_four = pull_four(grad_top)
    grad_feed_rows = block_rows(grad_feed.astype(jnp.bfloat16))
    grad_hidden = jnp.einsum(
        "srd,fd->srf", grad_feed_rows, bdown_weight, preferred_element_type=jnp.float32
    )
    grad_down_part = jnp.einsum(
        "srf,srd->fd", hidden, grad_feed_rows, preferred_element_type=jnp.float32
    )
    unused, pull_act = jax.vjp(geglu, gate, upper)
    grad_gate_act, grad_up_act = pull_act(grad_hidden)
    grad_gate_act = grad_gate_act.astype(jnp.bfloat16)
    grad_up_act = grad_up_act.astype(jnp.bfloat16)
    grad_rows_part = jnp.einsum(
        "srf,df->srd", grad_gate_act, bgate_weight, preferred_element_type=jnp.float32
    ) + jnp.einsum("srf,df->srd", grad_up_act, bup_weight, preferred_element_type=jnp.float32)
    grad_gate_part = jnp.einsum(
        "srd,srf->df", ffn_input, grad_gate_act, preferred_element_type=jnp.float32
    )
    grad_up_part = jnp.einsum(
        "srd,srf->df", ffn_input, grad_up_act, preferred_element_type=jnp.float32
    )
    ffn_grads = (
        lax.psum_scatter(
            grad_gate_part.astype(jnp.bfloat16), ("dp", "ctx"), scatter_dimension=0, tiled=True
        ).astype(jnp.float32),
        lax.psum_scatter(
            grad_up_part.astype(jnp.bfloat16), ("dp", "ctx"), scatter_dimension=0, tiled=True
        ).astype(jnp.float32),
        lax.psum_scatter(
            grad_down_part.astype(jnp.bfloat16), ("dp", "ctx"), scatter_dimension=1, tiled=True
        ).astype(jnp.float32),
    )
    grad_normed_two = row_total(grad_rows_part)
    unused, pull_three = jax.vjp(norm_gain, middle, gain_three)
    grad_mid_norm, grad_g_three = pull_three(grad_normed_two)
    grad_middle = grad_top + grad_mid_norm
    unused, pull_two = jax.vjp(norm_gain, project, gain_two)
    grad_project, grad_g_two = pull_two(grad_middle)
    grad_project = grad_project.astype(jnp.bfloat16)
    out_back = full_output(bo_weight)
    grad_heads_tok = jnp.einsum(
        "std,ed->ste", grad_project, out_back, preferred_element_type=jnp.float32
    ).astype(jnp.bfloat16)
    grad_output_part = lax.psum_scatter(
        jnp.einsum(
            "ste,std->ed", heads_tok, grad_project, preferred_element_type=jnp.float32
        ).astype(jnp.bfloat16),
        "seq",
        scatter_dimension=0,
        tiled=True,
    )
    grad_heads = lax.all_to_all(grad_heads_tok, "seq", split_axis=2, concat_axis=1, tiled=True)

    def backward_item(carry, pieces):
        key_acc, value_acc = carry
        queries, query_pos, first_row, seq_id, log_part, grad_part = pieces
        key_rows = lax.dynamic_index_in_dim(key_broadcast, seq_id, 0, keepdims=False)
        value_rows = lax.dynamic_index_in_dim(value_broadcast, seq_id, 0, keepdims=False)
        grad_query, grad_key, grad_value = attend_backward(
            queries, key_rows, value_rows, query_pos, first_row, log_part, grad_part
        )
        key_acc = lax.dynamic_update_index_in_dim(
            key_acc,
            lax.dynamic_index_in_dim(key_acc, seq_id, 0, keepdims=False) + grad_key,
            seq_id,
            0,
        )
        value_acc = lax.dynamic_update_index_in_dim(
            value_acc,
            lax.dynamic_index_in_dim(value_acc, seq_id, 0, keepdims=False) + grad_value,
            seq_id,
            0,
        )
        return ((key_acc, value_acc), grad_query)

    empty = jnp.zeros((seqs, full_len, head_cols), jnp.float32)
    (key_terms, value_terms), grad_query_items = lax.scan(
        backward_item,
        (empty, empty),
        (query_rot, positions, block_starts, seq_owner, log_total, grad_heads),
    )
    key_sums, value_sums = (
        lax.psum_scatter(
            key_terms.astype(jnp.bfloat16), "ctx", scatter_dimension=1, tiled=True
        ).astype(jnp.float32),
        lax.psum_scatter(
            value_terms.astype(jnp.bfloat16), "ctx", scatter_dimension=1, tiled=True
        ).astype(jnp.float32),
    )
    grad_query_rot = rounded(grad_query_items.reshape(seqs, block_len, head_count, HEAD_SIZE))
    grad_query_raw = (
        turn_back(grad_query_rot, cosine, sine)
        .astype(jnp.bfloat16)
        .reshape(seqs, block_len, head_cols)
    )
    grad_key_rot = rounded(key_sums.reshape(seqs, block_len, head_count, HEAD_SIZE))
    grad_key_raw = (
        turn_back(grad_key_rot, cosine, sine)
        .astype(jnp.bfloat16)
        .reshape(seqs, block_len, head_cols)
    )
    grad_value_raw = value_sums.astype(jnp.bfloat16)
    key_expand = jnp.repeat(
        bk_weight.reshape(width, kv_heads, HEAD_SIZE), repeat_by, axis=1
    ).reshape(width, head_cols)
    value_expand = jnp.repeat(
        bv_weight.reshape(width, kv_heads, HEAD_SIZE), repeat_by, axis=1
    ).reshape(width, head_cols)
    grad_block_one = jnp.einsum(
        "sre,de->srd", grad_query_raw, bq_weight, preferred_element_type=jnp.float32
    )
    grad_block_one = grad_block_one + jnp.einsum(
        "sre,de->srd", grad_key_raw, key_expand, preferred_element_type=jnp.float32
    )
    grad_block_one = grad_block_one + jnp.einsum(
        "sre,de->srd", grad_value_raw, value_expand, preferred_element_type=jnp.float32
    )
    grad_normed_one = row_total(grad_block_one)
    grad_query_part = jnp.einsum(
        "srd,sre->de", block_one, grad_query_raw, preferred_element_type=jnp.float32
    )
    grad_key_wide = jnp.einsum(
        "srd,sre->de", block_one, grad_key_raw, preferred_element_type=jnp.float32
    )
    grad_value_wide = jnp.einsum(
        "srd,sre->de", block_one, grad_value_raw, preferred_element_type=jnp.float32
    )
    grad_key_part = jnp.sum(
        grad_key_wide.reshape(width, kv_heads, repeat_by, HEAD_SIZE), axis=2
    ).reshape(width, kv_cols)
    grad_value_part = jnp.sum(
        grad_value_wide.reshape(width, kv_heads, repeat_by, HEAD_SIZE), axis=2
    ).reshape(width, kv_cols)
    unused, pull_one = jax.vjp(norm_gain, x_float, gain_one)
    grad_input_norm, grad_g_one = pull_one(grad_normed_one)
    input_grad = (grad_middle + grad_input_norm).astype(jnp.bfloat16)
    gain_grads = jnp.stack([grad_g_one, grad_g_two, grad_g_three, grad_g_four], axis=1)
    attention_gradients = (
        lax.psum_scatter(
            grad_query_part.astype(jnp.bfloat16), ("dp", "ctx"), scatter_dimension=0, tiled=True
        ).astype(jnp.float32),
        lax.psum_scatter(grad_output_part, ("dp", "ctx"), scatter_dimension=1, tiled=True).astype(
            jnp.float32
        ),
    )
    key_spread = lax.dynamic_update_slice_in_dim(
        jnp.zeros((width, KEY_VALUE_HEADS * HEAD_SIZE), jnp.float32),
        grad_key_part,
        key_value_begin,
        1,
    )
    value_spread = lax.dynamic_update_slice_in_dim(
        jnp.zeros((width, KEY_VALUE_HEADS * HEAD_SIZE), jnp.float32),
        grad_value_part,
        key_value_begin,
        1,
    )
    kv_sums = (
        lax.psum_scatter(key_spread, ("dp", "ctx", "seq"), scatter_dimension=0, tiled=True),
        lax.psum_scatter(value_spread, ("dp", "ctx", "seq"), scatter_dimension=0, tiled=True),
        lax.psum_scatter(gain_grads, ("dp", "ctx", "seq"), scatter_dimension=0, tiled=True),
    )
    gain_out = kv_sums[2]
    return (
        layer_output,
        input_grad,
        attention_gradients[0],
        kv_sums[0],
        kv_sums[1],
        attention_gradients[1],
        ffn_grads[0],
        ffn_grads[1],
        ffn_grads[2],
        gain_out[:, 0],
        gain_out[:, 1],
        gain_out[:, 2],
        gain_out[:, 3],
    )


def flip(value, axis):
    return lax.ppermute(value, axis, [(0, 1), (1, 0)])


def ordered(index, own, other, axis=0):
    return jnp.where(
        index == 0, jnp.stack([own, other], axis=axis), jnp.stack([other, own], axis=axis)
    )


def pick(value, index, axis=0):
    return lax.dynamic_index_in_dim(value, index, axis, keepdims=False)


def after(value, *earlier):
    return lax.optimization_barrier((value, *earlier))[0]


def total(kept, *got):
    value = kept.astype(jnp.float32)
    for more in got:
        value = value + more.astype(jnp.float32)
    return value


def trade_sequences(value):
    cy = lax.axis_index("cy")
    return ordered(cy, pick(value, cy), flip(pick(value, 1 - cy), "cy"))


def core_columns(matrices, core):
    parts = []
    for matrix, begin, width in matrices:
        at = core * (matrix.shape[1] // 2) + begin
        parts.append(lax.dynamic_slice_in_dim(matrix, at, width, 1))
    return jnp.concatenate(parts, axis=1) if len(parts) > 1 else parts[0]


def start_gather(*matrices):
    c = lax.axis_index("core")
    got = flip(core_columns(matrices, 1 - c), "core")
    rows = ordered(c, core_columns(matrices, c), got)
    return rows, flip(rows, "cy"), flip(rows, "dp")


def next_gather(rows, rows_y, rows_x):
    return rows, rows_y, rows_x, flip(rows_y[0], "dp"), flip(rows_x[1], "cy")


def place_kernel(moves, count, *refs):
    sources, outs = refs[:count], refs[count : len(refs) - count - 2]
    held, sem_in, sem_out = refs[-count - 2 : -2], refs[-2], refs[-1]
    x, y = lax.axis_index("dp"), lax.axis_index("cy")
    loads = [
        pltpu.make_async_copy(source, buffer, sem_in.at[i])
        for i, (source, buffer) in enumerate(zip(sources, held))
    ]
    for load in loads:
        load.start()
    stores = []
    for i, (load, buffer) in enumerate(zip(loads, held)):
        load.wait()
        for out, begin, to, cols in moves[i // 5]:
            out, to = outs[out], pl.ds(to, cols)
            target = (
                out.at[x, y, :, :, to],
                out.at[x, 1 - y, :, :, to],
                out.at[1 - x, y, :, :, to],
                out.at[1 - x, 1 - y, 0, :, to],
                out.at[1 - x, 1 - y, 1, :, to],
            )[i % 5]
            at = pl.ds(begin, cols)
            piece = buffer.at[:, :, at] if i % 5 < 3 else buffer.at[:, at]
            stores.append(pltpu.make_async_copy(piece, target, sem_out.at[len(stores)]))
            stores[-1].start()
    for store in stores:
        store.wait()


def end_gather(gathers, moves, widths):
    pieces = [piece for begun in gathers for piece in begun]
    rows, low = pieces[0].shape[1], pieces[0].dtype
    size = 8 * rows * sum(widths) * low.itemsize
    anywhere = pl.BlockSpec(memory_space=pl.ANY)
    stores = 5 * sum(len(some) for some in moves)
    outs = pl.pallas_call(
        functools.partial(place_kernel, moves, len(pieces)),
        out_shape=[jax.ShapeDtypeStruct((2, 2, 2, rows, width), low) for width in widths],
        in_specs=[anywhere] * len(pieces),
        out_specs=[anywhere] * len(widths),
        scratch_shapes=[pltpu.VMEM(piece.shape, low) for piece in pieces]
        + [pltpu.SemaphoreType.DMA((len(pieces),)), pltpu.SemaphoreType.DMA((stores,))],
        compiler_params=pltpu.CompilerParams(vmem_limit_bytes=size + (2 << 20)),
        cost_estimate=pl.CostEstimate(flops=0, bytes_accessed=2 * size, transcendentals=0),
        name="place_rows",
    )(*pieces)
    return [out.reshape(-1, out.shape[-1]) for out in outs]


def start_scatter(grad):
    x, y = lax.axis_index("dp"), lax.axis_index("cy")
    parts = grad.reshape(2, 2, 2, -1, grad.shape[-1])
    return parts, pick(parts, 1 - x)[:, 0], pick(parts, 1 - y, 1)[:, 1]


def send_scatter(parts, by_x, by_y):
    return parts, flip(by_x, "dp"), flip(by_y, "cy")


def next_scatter(parts, from_x, from_y):
    x, y = lax.axis_index("dp"), lax.axis_index("cy")
    by_y = total(pick(pick(parts, x), 1 - y)[0], pick(from_x, 1 - y)).astype(parts.dtype)
    by_x = total(pick(pick(parts, 1 - x), y)[1], pick(from_y, 1 - x)).astype(parts.dtype)
    return parts, from_x, from_y, flip(by_y, "cy"), flip(by_x, "dp")


def end_scatter(parts, from_x, from_y, last_y, last_x):
    x, y, c = lax.axis_index("dp"), lax.axis_index("cy"), lax.axis_index("core")
    own = pick(pick(parts, x), y)
    first = total(own[0], pick(from_x, y), last_y)
    second = total(own[1], pick(from_y, x), last_x)
    keep = jnp.where(c == 0, first, second)
    away = jnp.where(c == 0, second, first).astype(jnp.bfloat16)
    got = flip(away, "core").astype(jnp.float32)
    return jnp.where(c == 0, keep, got), jnp.where(c == 0, got, keep)


def gather_gains(table):
    table = ordered(lax.axis_index("core"), table, flip(table, "core"), axis=1)
    table = ordered(lax.axis_index("cy"), table, flip(table, "cy"), axis=1)
    table = ordered(lax.axis_index("dp"), table, flip(table, "dp"), axis=1)
    return table.reshape(table.shape[0], -1)


def exchange_seq(parts):
    z, size = lax.axis_index("seq"), lax.axis_size("seq")
    got = [pick(parts, z)]
    for step in range(1, size):
        ring = [(i, (i + step) % size) for i in range(size)]
        got.insert(0, lax.ppermute(pick(parts, lax.rem(z + step, size)), "seq", ring))
    got = jnp.stack(got + got[:-1])
    return lax.dynamic_slice_in_dim(got, size - 1 - z, size, 0)


def shift(value, step):
    size = lax.axis_size("seq")
    return lax.ppermute(value, "seq", [(i, (i + step) % size) for i in range(size)])


def gather_rows(local_rows):
    size = lax.axis_size("seq")
    got = {step: shift(local_rows, step) for step in (3, 1, 2)}
    pieces = [local_rows] + [got[size - ahead] for ahead in range(1, size)]
    return jnp.concatenate(pieces + [flip(piece, "core") for piece in pieces])


def join_kernel(whole, out, held, sem):
    c, z = lax.axis_index("core"), lax.axis_index("seq")
    size, rows = whole.shape[0] // 2, whole.shape[1]
    loads = []
    for i in range(2 * size):
        owner = (c if i < size else 1 - c) * size + lax.rem(z + i % size, size)
        target = held.at[pl.ds(i * rows, rows)]
        loads.append(pltpu.make_async_copy(whole.at[owner], target, sem.at[i]))
    for load in loads:
        load.start()
    for load in loads:
        load.wait()
    store = pltpu.make_async_copy(held, out, sem.at[2 * size])
    store.start()
    store.wait()


def gather_first(local_rows):
    whole = lax.all_gather(local_rows, ("core", "seq"), axis=0)
    shape, low = (whole.shape[0] * whole.shape[1], whole.shape[2]), whole.dtype
    size = whole.size * low.itemsize
    anywhere = pl.BlockSpec(memory_space=pl.ANY)
    return pl.pallas_call(
        join_kernel,
        out_shape=jax.ShapeDtypeStruct(shape, low),
        in_specs=[anywhere],
        out_specs=anywhere,
        scratch_shapes=[
            pltpu.VMEM(shape, low),
            pltpu.SemaphoreType.DMA((whole.shape[0] + 1,)),
        ],
        compiler_params=pltpu.CompilerParams(vmem_limit_bytes=size + (2 << 20)),
        cost_estimate=pl.CostEstimate(flops=0, bytes_accessed=2 * size, transcendentals=0),
        name="join_rows",
    )(whole)


def row_tokens(rows, length):
    c, z, size = lax.axis_index("core"), lax.axis_index("seq"), lax.axis_size("seq")
    shape = (2, size, 2, rows // 2)
    core = jnp.where(lax.broadcasted_iota(jnp.int32, shape, 0) == 0, c, 1 - c)
    owner = lax.rem(z + lax.broadcasted_iota(jnp.int32, shape, 1), size)
    begin = lax.broadcasted_iota(jnp.int32, shape, 2) * (length // 2)
    row = lax.broadcasted_iota(jnp.int32, shape, 3)
    return (begin + (core * size + owner) * (rows // 2) + row).reshape(-1)


def row_order(values):
    c, z, size = lax.axis_index("core"), lax.axis_index("seq"), lax.axis_size("seq")
    parts = values.reshape(2, 2, size, -1).transpose(1, 2, 0, 3)
    parts = jnp.stack([pick(parts, c), pick(parts, 1 - c)])
    parts = jnp.concatenate([parts, parts], axis=1)
    return lax.dynamic_slice_in_dim(parts, z, size, 1).reshape(-1)


def core_swap(value):
    half = value.shape[0] // 2
    got = flip(value, "core")
    return jnp.concatenate([got[half:], got[:half]])


def core_rows(left, right, dims):
    half = left.shape[0] // 2
    got = flip(dot(left[half:], right, dims).astype(jnp.bfloat16), "core")
    kept = lax.optimization_barrier(dot(left[:half], right, dims).astype(jnp.bfloat16))
    return total(kept, got).astype(jnp.bfloat16)


def core_sums(partial_rows):
    half = partial_rows.shape[0] // 2
    return total(partial_rows[:half], flip(partial_rows[half:], "core")).astype(jnp.bfloat16)


def scatter_rows(sums):
    size = lax.axis_size("seq")
    parts = sums.reshape(size, -1, sums.shape[-1])
    got = [shift(parts[step], step) for step in (3, 1, 2)]
    return total(parts[0], *got)


def chip_rows(*matrices):
    c = lax.axis_index("core")
    got = flip(core_columns(matrices, 1 - c), "core")
    return ordered(c, core_columns(matrices, c), got)


def gather_chips(rows):
    whole = lax.all_gather(rows.reshape(-1, rows.shape[-1]), ("dp", "cy"), axis=0, tiled=True)
    return whole


def scatter_chips(grad):
    sums = lax.psum_scatter(grad, ("dp", "cy"), scatter_dimension=0, tiled=True)
    return sums.reshape(2, -1, sums.shape[-1])


def both_columns(sums):
    c = lax.axis_index("core")
    keep = pick(sums, c).astype(jnp.float32)
    got = flip(pick(sums, 1 - c), "core").astype(jnp.float32)
    return jnp.where(c == 0, keep, got), jnp.where(c == 0, got, keep)


def dot(left, right, dims):
    return lax.dot_general(
        left, right, ((dims[:1], dims[1:]), ((), ())), preferred_element_type=jnp.float32
    )


def head_scores(queries, keys, visible):
    bent = jnp.tanh(dot(queries, keys, (1, 1)) * (HEAD_SIZE ** (-0.5) / CAP))
    return bent, jnp.where(visible, CAP * bent, -1e30)


def head_local(
    inputs,
    positions,
    query_weight,
    key_weight,
    value_weight,
    output_weight,
    gate_weight,
    up_weight,
    down_weight,
    pre_attn_gain,
    post_attn_gain,
    pre_ffn_gain,
    post_ffn_gain,
    cotangent,
):
    c, cy = lax.axis_index("core"), lax.axis_index("cy")
    low = jnp.bfloat16
    rows_own = query_weight.shape[0]
    ffn_cols = gate_weight.shape[1] // 2

    kv_stack = jnp.stack([key_weight, value_weight], axis=1)
    kv_stack = kv_stack.reshape(-1, 2, KEY_VALUE_HEADS, HEAD_SIZE).transpose(2, 0, 1, 3)
    kv_rows = exchange_seq(kv_stack).reshape(rows_own, 2 * HEAD_SIZE)
    x_local = after(trade_sequences(inputs), kv_rows)
    own_shape = x_local.shape
    x_local = x_local.reshape(-1, x_local.shape[-1])
    block_x = gather_first(x_local)
    x_float = x_local.astype(jnp.float32)
    gain_table = jnp.stack([pre_attn_gain, post_attn_gain, pre_ffn_gain, post_ffn_gain], axis=0)
    gain_one, gain_two, gain_three, gain_four = gather_gains(gain_table).astype(jnp.float32)

    pos_own = trade_sequences(positions)
    seq_pos = ordered(c, pos_own, flip(pos_own, "core"), axis=1).reshape(-1)
    half = HEAD_SIZE // 2
    freq = BASE ** (-jnp.arange(half, dtype=jnp.float32) * 2.0 / HEAD_SIZE)
    token = row_tokens(x_local.shape[0], seq_pos.shape[0])
    seq_pos = row_order(seq_pos)
    angle = seq_pos.astype(jnp.float32)[:, None] * freq
    cosine, sine = jnp.cos(angle), jnp.sin(angle)
    kv_cosine = jnp.where(c == 0, cosine, 1.0)
    kv_sine = jnp.where(c == 0, sine, 0.0)

    attn_begun = next_gather(
        *start_gather(
            (query_weight, 0, HEAD_SIZE), (kv_rows, 0, HEAD_SIZE), (output_weight.T, 0, HEAD_SIZE)
        )
    )
    split = 2 * HEAD_SIZE
    in_weight, out_weight = end_gather(
        [attn_begun], [((0, 0, 0, split), (1, split, 0, HEAD_SIZE))], (split, HEAD_SIZE)
    )
    gate_up_rows = chip_rows((gate_weight, 0, ffn_cols), (up_weight, 0, ffn_cols))
    gate_up_weight = gather_chips(gate_up_rows)
    down_back = gather_chips(chip_rows((down_weight.T, 0, ffn_cols)))
    grad_top = trade_sequences(after(cotangent, attn_begun))

    block_one = norm_gain(block_x.astype(jnp.float32), gain_one).astype(low)
    raw = dot(block_one, in_weight, (1, 0))
    queries = turn(raw[:, :HEAD_SIZE], cosine, sine).astype(low)
    kv_own = turn(raw[:, HEAD_SIZE:], kv_cosine, kv_sine).astype(low)
    kv_other = core_swap(kv_own)
    keys = jnp.where(c == 0, kv_own, kv_other)
    values = jnp.where(c == 0, kv_other, kv_own)
    visible = (token[None, :] <= token[:, None]) & (token[None, :] >= (token - seq_pos)[:, None])
    bent, masked = head_scores(queries, keys, visible)
    row_max = jnp.max(masked, axis=-1, keepdims=True)
    exponent = jnp.exp(masked - row_max)
    row_sum = jnp.sum(exponent, axis=-1, keepdims=True)
    heads = dot((exponent / row_sum).astype(low), values, (1, 0)).astype(low)
    log_total = row_max + jnp.log(row_sum)
    heads = after(heads, grad_top)
    grad_top = grad_top.reshape(x_local.shape).astype(jnp.float32)

    project_core = core_rows(heads, out_weight, (1, 1))
    project = scatter_rows(project_core)
    middle = x_float + norm_gain(project, gain_two)
    normed_two = norm_gain(middle, gain_three).astype(low)
    block_two = gather_rows(normed_two)
    gate_up = dot(block_two, gate_up_weight, (1, 0))
    gate, upper = gate_up[:, :ffn_cols], gate_up[:, ffn_cols:]
    hidden = geglu(gate, upper).astype(low)
    feed = scatter_rows(core_rows(hidden, down_back, (1, 1)))
    unused, pull_four = jax.vjp(norm_gain, feed, gain_four)
    grad_feed, grad_g_four = pull_four(grad_top)
    grad_feed = grad_feed.astype(low)
    layer_output = after((middle + norm_gain(feed, gain_four)).astype(low), grad_feed)
    layer_output = trade_sequences(layer_output.reshape(own_shape))

    grad_feed_rows = after(gather_rows(grad_feed), layer_output)
    grad_hidden = dot(grad_feed_rows, down_back, (1, 0))
    unused, pull_act = jax.vjp(geglu, gate, upper)
    grad_gate_act, grad_up_act = pull_act(grad_hidden)
    grad_gate_up = jnp.concatenate([grad_gate_act.astype(low), grad_up_act.astype(low)], axis=1)
    normed_two_core = core_sums(dot(grad_gate_up, gate_up_weight, (1, 1)).astype(low))
    grad_normed_two = scatter_rows(normed_two_core)
    late = after((hidden, block_two), normed_two_core)
    grad_down = dot(grad_feed_rows, late[0], (0, 0)).astype(low)
    grad_gu = dot(late[1], grad_gate_up, (0, 0)).astype(low)
    grad_normed_two = after(grad_normed_two, grad_down, grad_gu)
    grad_down, grad_gu = scatter_chips(grad_down), scatter_chips(grad_gu)

    unused, pull_three = jax.vjp(norm_gain, middle, gain_three)
    grad_mid_norm, grad_g_three = pull_three(grad_normed_two)
    grad_middle = grad_top + grad_mid_norm
    unused, pull_two = jax.vjp(norm_gain, project, gain_two)
    grad_project, grad_g_two = pull_two(grad_middle)
    grad_project = grad_project.astype(low)
    grad_project_rows = gather_rows(grad_project)
    grad_heads = dot(grad_project_rows, out_weight, (1, 0)).astype(low)

    bent, masked = head_scores(queries, keys, visible)
    probability = jnp.exp(masked - log_total)
    grad_value = dot(probability.astype(low), grad_heads, (0, 0)).astype(low)
    grad_prob = dot(grad_heads, values, (1, 1))
    delta = jnp.sum(probability * grad_prob, axis=-1, keepdims=True)
    grad_scores = (probability * (grad_prob - delta) * (1.0 - bent * bent)).astype(low)
    scale = HEAD_SIZE ** (-0.5)
    grad_query_rot = rounded(dot(grad_scores, keys, (1, 0)) * scale)
    grad_key_rot = rounded(dot(grad_scores, queries, (0, 0)) * scale)
    grad_query_raw = turn_back(grad_query_rot, cosine, sine).astype(low)
    grad_key_raw = turn_back(grad_key_rot, cosine, sine).astype(low)
    kv_grad_own = jnp.where(c == 0, grad_key_raw, grad_value)
    kv_grad_got = core_swap(jnp.where(c == 0, grad_value, grad_key_raw))
    grad_in = jnp.concatenate([grad_query_raw, total(kv_grad_own, kv_grad_got).astype(low)], axis=1)
    normed_one_part = dot(grad_in, in_weight, (1, 1)).astype(low)
    normed_one_core = core_sums(normed_one_part)
    grad_normed_one = scatter_rows(normed_one_core)
    block_one, heads = after((block_one, heads), normed_one_core)
    grad_in_part = dot(block_one, grad_in, (0, 0)).astype(low)
    grad_output_part = dot(grad_project_rows, heads, (0, 0)).astype(low)
    attn_grad_begun = start_scatter(jnp.concatenate([grad_in_part, grad_output_part], axis=1))
    attn_grad_begun = send_scatter(*attn_grad_begun)
    grad_normed_one = after(grad_normed_one, attn_grad_begun)
    attn_grad_begun = next_scatter(*attn_grad_begun)
    attn_grads = end_scatter(*attn_grad_begun)
    grad_down, grad_gu = after((grad_down, grad_gu), attn_grad_begun)
    grad_down, grad_gu = both_columns(grad_down), both_columns(grad_gu)

    block_x = after(block_x, attn_grad_begun[0]).astype(jnp.float32)
    unused, pull_gain = jax.vjp(lambda gain: norm_gain(block_x, gain), gain_one)
    (grad_g_one,) = pull_gain(normed_one_part.astype(jnp.float32))
    everyone = ("dp", "cy", "core", "seq")
    gain_grads = jnp.stack([grad_g_one, grad_g_two, grad_g_three, grad_g_four], axis=0)
    gain_grads = after(gain_grads, grad_normed_one, attn_grad_begun)
    gain_parts = gain_grads.reshape(4, lax.axis_size(everyone), -1).transpose(1, 0, 2)
    gain_out = jnp.sum(
        lax.all_to_all(gain_parts, everyone, split_axis=0, concat_axis=0, tiled=True), axis=0
    )

    unused, pull_one = jax.vjp(lambda rows: norm_gain(rows, gain_one), x_float)
    (grad_input_norm,) = pull_one(grad_normed_one)
    input_grad = trade_sequences((grad_middle + grad_input_norm).astype(low).reshape(own_shape))

    def whole(pair, begin, cols):
        return jnp.concatenate([part[:, begin : begin + cols] for part in pair], axis=1)

    kv_back = whole(attn_grads, HEAD_SIZE, HEAD_SIZE).astype(low)
    kv_back = exchange_seq(kv_back.reshape(KEY_VALUE_HEADS, -1, 2 * HEAD_SIZE))
    kv_back = kv_back.reshape(KEY_VALUE_HEADS, -1, 2, HEAD_SIZE).transpose(2, 1, 0, 3)
    kv_back = kv_back.reshape(2, -1, KEY_VALUE_HEADS * HEAD_SIZE).astype(jnp.float32)
    return (
        layer_output,
        input_grad,
        whole(attn_grads, 0, HEAD_SIZE),
        kv_back[0],
        kv_back[1],
        whole(attn_grads, 2 * HEAD_SIZE, HEAD_SIZE).T,
        whole(grad_gu, 0, ffn_cols),
        whole(grad_gu, ffn_cols, ffn_cols),
        whole(grad_down, 0, ffn_cols).T,
        gain_out[0],
        gain_out[1],
        gain_out[2],
        gain_out[3],
    )


def one_head_each(mesh):
    sizes = mesh.shape
    return (
        sizes["dp"] == 2
        and sizes["ctx"] == 4
        and sizes["seq"] == KEY_VALUE_HEADS
        and QUERY_HEAD_COUNT == 2 * KEY_VALUE_HEADS
    )


def solution(mesh):
    if one_head_each(mesh):
        body, ctx = head_local, ("cy", "core")
        grid = jax.sharding.Mesh(
            mesh.devices.reshape(mesh.shape["dp"], -1, 2, mesh.shape["seq"]),
            ("dp", "cy", "core", "seq"),
        )
    else:
        body, ctx, grid = general_local, ("ctx",), mesh
    owners, everyone = ("dp", *ctx), ("dp", *ctx, "seq")
    rows = P("dp", (*ctx, "seq"), None)
    tall, flat, wide = P(owners, "seq"), P(everyone, None), P("seq", owners)
    gains = (P(owners),) * 4
    return jax.shard_map(
        body,
        mesh=grid,
        in_specs=(rows, P("dp", ctx), tall, flat, flat, wide, tall, tall, wide, *gains, rows),
        out_specs=(rows, rows, tall, flat, flat, wide, tall, tall, wide, *((P(everyone),) * 4)),
        check_vma=False,
    )
```

```python
import functools
import math

import jax
import jax.numpy as jnp
from jax import lax
from jax.experimental import pallas as pl
from jax.experimental.pallas import tpu as pltpu
from jax.sharding import PartitionSpec as P

QUERY_HEAD_COUNT = 8
KEY_VALUE_HEADS = 4
HEAD_SIZE = 256


EPS = 1e-06
CAP = 50.0
BASE = 10000.0


def norm_gain(vector, gain):
    return vector * lax.rsqrt(jnp.mean(vector * vector, axis=-1, keepdims=True) + EPS) * gain


def geglu(gate_in, up_in):
    return jax.nn.gelu(gate_in, approximate=True) * up_in


def rounded(value):
    return lax.optimization_barrier(value.astype(jnp.bfloat16)).astype(jnp.float32)


def angle_tables(block_pos):
    half = HEAD_SIZE // 2
    freq = BASE ** (-jnp.arange(half, dtype=jnp.float32) * 2.0 / HEAD_SIZE)
    angle = block_pos.astype(jnp.float32)[..., None] * freq
    return (jnp.cos(angle)[:, :, None, :], jnp.sin(angle)[:, :, None, :])


def turn(vector, cosine, sine):
    half = HEAD_SIZE // 2
    lower = vector[..., :half]
    upper = vector[..., half:]
    return jnp.concatenate([lower * cosine - upper * sine, upper * cosine + lower * sine], axis=-1)


def turn_back(grad, cosine, sine):
    half = HEAD_SIZE // 2
    lower = grad[..., :half]
    upper = grad[..., half:]
    return jnp.concatenate([lower * cosine + upper * sine, upper * cosine - lower * sine], axis=-1)


def load_attention(
    query_weight, key_weight, value_weight, output_weight, gain_table, key_value_begin, kv_cols
):
    key_full, value_full = (
        lax.all_gather(key_weight, ("dp", "ctx", "seq"), axis=0, tiled=True),
        lax.all_gather(value_weight, ("dp", "ctx", "seq"), axis=0, tiled=True),
    )
    key_part = lax.dynamic_slice_in_dim(key_full, key_value_begin, kv_cols, 1)
    value_part = lax.dynamic_slice_in_dim(value_full, key_value_begin, kv_cols, 1)
    w_query, w_output, gain_full = (
        lax.all_gather(query_weight, ("dp", "ctx"), axis=0, tiled=True),
        lax.all_gather(output_weight, ("dp", "ctx"), axis=1, tiled=True),
        lax.all_gather(gain_table, ("dp", "ctx"), axis=0, tiled=True),
    )
    return (w_query, key_part, value_part, w_output, gain_full)


def load_ffn(w_gate, w_up, w_down):
    return (
        lax.all_gather(w_gate, ("dp", "ctx"), axis=0, tiled=True),
        lax.all_gather(w_up, ("dp", "ctx"), axis=0, tiled=True),
        lax.all_gather(w_down, ("dp", "ctx"), axis=1, tiled=True),
    )


def full_output(output_part):
    return lax.all_gather(output_part, "seq", axis=0, tiled=True)


def block_rows(local_rows):
    return lax.all_gather(local_rows, "seq", axis=1, tiled=True)


def row_total(partial_rows):
    return lax.psum_scatter(
        partial_rows.astype(jnp.bfloat16), "seq", scatter_dimension=1, tiled=True
    ).astype(jnp.float32)


def visible_mask(first_row, row_count, key_count, query_pos):
    query_idx = first_row + jnp.arange(row_count, dtype=jnp.int32)
    key_idx = jnp.arange(key_count, dtype=jnp.int32)
    return (key_idx[None, :] <= query_idx[:, None]) & (
        key_idx[None, :] >= (query_idx - query_pos)[:, None]
    )


def scores_of(queries, key_rows, first_row, query_pos):
    row_count = queries.shape[0]
    head_count = queries.shape[1] // HEAD_SIZE
    query_heads = queries.reshape(row_count, head_count, HEAD_SIZE)
    key_heads = key_rows.reshape(key_rows.shape[0], head_count, HEAD_SIZE)
    scores = jnp.einsum(
        "qhd,khd->hqk", query_heads, key_heads, preferred_element_type=jnp.float32
    ) * HEAD_SIZE ** (-0.5)
    bent = jnp.tanh(scores / CAP)
    visible = visible_mask(first_row, row_count, key_rows.shape[0], query_pos)
    masked = jnp.where(visible[None], CAP * bent, -1e30)
    return (query_heads, key_heads, bent, masked)


def attend_forward(queries, key_rows, value_rows, query_pos, first_row):
    query_heads, key_heads, bent, masked = scores_of(queries, key_rows, first_row, query_pos)
    head_count = query_heads.shape[1]
    value_heads = value_rows.reshape(value_rows.shape[0], head_count, HEAD_SIZE)
    row_max = jnp.max(masked, axis=-1, keepdims=True)
    exponent = jnp.exp(masked - row_max)
    row_sum = jnp.sum(exponent, axis=-1, keepdims=True)
    probability = (exponent / row_sum).astype(jnp.bfloat16)
    log_total = (row_max + jnp.log(row_sum))[..., 0]
    result = jnp.einsum(
        "hqk,khd->qhd", probability, value_heads, preferred_element_type=jnp.float32
    )
    return (
        result.astype(jnp.bfloat16).reshape(queries.shape[0], head_count * HEAD_SIZE),
        log_total,
    )


def attend_backward(queries, key_rows, value_rows, query_pos, first_row, log_total, grad_rows):
    query_heads, key_heads, bent, masked = scores_of(queries, key_rows, first_row, query_pos)
    head_count = query_heads.shape[1]
    value_heads = value_rows.reshape(value_rows.shape[0], head_count, HEAD_SIZE)
    grad_heads = grad_rows.reshape(queries.shape[0], head_count, HEAD_SIZE)
    probability = jnp.exp(masked - log_total[..., None])
    prob_low = probability.astype(jnp.bfloat16)
    grad_value = jnp.einsum(
        "hqk,qhd->khd", prob_low, grad_heads, preferred_element_type=jnp.float32
    )
    grad_prob = jnp.einsum(
        "qhd,khd->hqk", grad_heads, value_heads, preferred_element_type=jnp.float32
    )
    delta = jnp.sum(probability * grad_prob, axis=-1, keepdims=True)
    grad_scores = (probability * (grad_prob - delta) * (1.0 - bent * bent)).astype(jnp.bfloat16)
    grad_query = jnp.einsum(
        "hqk,khd->qhd", grad_scores, key_heads, preferred_element_type=jnp.float32
    ) * HEAD_SIZE ** (-0.5)
    grad_key = jnp.einsum(
        "hqk,qhd->khd", grad_scores, query_heads, preferred_element_type=jnp.float32
    ) * HEAD_SIZE ** (-0.5)
    key_count = key_rows.shape[0]
    return (
        grad_query.reshape(queries.shape[0], head_count * HEAD_SIZE),
        grad_key.reshape(key_count, head_count * HEAD_SIZE),
        grad_value.reshape(key_count, head_count * HEAD_SIZE),
    )


def general_local(
    inputs,
    positions,
    query_weight,
    key_weight,
    value_weight,
    output_weight,
    gate_weight,
    up_weight,
    down_weight,
    pre_attn_gain,
    post_attn_gain,
    pre_ffn_gain,
    post_ffn_gain,
    cotangent,
):
    seqs, tokens, width = inputs.shape
    block_len = positions.shape[1]
    full_len = block_len * lax.axis_size("ctx")
    offset = lax.axis_index("ctx") * block_len
    head_count = QUERY_HEAD_COUNT // lax.axis_size("seq")
    key_value_group = QUERY_HEAD_COUNT // KEY_VALUE_HEADS
    kv_heads = max(head_count // key_value_group, 1)
    kv_cols = kv_heads * HEAD_SIZE
    repeat_by = head_count // kv_heads
    head_cols = head_count * HEAD_SIZE
    key_value_begin = lax.axis_index("seq") * head_count // key_value_group * HEAD_SIZE
    cosine, sine = angle_tables(positions)
    gain_table = jnp.stack([pre_attn_gain, post_attn_gain, pre_ffn_gain, post_ffn_gain], axis=1)
    fwd_attn = load_attention(
        query_weight, key_weight, value_weight, output_weight, gain_table, key_value_begin, kv_cols
    )
    fwd_ffn = load_ffn(gate_weight, up_weight, down_weight)
    w_query, key_matrix, value_matrix, w_output, gain_full = fwd_attn
    w_gate, w_up, w_down = fwd_ffn
    gain_float = gain_full.astype(jnp.float32)
    gain_one = gain_float[:, 0]
    gain_two = gain_float[:, 1]
    gain_three = gain_float[:, 2]
    gain_four = gain_float[:, 3]
    x_float = inputs.astype(jnp.float32)
    normed_one = norm_gain(x_float, gain_one).astype(jnp.bfloat16)
    block_one = block_rows(normed_one)
    query_raw = jnp.einsum("srd,de->sre", block_one, w_query, preferred_element_type=jnp.float32)
    key_raw = jnp.einsum("srd,de->sre", block_one, key_matrix, preferred_element_type=jnp.float32)
    value_raw = jnp.einsum(
        "srd,de->sre", block_one, value_matrix, preferred_element_type=jnp.float32
    )
    query_rot = (
        turn(query_raw.reshape(seqs, block_len, head_count, HEAD_SIZE), cosine, sine)
        .astype(jnp.bfloat16)
        .reshape(seqs, block_len, head_cols)
    )
    key_rot = (
        turn(key_raw.reshape(seqs, block_len, kv_heads, HEAD_SIZE), cosine, sine)
        .astype(jnp.bfloat16)
        .reshape(seqs, block_len, kv_cols)
    )
    key_all, value_all = (
        lax.all_gather(key_rot, "ctx", axis=1, tiled=True),
        lax.all_gather(value_raw.astype(jnp.bfloat16), "ctx", axis=1, tiled=True),
    )
    key_broadcast = jnp.repeat(
        key_all.reshape(seqs, full_len, kv_heads, HEAD_SIZE), repeat_by, axis=2
    ).reshape(seqs, full_len, head_cols)
    value_broadcast = jnp.repeat(
        value_all.reshape(seqs, full_len, kv_heads, HEAD_SIZE), repeat_by, axis=2
    ).reshape(seqs, full_len, head_cols)
    query_block = math.gcd(block_len, 512)
    block_count = block_len // query_block
    item_count = seqs * block_count
    item_index = jnp.arange(item_count, dtype=jnp.int32)
    block_starts = offset + item_index % block_count * query_block
    seq_owner = item_index // block_count

    def forward_item(pieces):
        queries, query_pos, first_row, seq_id = pieces
        key_rows = lax.dynamic_index_in_dim(key_broadcast, seq_id, 0, keepdims=False)
        value_rows = lax.dynamic_index_in_dim(value_broadcast, seq_id, 0, keepdims=False)
        return attend_forward(queries, key_rows, value_rows, query_pos, first_row)

    head_items, log_total = lax.map(forward_item, (query_rot, positions, block_starts, seq_owner))
    out_full = full_output(w_output)
    heads_tok = lax.all_to_all(head_items, "seq", split_axis=1, concat_axis=2, tiled=True)
    project = jnp.einsum("ste,ed->std", heads_tok, out_full, preferred_element_type=jnp.float32)
    middle = x_float + norm_gain(project, gain_two)
    normed_two = norm_gain(middle, gain_three).astype(jnp.bfloat16)
    ffn_input = block_rows(normed_two)
    gate = jnp.einsum("srd,df->srf", ffn_input, w_gate, preferred_element_type=jnp.float32)
    upper = jnp.einsum("srd,df->srf", ffn_input, w_up, preferred_element_type=jnp.float32)
    hidden = geglu(gate, upper).astype(jnp.bfloat16)
    feed = row_total(jnp.einsum("srf,fd->srd", hidden, w_down, preferred_element_type=jnp.float32))
    layer_output = (middle + norm_gain(feed, gain_four)).astype(jnp.bfloat16)
    back_attn = load_attention(
        query_weight, key_weight, value_weight, output_weight, gain_table, key_value_begin, kv_cols
    )
    back_ffn = load_ffn(gate_weight, up_weight, down_weight)
    bq_weight, bk_weight, bv_weight, bo_weight = (
        back_attn[0],
        back_attn[1],
        back_attn[2],
        back_attn[3],
    )
    bgate_weight, bup_weight, bdown_weight = back_ffn
    grad_top = cotangent.astype(jnp.float32)
    unused, pull_four = jax.vjp(norm_gain, feed, gain_four)
    grad_feed, grad_g_four = pull_four(grad_top)
    grad_feed_rows = block_rows(grad_feed.astype(jnp.bfloat16))
    grad_hidden = jnp.einsum(
        "srd,fd->srf", grad_feed_rows, bdown_weight, preferred_element_type=jnp.float32
    )
    grad_down_part = jnp.einsum(
        "srf,srd->fd", hidden, grad_feed_rows, preferred_element_type=jnp.float32
    )
    unused, pull_act = jax.vjp(geglu, gate, upper)
    grad_gate_act, grad_up_act = pull_act(grad_hidden)
    grad_gate_act = grad_gate_act.astype(jnp.bfloat16)
    grad_up_act = grad_up_act.astype(jnp.bfloat16)
    grad_rows_part = jnp.einsum(
        "srf,df->srd", grad_gate_act, bgate_weight, preferred_element_type=jnp.float32
    ) + jnp.einsum("srf,df->srd", grad_up_act, bup_weight, preferred_element_type=jnp.float32)
    grad_gate_part = jnp.einsum(
        "srd,srf->df", ffn_input, grad_gate_act, preferred_element_type=jnp.float32
    )
    grad_up_part = jnp.einsum(
        "srd,srf->df", ffn_input, grad_up_act, preferred_element_type=jnp.float32
    )
    ffn_grads = (
        lax.psum_scatter(
            grad_gate_part.astype(jnp.bfloat16), ("dp", "ctx"), scatter_dimension=0, tiled=True
        ).astype(jnp.float32),
        lax.psum_scatter(
            grad_up_part.astype(jnp.bfloat16), ("dp", "ctx"), scatter_dimension=0, tiled=True
        ).astype(jnp.float32),
        lax.psum_scatter(
            grad_down_part.astype(jnp.bfloat16), ("dp", "ctx"), scatter_dimension=1, tiled=True
        ).astype(jnp.float32),
    )
    grad_normed_two = row_total(grad_rows_part)
    unused, pull_three = jax.vjp(norm_gain, middle, gain_three)
    grad_mid_norm, grad_g_three = pull_three(grad_normed_two)
    grad_middle = grad_top + grad_mid_norm
    unused, pull_two = jax.vjp(norm_gain, project, gain_two)
    grad_project, grad_g_two = pull_two(grad_middle)
    grad_project = grad_project.astype(jnp.bfloat16)
    out_back = full_output(bo_weight)
    grad_heads_tok = jnp.einsum(
        "std,ed->ste", grad_project, out_back, preferred_element_type=jnp.float32
    ).astype(jnp.bfloat16)
    grad_output_part = lax.psum_scatter(
        jnp.einsum(
            "ste,std->ed", heads_tok, grad_project, preferred_element_type=jnp.float32
        ).astype(jnp.bfloat16),
        "seq",
        scatter_dimension=0,
        tiled=True,
    )
    grad_heads = lax.all_to_all(grad_heads_tok, "seq", split_axis=2, concat_axis=1, tiled=True)

    def backward_item(carry, pieces):
        key_acc, value_acc = carry
        queries, query_pos, first_row, seq_id, log_part, grad_part = pieces
        key_rows = lax.dynamic_index_in_dim(key_broadcast, seq_id, 0, keepdims=False)
        value_rows = lax.dynamic_index_in_dim(value_broadcast, seq_id, 0, keepdims=False)
        grad_query, grad_key, grad_value = attend_backward(
            queries, key_rows, value_rows, query_pos, first_row, log_part, grad_part
        )
        key_acc = lax.dynamic_update_index_in_dim(
            key_acc,
            lax.dynamic_index_in_dim(key_acc, seq_id, 0, keepdims=False) + grad_key,
            seq_id,
            0,
        )
        value_acc = lax.dynamic_update_index_in_dim(
            value_acc,
            lax.dynamic_index_in_dim(value_acc, seq_id, 0, keepdims=False) + grad_value,
            seq_id,
            0,
        )
        return ((key_acc, value_acc), grad_query)

    empty = jnp.zeros((seqs, full_len, head_cols), jnp.float32)
    (key_terms, value_terms), grad_query_items = lax.scan(
        backward_item,
        (empty, empty),
        (query_rot, positions, block_starts, seq_owner, log_total, grad_heads),
    )
    key_sums, value_sums = (
        lax.psum_scatter(
            key_terms.astype(jnp.bfloat16), "ctx", scatter_dimension=1, tiled=True
        ).astype(jnp.float32),
        lax.psum_scatter(
            value_terms.astype(jnp.bfloat16), "ctx", scatter_dimension=1, tiled=True
        ).astype(jnp.float32),
    )
    grad_query_rot = rounded(grad_query_items.reshape(seqs, block_len, head_count, HEAD_SIZE))
    grad_query_raw = (
        turn_back(grad_query_rot, cosine, sine)
        .astype(jnp.bfloat16)
        .reshape(seqs, block_len, head_cols)
    )
    grad_key_rot = rounded(key_sums.reshape(seqs, block_len, head_count, HEAD_SIZE))
    grad_key_raw = (
        turn_back(grad_key_rot, cosine, sine)
        .astype(jnp.bfloat16)
        .reshape(seqs, block_len, head_cols)
    )
    grad_value_raw = value_sums.astype(jnp.bfloat16)
    key_expand = jnp.repeat(
        bk_weight.reshape(width, kv_heads, HEAD_SIZE), repeat_by, axis=1
    ).reshape(width, head_cols)
    value_expand = jnp.repeat(
        bv_weight.reshape(width, kv_heads, HEAD_SIZE), repeat_by, axis=1
    ).reshape(width, head_cols)
    grad_block_one = jnp.einsum(
        "sre,de->srd", grad_query_raw, bq_weight, preferred_element_type=jnp.float32
    )
    grad_block_one = grad_block_one + jnp.einsum(
        "sre,de->srd", grad_key_raw, key_expand, preferred_element_type=jnp.float32
    )
    grad_block_one = grad_block_one + jnp.einsum(
        "sre,de->srd", grad_value_raw, value_expand, preferred_element_type=jnp.float32
    )
    grad_normed_one = row_total(grad_block_one)
    grad_query_part = jnp.einsum(
        "srd,sre->de", block_one, grad_query_raw, preferred_element_type=jnp.float32
    )
    grad_key_wide = jnp.einsum(
        "srd,sre->de", block_one, grad_key_raw, preferred_element_type=jnp.float32
    )
    grad_value_wide = jnp.einsum(
        "srd,sre->de", block_one, grad_value_raw, preferred_element_type=jnp.float32
    )
    grad_key_part = jnp.sum(
        grad_key_wide.reshape(width, kv_heads, repeat_by, HEAD_SIZE), axis=2
    ).reshape(width, kv_cols)
    grad_value_part = jnp.sum(
        grad_value_wide.reshape(width, kv_heads, repeat_by, HEAD_SIZE), axis=2
    ).reshape(width, kv_cols)
    unused, pull_one = jax.vjp(norm_gain, x_float, gain_one)
    grad_input_norm, grad_g_one = pull_one(grad_normed_one)
    input_grad = (grad_middle + grad_input_norm).astype(jnp.bfloat16)
    gain_grads = jnp.stack([grad_g_one, grad_g_two, grad_g_three, grad_g_four], axis=1)
    attention_gradients = (
        lax.psum_scatter(
            grad_query_part.astype(jnp.bfloat16), ("dp", "ctx"), scatter_dimension=0, tiled=True
        ).astype(jnp.float32),
        lax.psum_scatter(grad_output_part, ("dp", "ctx"), scatter_dimension=1, tiled=True).astype(
            jnp.float32
        ),
    )
    key_spread = lax.dynamic_update_slice_in_dim(
        jnp.zeros((width, KEY_VALUE_HEADS * HEAD_SIZE), jnp.float32),
        grad_key_part,
        key_value_begin,
        1,
    )
    value_spread = lax.dynamic_update_slice_in_dim(
        jnp.zeros((width, KEY_VALUE_HEADS * HEAD_SIZE), jnp.float32),
        grad_value_part,
        key_value_begin,
        1,
    )
    kv_sums = (
        lax.psum_scatter(key_spread, ("dp", "ctx", "seq"), scatter_dimension=0, tiled=True),
        lax.psum_scatter(value_spread, ("dp", "ctx", "seq"), scatter_dimension=0, tiled=True),
        lax.psum_scatter(gain_grads, ("dp", "ctx", "seq"), scatter_dimension=0, tiled=True),
    )
    gain_out = kv_sums[2]
    return (
        layer_output,
        input_grad,
        attention_gradients[0],
        kv_sums[0],
        kv_sums[1],
        attention_gradients[1],
        ffn_grads[0],
        ffn_grads[1],
        ffn_grads[2],
        gain_out[:, 0],
        gain_out[:, 1],
        gain_out[:, 2],
        gain_out[:, 3],
    )


def flip(value, axis):
    return lax.ppermute(value, axis, [(0, 1), (1, 0)])


def ordered(index, own, other, axis=0):
    return jnp.where(
        index == 0, jnp.stack([own, other], axis=axis), jnp.stack([other, own], axis=axis)
    )


def pick(value, index, axis=0):
    return lax.dynamic_index_in_dim(value, index, axis, keepdims=False)


def after(value, *earlier):
    return lax.optimization_barrier((value, *earlier))[0]


def total(kept, *got):
    value = kept.astype(jnp.float32)
    for more in got:
        value = value + more.astype(jnp.float32)
    return value


def trade_sequences(value):
    cy = lax.axis_index("cy")
    return ordered(cy, pick(value, cy), flip(pick(value, 1 - cy), "cy"))


def core_columns(matrices, core):
    parts = []
    for matrix, begin, width in matrices:
        at = core * (matrix.shape[1] // 2) + begin
        parts.append(lax.dynamic_slice_in_dim(matrix, at, width, 1))
    return jnp.concatenate(parts, axis=1) if len(parts) > 1 else parts[0]


def start_gather(*matrices):
    c = lax.axis_index("core")
    got = flip(core_columns(matrices, 1 - c), "core")
    rows = ordered(c, core_columns(matrices, c), got)
    return rows, flip(rows, "cy"), flip(rows, "dp")


def next_gather(rows, rows_y, rows_x):
    return rows, rows_y, rows_x, flip(rows_y[0], "dp"), flip(rows_x[1], "cy")


def place_kernel(moves, count, *refs):
    sources, outs = refs[:count], refs[count : len(refs) - count - 2]
    held, sem_in, sem_out = refs[-count - 2 : -2], refs[-2], refs[-1]
    x, y = lax.axis_index("dp"), lax.axis_index("cy")
    loads = [
        pltpu.make_async_copy(source, buffer, sem_in.at[i])
        for i, (source, buffer) in enumerate(zip(sources, held))
    ]
    for load in loads:
        load.start()
    stores = []
    for i, (load, buffer) in enumerate(zip(loads, held)):
        load.wait()
        for out, begin, to, cols in moves[i // 5]:
            out, to = outs[out], pl.ds(to, cols)
            target = (
                out.at[x, y, :, :, to],
                out.at[x, 1 - y, :, :, to],
                out.at[1 - x, y, :, :, to],
                out.at[1 - x, 1 - y, 0, :, to],
                out.at[1 - x, 1 - y, 1, :, to],
            )[i % 5]
            at = pl.ds(begin, cols)
            piece = buffer.at[:, :, at] if i % 5 < 3 else buffer.at[:, at]
            stores.append(pltpu.make_async_copy(piece, target, sem_out.at[len(stores)]))
            stores[-1].start()
    for store in stores:
        store.wait()


def end_gather(gathers, moves, widths):
    pieces = [piece for begun in gathers for piece in begun]
    rows, low = pieces[0].shape[1], pieces[0].dtype
    size = 8 * rows * sum(widths) * low.itemsize
    anywhere = pl.BlockSpec(memory_space=pl.ANY)
    stores = 5 * sum(len(some) for some in moves)
    outs = pl.pallas_call(
        functools.partial(place_kernel, moves, len(pieces)),
        out_shape=[jax.ShapeDtypeStruct((2, 2, 2, rows, width), low) for width in widths],
        in_specs=[anywhere] * len(pieces),
        out_specs=[anywhere] * len(widths),
        scratch_shapes=[pltpu.VMEM(piece.shape, low) for piece in pieces]
        + [pltpu.SemaphoreType.DMA((len(pieces),)), pltpu.SemaphoreType.DMA((stores,))],
        compiler_params=pltpu.CompilerParams(vmem_limit_bytes=size + (2 << 20)),
        cost_estimate=pl.CostEstimate(flops=0, bytes_accessed=2 * size, transcendentals=0),
        name="place_rows",
    )(*pieces)
    return [out.reshape(-1, out.shape[-1]) for out in outs]


def start_scatter(grad):
    x, y = lax.axis_index("dp"), lax.axis_index("cy")
    parts = grad.reshape(2, 2, 2, -1, grad.shape[-1])
    return parts, pick(parts, 1 - x)[:, 0], pick(parts, 1 - y, 1)[:, 1]


def send_scatter(parts, by_x, by_y):
    return parts, flip(by_x, "dp"), flip(by_y, "cy")


def next_scatter(parts, from_x, from_y):
    x, y = lax.axis_index("dp"), lax.axis_index("cy")
    by_y = total(pick(pick(parts, x), 1 - y)[0], pick(from_x, 1 - y)).astype(parts.dtype)
    by_x = total(pick(pick(parts, 1 - x), y)[1], pick(from_y, 1 - x)).astype(parts.dtype)
    return parts, from_x, from_y, flip(by_y, "cy"), flip(by_x, "dp")


def end_scatter(parts, from_x, from_y, last_y, last_x):
    x, y, c = lax.axis_index("dp"), lax.axis_index("cy"), lax.axis_index("core")
    own = pick(pick(parts, x), y)
    first = total(own[0], pick(from_x, y), last_y)
    second = total(own[1], pick(from_y, x), last_x)
    keep = jnp.where(c == 0, first, second)
    away = jnp.where(c == 0, second, first).astype(jnp.bfloat16)
    got = flip(away, "core").astype(jnp.float32)
    return jnp.where(c == 0, keep, got), jnp.where(c == 0, got, keep)


def gather_gains(table):
    table = ordered(lax.axis_index("core"), table, flip(table, "core"), axis=1)
    table = ordered(lax.axis_index("cy"), table, flip(table, "cy"), axis=1)
    table = ordered(lax.axis_index("dp"), table, flip(table, "dp"), axis=1)
    return table.reshape(table.shape[0], -1)


def exchange_seq(parts):
    z, size = lax.axis_index("seq"), lax.axis_size("seq")
    got = [pick(parts, z)]
    for step in range(1, size):
        ring = [(i, (i + step) % size) for i in range(size)]
        got.insert(0, lax.ppermute(pick(parts, lax.rem(z + step, size)), "seq", ring))
    got = jnp.stack(got + got[:-1])
    return lax.dynamic_slice_in_dim(got, size - 1 - z, size, 0)


def shift(value, step):
    size = lax.axis_size("seq")
    return lax.ppermute(value, "seq", [(i, (i + step) % size) for i in range(size)])


def gather_rows(local_rows):
    size = lax.axis_size("seq")
    got = {step: shift(local_rows, step) for step in (3, 1, 2)}
    pieces = [local_rows] + [got[size - ahead] for ahead in range(1, size)]
    return jnp.concatenate(pieces + [flip(piece, "core") for piece in pieces])


def join_kernel(whole, out, held, sem):
    c, z = lax.axis_index("core"), lax.axis_index("seq")
    size, rows = whole.shape[0] // 2, whole.shape[1]
    loads = []
    for i in range(2 * size):
        owner = (c if i < size else 1 - c) * size + lax.rem(z + i % size, size)
        target = held.at[pl.ds(i * rows, rows)]
        loads.append(pltpu.make_async_copy(whole.at[owner], target, sem.at[i]))
    for load in loads:
        load.start()
    for load in loads:
        load.wait()
    store = pltpu.make_async_copy(held, out, sem.at[2 * size])
    store.start()
    store.wait()


def gather_first(local_rows):
    whole = lax.all_gather(local_rows, ("core", "seq"), axis=0)
    shape, low = (whole.shape[0] * whole.shape[1], whole.shape[2]), whole.dtype
    size = whole.size * low.itemsize
    anywhere = pl.BlockSpec(memory_space=pl.ANY)
    return pl.pallas_call(
        join_kernel,
        out_shape=jax.ShapeDtypeStruct(shape, low),
        in_specs=[anywhere],
        out_specs=anywhere,
        scratch_shapes=[
            pltpu.VMEM(shape, low),
            pltpu.SemaphoreType.DMA((whole.shape[0] + 1,)),
        ],
        compiler_params=pltpu.CompilerParams(vmem_limit_bytes=size + (2 << 20)),
        cost_estimate=pl.CostEstimate(flops=0, bytes_accessed=2 * size, transcendentals=0),
        name="join_rows",
    )(whole)


def row_tokens(rows, length):
    c, z, size = lax.axis_index("core"), lax.axis_index("seq"), lax.axis_size("seq")
    shape = (2, size, 2, rows // 2)
    core = jnp.where(lax.broadcasted_iota(jnp.int32, shape, 0) == 0, c, 1 - c)
    owner = lax.rem(z + lax.broadcasted_iota(jnp.int32, shape, 1), size)
    begin = lax.broadcasted_iota(jnp.int32, shape, 2) * (length // 2)
    row = lax.broadcasted_iota(jnp.int32, shape, 3)
    return (begin + (core * size + owner) * (rows // 2) + row).reshape(-1)


def row_order(values):
    c, z, size = lax.axis_index("core"), lax.axis_index("seq"), lax.axis_size("seq")
    parts = values.reshape(2, 2, size, -1).transpose(1, 2, 0, 3)
    parts = jnp.stack([pick(parts, c), pick(parts, 1 - c)])
    parts = jnp.concatenate([parts, parts], axis=1)
    return lax.dynamic_slice_in_dim(parts, z, size, 1).reshape(-1)


def core_swap(value):
    half = value.shape[0] // 2
    got = flip(value, "core")
    return jnp.concatenate([got[half:], got[:half]])


def core_rows(left, right, dims):
    half = left.shape[0] // 2
    got = flip(dot(left[half:], right, dims).astype(jnp.bfloat16), "core")
    kept = lax.optimization_barrier(dot(left[:half], right, dims).astype(jnp.bfloat16))
    return total(kept, got).astype(jnp.bfloat16)


def core_sums(partial_rows):
    half = partial_rows.shape[0] // 2
    return total(partial_rows[:half], flip(partial_rows[half:], "core")).astype(jnp.bfloat16)


def scatter_rows(sums):
    size = lax.axis_size("seq")
    parts = sums.reshape(size, -1, sums.shape[-1])
    got = [shift(parts[step], step) for step in (3, 1, 2)]
    return total(parts[0], *got)


def chip_rows(*matrices):
    c = lax.axis_index("core")
    got = flip(core_columns(matrices, 1 - c), "core")
    return ordered(c, core_columns(matrices, c), got)


def gather_chips(rows):
    whole = lax.all_gather(rows.reshape(-1, rows.shape[-1]), ("dp", "cy"), axis=0, tiled=True)
    return whole


def scatter_chips(grad):
    sums = lax.psum_scatter(grad, ("dp", "cy"), scatter_dimension=0, tiled=True)
    return sums.reshape(2, -1, sums.shape[-1])


def both_columns(sums):
    c = lax.axis_index("core")
    keep = pick(sums, c).astype(jnp.float32)
    got = flip(pick(sums, 1 - c), "core").astype(jnp.float32)
    return jnp.where(c == 0, keep, got), jnp.where(c == 0, got, keep)


def dot(left, right, dims):
    return lax.dot_general(
        left, right, ((dims[:1], dims[1:]), ((), ())), preferred_element_type=jnp.float32
    )


def head_scores(queries, keys, visible):
    bent = jnp.tanh(dot(queries, keys, (1, 1)) * (HEAD_SIZE ** (-0.5) / CAP))
    return bent, jnp.where(visible, CAP * bent, -1e30)


def head_local(
    inputs,
    positions,
    query_weight,
    key_weight,
    value_weight,
    output_weight,
    gate_weight,
    up_weight,
    down_weight,
    pre_attn_gain,
    post_attn_gain,
    pre_ffn_gain,
    post_ffn_gain,
    cotangent,
):
    c, cy = lax.axis_index("core"), lax.axis_index("cy")
    low = jnp.bfloat16
    rows_own = query_weight.shape[0]
    ffn_cols = gate_weight.shape[1] // 2

    kv_stack = jnp.stack([key_weight, value_weight], axis=1)
    kv_stack = kv_stack.reshape(-1, 2, KEY_VALUE_HEADS, HEAD_SIZE).transpose(2, 0, 1, 3)
    kv_rows = exchange_seq(kv_stack).reshape(rows_own, 2 * HEAD_SIZE)
    x_local = after(trade_sequences(inputs), kv_rows)
    own_shape = x_local.shape
    x_local = x_local.reshape(-1, x_local.shape[-1])
    block_x = gather_first(x_local)
    x_float = x_local.astype(jnp.float32)
    gain_table = jnp.stack([pre_attn_gain, post_attn_gain, pre_ffn_gain, post_ffn_gain], axis=0)
    gain_one, gain_two, gain_three, gain_four = gather_gains(gain_table).astype(jnp.float32)

    pos_own = trade_sequences(positions)
    seq_pos = ordered(c, pos_own, flip(pos_own, "core"), axis=1).reshape(-1)
    half = HEAD_SIZE // 2
    freq = BASE ** (-jnp.arange(half, dtype=jnp.float32) * 2.0 / HEAD_SIZE)
    token = row_tokens(x_local.shape[0], seq_pos.shape[0])
    seq_pos = row_order(seq_pos)
    angle = seq_pos.astype(jnp.float32)[:, None] * freq
    cosine, sine = jnp.cos(angle), jnp.sin(angle)
    kv_cosine = jnp.where(c == 0, cosine, 1.0)
    kv_sine = jnp.where(c == 0, sine, 0.0)

    attn_begun = next_gather(
        *start_gather(
            (query_weight, 0, HEAD_SIZE), (kv_rows, 0, HEAD_SIZE), (output_weight.T, 0, HEAD_SIZE)
        )
    )
    split = 2 * HEAD_SIZE
    in_weight, out_weight = end_gather(
        [attn_begun], [((0, 0, 0, split), (1, split, 0, HEAD_SIZE))], (split, HEAD_SIZE)
    )
    gate_up_rows = chip_rows((gate_weight, 0, ffn_cols), (up_weight, 0, ffn_cols))
    gate_up_weight = gather_chips(gate_up_rows)
    down_back = gather_chips(chip_rows((down_weight.T, 0, ffn_cols)))
    grad_top = trade_sequences(after(cotangent, attn_begun))

    block_one = norm_gain(block_x.astype(jnp.float32), gain_one).astype(low)
    raw = dot(block_one, in_weight, (1, 0))
    queries = turn(raw[:, :HEAD_SIZE], cosine, sine).astype(low)
    kv_own = turn(raw[:, HEAD_SIZE:], kv_cosine, kv_sine).astype(low)
    kv_other = core_swap(kv_own)
    keys = jnp.where(c == 0, kv_own, kv_other)
    values = jnp.where(c == 0, kv_other, kv_own)
    visible = (token[None, :] <= token[:, None]) & (token[None, :] >= (token - seq_pos)[:, None])
    bent, masked = head_scores(queries, keys, visible)
    row_max = jnp.max(masked, axis=-1, keepdims=True)
    exponent = jnp.exp(masked - row_max)
    row_sum = jnp.sum(exponent, axis=-1, keepdims=True)
    heads = dot((exponent / row_sum).astype(low), values, (1, 0)).astype(low)
    log_total = row_max + jnp.log(row_sum)
    heads = after(heads, grad_top)
    grad_top = grad_top.reshape(x_local.shape).astype(jnp.float32)

    project_core = core_sums(dot(heads, out_weight, (1, 1)).astype(low))
    project = scatter_rows(project_core)
    middle = x_float + norm_gain(project, gain_two)
    normed_two = norm_gain(middle, gain_three).astype(low)
    block_two = gather_rows(normed_two)
    gate_up = dot(block_two, gate_up_weight, (1, 0))
    gate, upper = gate_up[:, :ffn_cols], gate_up[:, ffn_cols:]
    hidden = geglu(gate, upper).astype(low)
    feed = scatter_rows(core_rows(hidden, down_back, (1, 1)))
    unused, pull_four = jax.vjp(norm_gain, feed, gain_four)
    grad_feed, grad_g_four = pull_four(grad_top)
    grad_feed = grad_feed.astype(low)
    layer_output = after((middle + norm_gain(feed, gain_four)).astype(low), grad_feed)
    layer_output = trade_sequences(layer_output.reshape(own_shape))

    grad_feed_rows = after(gather_rows(grad_feed), layer_output)
    grad_hidden = dot(grad_feed_rows, down_back, (1, 0))
    unused, pull_act = jax.vjp(geglu, gate, upper)
    grad_gate_act, grad_up_act = pull_act(grad_hidden)
    grad_gate_up = jnp.concatenate([grad_gate_act.astype(low), grad_up_act.astype(low)], axis=1)
    normed_two_core = core_sums(dot(grad_gate_up, gate_up_weight, (1, 1)).astype(low))
    grad_normed_two = scatter_rows(normed_two_core)
    late = after((hidden, block_two), normed_two_core)
    grad_down = dot(grad_feed_rows, late[0], (0, 0)).astype(low)
    grad_gu = dot(late[1], grad_gate_up, (0, 0)).astype(low)
    grad_normed_two = after(grad_normed_two, grad_down, grad_gu)
    grad_down, grad_gu = scatter_chips(grad_down), scatter_chips(grad_gu)

    unused, pull_three = jax.vjp(norm_gain, middle, gain_three)
    grad_mid_norm, grad_g_three = pull_three(grad_normed_two)
    grad_middle = grad_top + grad_mid_norm
    unused, pull_two = jax.vjp(norm_gain, project, gain_two)
    grad_project, grad_g_two = pull_two(grad_middle)
    grad_project = grad_project.astype(low)
    grad_project_rows = gather_rows(grad_project)
    grad_heads = dot(grad_project_rows, out_weight, (1, 0)).astype(low)

    bent, masked = head_scores(queries, keys, visible)
    probability = jnp.exp(masked - log_total)
    grad_value = dot(probability.astype(low), grad_heads, (0, 0)).astype(low)
    grad_prob = dot(grad_heads, values, (1, 1))
    delta = jnp.sum(probability * grad_prob, axis=-1, keepdims=True)
    grad_scores = (probability * (grad_prob - delta) * (1.0 - bent * bent)).astype(low)
    scale = HEAD_SIZE ** (-0.5)
    grad_query_rot = rounded(dot(grad_scores, keys, (1, 0)) * scale)
    grad_key_rot = rounded(dot(grad_scores, queries, (0, 0)) * scale)
    grad_query_raw = turn_back(grad_query_rot, cosine, sine).astype(low)
    grad_key_raw = turn_back(grad_key_rot, cosine, sine).astype(low)
    kv_grad_own = jnp.where(c == 0, grad_key_raw, grad_value)
    kv_grad_got = core_swap(jnp.where(c == 0, grad_value, grad_key_raw))
    grad_in = jnp.concatenate([grad_query_raw, total(kv_grad_own, kv_grad_got).astype(low)], axis=1)
    normed_one_part = dot(grad_in, in_weight, (1, 1)).astype(low)
    normed_one_core = core_sums(normed_one_part)
    grad_normed_one = scatter_rows(normed_one_core)
    block_one, heads = after((block_one, heads), normed_one_core)
    grad_in_part = dot(block_one, grad_in, (0, 0)).astype(low)
    grad_output_part = dot(grad_project_rows, heads, (0, 0)).astype(low)
    attn_grad_begun = start_scatter(jnp.concatenate([grad_in_part, grad_output_part], axis=1))
    attn_grad_begun = send_scatter(*attn_grad_begun)
    grad_normed_one = after(grad_normed_one, attn_grad_begun)
    attn_grad_begun = next_scatter(*attn_grad_begun)
    attn_grads = end_scatter(*attn_grad_begun)
    grad_down, grad_gu = after((grad_down, grad_gu), attn_grad_begun)
    grad_down, grad_gu = both_columns(grad_down), both_columns(grad_gu)

    block_x = after(block_x, attn_grad_begun[0]).astype(jnp.float32)
    unused, pull_gain = jax.vjp(lambda gain: norm_gain(block_x, gain), gain_one)
    (grad_g_one,) = pull_gain(normed_one_part.astype(jnp.float32))
    everyone = ("dp", "cy", "core", "seq")
    gain_grads = jnp.stack([grad_g_one, grad_g_two, grad_g_three, grad_g_four], axis=0)
    gain_grads = after(gain_grads, grad_normed_one, attn_grad_begun)
    gain_parts = gain_grads.reshape(4, lax.axis_size(everyone), -1).transpose(1, 0, 2)
    gain_out = jnp.sum(
        lax.all_to_all(gain_parts, everyone, split_axis=0, concat_axis=0, tiled=True), axis=0
    )

    unused, pull_one = jax.vjp(lambda rows: norm_gain(rows, gain_one), x_float)
    (grad_input_norm,) = pull_one(grad_normed_one)
    input_grad = trade_sequences((grad_middle + grad_input_norm).astype(low).reshape(own_shape))

    def whole(pair, begin, cols):
        return jnp.concatenate([part[:, begin : begin + cols] for part in pair], axis=1)

    kv_back = whole(attn_grads, HEAD_SIZE, HEAD_SIZE).astype(low)
    kv_back = exchange_seq(kv_back.reshape(KEY_VALUE_HEADS, -1, 2 * HEAD_SIZE))
    kv_back = kv_back.reshape(KEY_VALUE_HEADS, -1, 2, HEAD_SIZE).transpose(2, 1, 0, 3)
    kv_back = kv_back.reshape(2, -1, KEY_VALUE_HEADS * HEAD_SIZE).astype(jnp.float32)
    return (
        layer_output,
        input_grad,
        whole(attn_grads, 0, HEAD_SIZE),
        kv_back[0],
        kv_back[1],
        whole(attn_grads, 2 * HEAD_SIZE, HEAD_SIZE).T,
        whole(grad_gu, 0, ffn_cols),
        whole(grad_gu, ffn_cols, ffn_cols),
        whole(grad_down, 0, ffn_cols).T,
        gain_out[0],
        gain_out[1],
        gain_out[2],
        gain_out[3],
    )


def one_head_each(mesh):
    sizes = mesh.shape
    return (
        sizes["dp"] == 2
        and sizes["ctx"] == 4
        and sizes["seq"] == KEY_VALUE_HEADS
        and QUERY_HEAD_COUNT == 2 * KEY_VALUE_HEADS
    )


def solution(mesh):
    if one_head_each(mesh):
        body, ctx = head_local, ("cy", "core")
        grid = jax.sharding.Mesh(
            mesh.devices.reshape(mesh.shape["dp"], -1, 2, mesh.shape["seq"]),
            ("dp", "cy", "core", "seq"),
        )
    else:
        body, ctx, grid = general_local, ("ctx",), mesh
    owners, everyone = ("dp", *ctx), ("dp", *ctx, "seq")
    rows = P("dp", (*ctx, "seq"), None)
    tall, flat, wide = P(owners, "seq"), P(everyone, None), P("seq", owners)
    gains = (P(owners),) * 4
    return jax.shard_map(
        body,
        mesh=grid,
        in_specs=(rows, P("dp", ctx), tall, flat, flat, wide, tall, tall, wide, *gains, rows),
        out_specs=(rows, rows, tall, flat, flat, wide, tall, tall, wide, *((P(everyone),) * 4)),
        check_vma=False,
    )
```

```python
import functools
import math

import jax
import jax.numpy as jnp
from jax import lax
from jax.experimental import pallas as pl
from jax.experimental.pallas import tpu as pltpu
from jax.sharding import PartitionSpec as P

QUERY_HEAD_COUNT = 8
KEY_VALUE_HEADS = 4
HEAD_SIZE = 256


EPS = 1e-06
CAP = 50.0
BASE = 10000.0


def norm_gain(vector, gain):
    return vector * lax.rsqrt(jnp.mean(vector * vector, axis=-1, keepdims=True) + EPS) * gain


def geglu(gate_in, up_in):
    return jax.nn.gelu(gate_in, approximate=True) * up_in


def rounded(value):
    return lax.optimization_barrier(value.astype(jnp.bfloat16)).astype(jnp.float32)


def angle_tables(block_pos):
    half = HEAD_SIZE // 2
    freq = BASE ** (-jnp.arange(half, dtype=jnp.float32) * 2.0 / HEAD_SIZE)
    angle = block_pos.astype(jnp.float32)[..., None] * freq
    return (jnp.cos(angle)[:, :, None, :], jnp.sin(angle)[:, :, None, :])


def turn(vector, cosine, sine):
    half = HEAD_SIZE // 2
    lower = vector[..., :half]
    upper = vector[..., half:]
    return jnp.concatenate([lower * cosine - upper * sine, upper * cosine + lower * sine], axis=-1)


def turn_back(grad, cosine, sine):
    half = HEAD_SIZE // 2
    lower = grad[..., :half]
    upper = grad[..., half:]
    return jnp.concatenate([lower * cosine + upper * sine, upper * cosine - lower * sine], axis=-1)


def load_attention(
    query_weight, key_weight, value_weight, output_weight, gain_table, key_value_begin, kv_cols
):
    key_full, value_full = (
        lax.all_gather(key_weight, ("dp", "ctx", "seq"), axis=0, tiled=True),
        lax.all_gather(value_weight, ("dp", "ctx", "seq"), axis=0, tiled=True),
    )
    key_part = lax.dynamic_slice_in_dim(key_full, key_value_begin, kv_cols, 1)
    value_part = lax.dynamic_slice_in_dim(value_full, key_value_begin, kv_cols, 1)
    w_query, w_output, gain_full = (
        lax.all_gather(query_weight, ("dp", "ctx"), axis=0, tiled=True),
        lax.all_gather(output_weight, ("dp", "ctx"), axis=1, tiled=True),
        lax.all_gather(gain_table, ("dp", "ctx"), axis=0, tiled=True),
    )
    return (w_query, key_part, value_part, w_output, gain_full)


def load_ffn(w_gate, w_up, w_down):
    return (
        lax.all_gather(w_gate, ("dp", "ctx"), axis=0, tiled=True),
        lax.all_gather(w_up, ("dp", "ctx"), axis=0, tiled=True),
        lax.all_gather(w_down, ("dp", "ctx"), axis=1, tiled=True),
    )


def full_output(output_part):
    return lax.all_gather(output_part, "seq", axis=0, tiled=True)


def block_rows(local_rows):
    return lax.all_gather(local_rows, "seq", axis=1, tiled=True)


def row_total(partial_rows):
    return lax.psum_scatter(
        partial_rows.astype(jnp.bfloat16), "seq", scatter_dimension=1, tiled=True
    ).astype(jnp.float32)


def visible_mask(first_row, row_count, key_count, query_pos):
    query_idx = first_row + jnp.arange(row_count, dtype=jnp.int32)
    key_idx = jnp.arange(key_count, dtype=jnp.int32)
    return (key_idx[None, :] <= query_idx[:, None]) & (
        key_idx[None, :] >= (query_idx - query_pos)[:, None]
    )


def scores_of(queries, key_rows, first_row, query_pos):
    row_count = queries.shape[0]
    head_count = queries.shape[1] // HEAD_SIZE
    query_heads = queries.reshape(row_count, head_count, HEAD_SIZE)
    key_heads = key_rows.reshape(key_rows.shape[0], head_count, HEAD_SIZE)
    scores = jnp.einsum(
        "qhd,khd->hqk", query_heads, key_heads, preferred_element_type=jnp.float32
    ) * HEAD_SIZE ** (-0.5)
    bent = jnp.tanh(scores / CAP)
    visible = visible_mask(first_row, row_count, key_rows.shape[0], query_pos)
    masked = jnp.where(visible[None], CAP * bent, -1e30)
    return (query_heads, key_heads, bent, masked)


def attend_forward(queries, key_rows, value_rows, query_pos, first_row):
    query_heads, key_heads, bent, masked = scores_of(queries, key_rows, first_row, query_pos)
    head_count = query_heads.shape[1]
    value_heads = value_rows.reshape(value_rows.shape[0], head_count, HEAD_SIZE)
    row_max = jnp.max(masked, axis=-1, keepdims=True)
    exponent = jnp.exp(masked - row_max)
    row_sum = jnp.sum(exponent, axis=-1, keepdims=True)
    probability = (exponent / row_sum).astype(jnp.bfloat16)
    log_total = (row_max + jnp.log(row_sum))[..., 0]
    result = jnp.einsum(
        "hqk,khd->qhd", probability, value_heads, preferred_element_type=jnp.float32
    )
    return (
        result.astype(jnp.bfloat16).reshape(queries.shape[0], head_count * HEAD_SIZE),
        log_total,
    )


def attend_backward(queries, key_rows, value_rows, query_pos, first_row, log_total, grad_rows):
    query_heads, key_heads, bent, masked = scores_of(queries, key_rows, first_row, query_pos)
    head_count = query_heads.shape[1]
    value_heads = value_rows.reshape(value_rows.shape[0], head_count, HEAD_SIZE)
    grad_heads = grad_rows.reshape(queries.shape[0], head_count, HEAD_SIZE)
    probability = jnp.exp(masked - log_total[..., None])
    prob_low = probability.astype(jnp.bfloat16)
    grad_value = jnp.einsum(
        "hqk,qhd->khd", prob_low, grad_heads, preferred_element_type=jnp.float32
    )
    grad_prob = jnp.einsum(
        "qhd,khd->hqk", grad_heads, value_heads, preferred_element_type=jnp.float32
    )
    delta = jnp.sum(probability * grad_prob, axis=-1, keepdims=True)
    grad_scores = (probability * (grad_prob - delta) * (1.0 - bent * bent)).astype(jnp.bfloat16)
    grad_query = jnp.einsum(
        "hqk,khd->qhd", grad_scores, key_heads, preferred_element_type=jnp.float32
    ) * HEAD_SIZE ** (-0.5)
    grad_key = jnp.einsum(
        "hqk,qhd->khd", grad_scores, query_heads, preferred_element_type=jnp.float32
    ) * HEAD_SIZE ** (-0.5)
    key_count = key_rows.shape[0]
    return (
        grad_query.reshape(queries.shape[0], head_count * HEAD_SIZE),
        grad_key.reshape(key_count, head_count * HEAD_SIZE),
        grad_value.reshape(key_count, head_count * HEAD_SIZE),
    )


def general_local(
    inputs,
    positions,
    query_weight,
    key_weight,
    value_weight,
    output_weight,
    gate_weight,
    up_weight,
    down_weight,
    pre_attn_gain,
    post_attn_gain,
    pre_ffn_gain,
    post_ffn_gain,
    cotangent,
):
    seqs, tokens, width = inputs.shape
    block_len = positions.shape[1]
    full_len = block_len * lax.axis_size("ctx")
    offset = lax.axis_index("ctx") * block_len
    head_count = QUERY_HEAD_COUNT // lax.axis_size("seq")
    key_value_group = QUERY_HEAD_COUNT // KEY_VALUE_HEADS
    kv_heads = max(head_count // key_value_group, 1)
    kv_cols = kv_heads * HEAD_SIZE
    repeat_by = head_count // kv_heads
    head_cols = head_count * HEAD_SIZE
    key_value_begin = lax.axis_index("seq") * head_count // key_value_group * HEAD_SIZE
    cosine, sine = angle_tables(positions)
    gain_table = jnp.stack([pre_attn_gain, post_attn_gain, pre_ffn_gain, post_ffn_gain], axis=1)
    fwd_attn = load_attention(
        query_weight, key_weight, value_weight, output_weight, gain_table, key_value_begin, kv_cols
    )
    fwd_ffn = load_ffn(gate_weight, up_weight, down_weight)
    w_query, key_matrix, value_matrix, w_output, gain_full = fwd_attn
    w_gate, w_up, w_down = fwd_ffn
    gain_float = gain_full.astype(jnp.float32)
    gain_one = gain_float[:, 0]
    gain_two = gain_float[:, 1]
    gain_three = gain_float[:, 2]
    gain_four = gain_float[:, 3]
    x_float = inputs.astype(jnp.float32)
    normed_one = norm_gain(x_float, gain_one).astype(jnp.bfloat16)
    block_one = block_rows(normed_one)
    query_raw = jnp.einsum("srd,de->sre", block_one, w_query, preferred_element_type=jnp.float32)
    key_raw = jnp.einsum("srd,de->sre", block_one, key_matrix, preferred_element_type=jnp.float32)
    value_raw = jnp.einsum(
        "srd,de->sre", block_one, value_matrix, preferred_element_type=jnp.float32
    )
    query_rot = (
        turn(query_raw.reshape(seqs, block_len, head_count, HEAD_SIZE), cosine, sine)
        .astype(jnp.bfloat16)
        .reshape(seqs, block_len, head_cols)
    )
    key_rot = (
        turn(key_raw.reshape(seqs, block_len, kv_heads, HEAD_SIZE), cosine, sine)
        .astype(jnp.bfloat16)
        .reshape(seqs, block_len, kv_cols)
    )
    key_all, value_all = (
        lax.all_gather(key_rot, "ctx", axis=1, tiled=True),
        lax.all_gather(value_raw.astype(jnp.bfloat16), "ctx", axis=1, tiled=True),
    )
    key_broadcast = jnp.repeat(
        key_all.reshape(seqs, full_len, kv_heads, HEAD_SIZE), repeat_by, axis=2
    ).reshape(seqs, full_len, head_cols)
    value_broadcast = jnp.repeat(
        value_all.reshape(seqs, full_len, kv_heads, HEAD_SIZE), repeat_by, axis=2
    ).reshape(seqs, full_len, head_cols)
    query_block = math.gcd(block_len, 512)
    block_count = block_len // query_block
    item_count = seqs * block_count
    item_index = jnp.arange(item_count, dtype=jnp.int32)
    block_starts = offset + item_index % block_count * query_block
    seq_owner = item_index // block_count

    def forward_item(pieces):
        queries, query_pos, first_row, seq_id = pieces
        key_rows = lax.dynamic_index_in_dim(key_broadcast, seq_id, 0, keepdims=False)
        value_rows = lax.dynamic_index_in_dim(value_broadcast, seq_id, 0, keepdims=False)
        return attend_forward(queries, key_rows, value_rows, query_pos, first_row)

    head_items, log_total = lax.map(forward_item, (query_rot, positions, block_starts, seq_owner))
    out_full = full_output(w_output)
    heads_tok = lax.all_to_all(head_items, "seq", split_axis=1, concat_axis=2, tiled=True)
    project = jnp.einsum("ste,ed->std", heads_tok, out_full, preferred_element_type=jnp.float32)
    middle = x_float + norm_gain(project, gain_two)
    normed_two = norm_gain(middle, gain_three).astype(jnp.bfloat16)
    ffn_input = block_rows(normed_two)
    gate = jnp.einsum("srd,df->srf", ffn_input, w_gate, preferred_element_type=jnp.float32)
    upper = jnp.einsum("srd,df->srf", ffn_input, w_up, preferred_element_type=jnp.float32)
    hidden = geglu(gate, upper).astype(jnp.bfloat16)
    feed = row_total(jnp.einsum("srf,fd->srd", hidden, w_down, preferred_element_type=jnp.float32))
    layer_output = (middle + norm_gain(feed, gain_four)).astype(jnp.bfloat16)
    back_attn = load_attention(
        query_weight, key_weight, value_weight, output_weight, gain_table, key_value_begin, kv_cols
    )
    back_ffn = load_ffn(gate_weight, up_weight, down_weight)
    bq_weight, bk_weight, bv_weight, bo_weight = (
        back_attn[0],
        back_attn[1],
        back_attn[2],
        back_attn[3],
    )
    bgate_weight, bup_weight, bdown_weight = back_ffn
    grad_top = cotangent.astype(jnp.float32)
    unused, pull_four = jax.vjp(norm_gain, feed, gain_four)
    grad_feed, grad_g_four = pull_four(grad_top)
    grad_feed_rows = block_rows(grad_feed.astype(jnp.bfloat16))
    grad_hidden = jnp.einsum(
        "srd,fd->srf", grad_feed_rows, bdown_weight, preferred_element_type=jnp.float32
    )
    grad_down_part = jnp.einsum(
        "srf,srd->fd", hidden, grad_feed_rows, preferred_element_type=jnp.float32
    )
    unused, pull_act = jax.vjp(geglu, gate, upper)
    grad_gate_act, grad_up_act = pull_act(grad_hidden)
    grad_gate_act = grad_gate_act.astype(jnp.bfloat16)
    grad_up_act = grad_up_act.astype(jnp.bfloat16)
    grad_rows_part = jnp.einsum(
        "srf,df->srd", grad_gate_act, bgate_weight, preferred_element_type=jnp.float32
    ) + jnp.einsum("srf,df->srd", grad_up_act, bup_weight, preferred_element_type=jnp.float32)
    grad_gate_part = jnp.einsum(
        "srd,srf->df", ffn_input, grad_gate_act, preferred_element_type=jnp.float32
    )
    grad_up_part = jnp.einsum(
        "srd,srf->df", ffn_input, grad_up_act, preferred_element_type=jnp.float32
    )
    ffn_grads = (
        lax.psum_scatter(
            grad_gate_part.astype(jnp.bfloat16), ("dp", "ctx"), scatter_dimension=0, tiled=True
        ).astype(jnp.float32),
        lax.psum_scatter(
            grad_up_part.astype(jnp.bfloat16), ("dp", "ctx"), scatter_dimension=0, tiled=True
        ).astype(jnp.float32),
        lax.psum_scatter(
            grad_down_part.astype(jnp.bfloat16), ("dp", "ctx"), scatter_dimension=1, tiled=True
        ).astype(jnp.float32),
    )
    grad_normed_two = row_total(grad_rows_part)
    unused, pull_three = jax.vjp(norm_gain, middle, gain_three)
    grad_mid_norm, grad_g_three = pull_three(grad_normed_two)
    grad_middle = grad_top + grad_mid_norm
    unused, pull_two = jax.vjp(norm_gain, project, gain_two)
    grad_project, grad_g_two = pull_two(grad_middle)
    grad_project = grad_project.astype(jnp.bfloat16)
    out_back = full_output(bo_weight)
    grad_heads_tok = jnp.einsum(
        "std,ed->ste", grad_project, out_back, preferred_element_type=jnp.float32
    ).astype(jnp.bfloat16)
    grad_output_part = lax.psum_scatter(
        jnp.einsum(
            "ste,std->ed", heads_tok, grad_project, preferred_element_type=jnp.float32
        ).astype(jnp.bfloat16),
        "seq",
        scatter_dimension=0,
        tiled=True,
    )
    grad_heads = lax.all_to_all(grad_heads_tok, "seq", split_axis=2, concat_axis=1, tiled=True)

    def backward_item(carry, pieces):
        key_acc, value_acc = carry
        queries, query_pos, first_row, seq_id, log_part, grad_part = pieces
        key_rows = lax.dynamic_index_in_dim(key_broadcast, seq_id, 0, keepdims=False)
        value_rows = lax.dynamic_index_in_dim(value_broadcast, seq_id, 0, keepdims=False)
        grad_query, grad_key, grad_value = attend_backward(
            queries, key_rows, value_rows, query_pos, first_row, log_part, grad_part
        )
        key_acc = lax.dynamic_update_index_in_dim(
            key_acc,
            lax.dynamic_index_in_dim(key_acc, seq_id, 0, keepdims=False) + grad_key,
            seq_id,
            0,
        )
        value_acc = lax.dynamic_update_index_in_dim(
            value_acc,
            lax.dynamic_index_in_dim(value_acc, seq_id, 0, keepdims=False) + grad_value,
            seq_id,
            0,
        )
        return ((key_acc, value_acc), grad_query)

    empty = jnp.zeros((seqs, full_len, head_cols), jnp.float32)
    (key_terms, value_terms), grad_query_items = lax.scan(
        backward_item,
        (empty, empty),
        (query_rot, positions, block_starts, seq_owner, log_total, grad_heads),
    )
    key_sums, value_sums = (
        lax.psum_scatter(
            key_terms.astype(jnp.bfloat16), "ctx", scatter_dimension=1, tiled=True
        ).astype(jnp.float32),
        lax.psum_scatter(
            value_terms.astype(jnp.bfloat16), "ctx", scatter_dimension=1, tiled=True
        ).astype(jnp.float32),
    )
    grad_query_rot = rounded(grad_query_items.reshape(seqs, block_len, head_count, HEAD_SIZE))
    grad_query_raw = (
        turn_back(grad_query_rot, cosine, sine)
        .astype(jnp.bfloat16)
        .reshape(seqs, block_len, head_cols)
    )
    grad_key_rot = rounded(key_sums.reshape(seqs, block_len, head_count, HEAD_SIZE))
    grad_key_raw = (
        turn_back(grad_key_rot, cosine, sine)
        .astype(jnp.bfloat16)
        .reshape(seqs, block_len, head_cols)
    )
    grad_value_raw = value_sums.astype(jnp.bfloat16)
    key_expand = jnp.repeat(
        bk_weight.reshape(width, kv_heads, HEAD_SIZE), repeat_by, axis=1
    ).reshape(width, head_cols)
    value_expand = jnp.repeat(
        bv_weight.reshape(width, kv_heads, HEAD_SIZE), repeat_by, axis=1
    ).reshape(width, head_cols)
    grad_block_one = jnp.einsum(
        "sre,de->srd", grad_query_raw, bq_weight, preferred_element_type=jnp.float32
    )
    grad_block_one = grad_block_one + jnp.einsum(
        "sre,de->srd", grad_key_raw, key_expand, preferred_element_type=jnp.float32
    )
    grad_block_one = grad_block_one + jnp.einsum(
        "sre,de->srd", grad_value_raw, value_expand, preferred_element_type=jnp.float32
    )
    grad_normed_one = row_total(grad_block_one)
    grad_query_part = jnp.einsum(
        "srd,sre->de", block_one, grad_query_raw, preferred_element_type=jnp.float32
    )
    grad_key_wide = jnp.einsum(
        "srd,sre->de", block_one, grad_key_raw, preferred_element_type=jnp.float32
    )
    grad_value_wide = jnp.einsum(
        "srd,sre->de", block_one, grad_value_raw, preferred_element_type=jnp.float32
    )
    grad_key_part = jnp.sum(
        grad_key_wide.reshape(width, kv_heads, repeat_by, HEAD_SIZE), axis=2
    ).reshape(width, kv_cols)
    grad_value_part = jnp.sum(
        grad_value_wide.reshape(width, kv_heads, repeat_by, HEAD_SIZE), axis=2
    ).reshape(width, kv_cols)
    unused, pull_one = jax.vjp(norm_gain, x_float, gain_one)
    grad_input_norm, grad_g_one = pull_one(grad_normed_one)
    input_grad = (grad_middle + grad_input_norm).astype(jnp.bfloat16)
    gain_grads = jnp.stack([grad_g_one, grad_g_two, grad_g_three, grad_g_four], axis=1)
    attention_gradients = (
        lax.psum_scatter(
            grad_query_part.astype(jnp.bfloat16), ("dp", "ctx"), scatter_dimension=0, tiled=True
        ).astype(jnp.float32),
        lax.psum_scatter(grad_output_part, ("dp", "ctx"), scatter_dimension=1, tiled=True).astype(
            jnp.float32
        ),
    )
    key_spread = lax.dynamic_update_slice_in_dim(
        jnp.zeros((width, KEY_VALUE_HEADS * HEAD_SIZE), jnp.float32),
        grad_key_part,
        key_value_begin,
        1,
    )
    value_spread = lax.dynamic_update_slice_in_dim(
        jnp.zeros((width, KEY_VALUE_HEADS * HEAD_SIZE), jnp.float32),
        grad_value_part,
        key_value_begin,
        1,
    )
    kv_sums = (
        lax.psum_scatter(key_spread, ("dp", "ctx", "seq"), scatter_dimension=0, tiled=True),
        lax.psum_scatter(value_spread, ("dp", "ctx", "seq"), scatter_dimension=0, tiled=True),
        lax.psum_scatter(gain_grads, ("dp", "ctx", "seq"), scatter_dimension=0, tiled=True),
    )
    gain_out = kv_sums[2]
    return (
        layer_output,
        input_grad,
        attention_gradients[0],
        kv_sums[0],
        kv_sums[1],
        attention_gradients[1],
        ffn_grads[0],
        ffn_grads[1],
        ffn_grads[2],
        gain_out[:, 0],
        gain_out[:, 1],
        gain_out[:, 2],
        gain_out[:, 3],
    )


def flip(value, axis):
    return lax.ppermute(value, axis, [(0, 1), (1, 0)])


def ordered(index, own, other, axis=0):
    return jnp.where(
        index == 0, jnp.stack([own, other], axis=axis), jnp.stack([other, own], axis=axis)
    )


def pick(value, index, axis=0):
    return lax.dynamic_index_in_dim(value, index, axis, keepdims=False)


def after(value, *earlier):
    return lax.optimization_barrier((value, *earlier))[0]


def total(kept, *got):
    value = kept.astype(jnp.float32)
    for more in got:
        value = value + more.astype(jnp.float32)
    return value


def trade_sequences(value):
    cy = lax.axis_index("cy")
    return ordered(cy, pick(value, cy), flip(pick(value, 1 - cy), "cy"))


def core_columns(matrices, core):
    parts = []
    for matrix, begin, width in matrices:
        at = core * (matrix.shape[1] // 2) + begin
        parts.append(lax.dynamic_slice_in_dim(matrix, at, width, 1))
    return jnp.concatenate(parts, axis=1) if len(parts) > 1 else parts[0]


def start_gather(*matrices):
    c = lax.axis_index("core")
    got = flip(core_columns(matrices, 1 - c), "core")
    rows = ordered(c, core_columns(matrices, c), got)
    return rows, flip(rows, "cy"), flip(rows, "dp")


def next_gather(rows, rows_y, rows_x):
    return rows, rows_y, rows_x, flip(rows_y[0], "dp"), flip(rows_x[1], "cy")


def place_kernel(moves, count, *refs):
    sources, outs = refs[:count], refs[count : len(refs) - count - 2]
    held, sem_in, sem_out = refs[-count - 2 : -2], refs[-2], refs[-1]
    x, y = lax.axis_index("dp"), lax.axis_index("cy")
    loads = [
        pltpu.make_async_copy(source, buffer, sem_in.at[i])
        for i, (source, buffer) in enumerate(zip(sources, held))
    ]
    for load in loads:
        load.start()
    stores = []
    for i, (load, buffer) in enumerate(zip(loads, held)):
        load.wait()
        for out, begin, to, cols in moves[i // 5]:
            out, to = outs[out], pl.ds(to, cols)
            target = (
                out.at[x, y, :, :, to],
                out.at[x, 1 - y, :, :, to],
                out.at[1 - x, y, :, :, to],
                out.at[1 - x, 1 - y, 0, :, to],
                out.at[1 - x, 1 - y, 1, :, to],
            )[i % 5]
            at = pl.ds(begin, cols)
            piece = buffer.at[:, :, at] if i % 5 < 3 else buffer.at[:, at]
            stores.append(pltpu.make_async_copy(piece, target, sem_out.at[len(stores)]))
            stores[-1].start()
    for store in stores:
        store.wait()


def end_gather(gathers, moves, widths):
    pieces = [piece for begun in gathers for piece in begun]
    rows, low = pieces[0].shape[1], pieces[0].dtype
    size = 8 * rows * sum(widths) * low.itemsize
    anywhere = pl.BlockSpec(memory_space=pl.ANY)
    stores = 5 * sum(len(some) for some in moves)
    outs = pl.pallas_call(
        functools.partial(place_kernel, moves, len(pieces)),
        out_shape=[jax.ShapeDtypeStruct((2, 2, 2, rows, width), low) for width in widths],
        in_specs=[anywhere] * len(pieces),
        out_specs=[anywhere] * len(widths),
        scratch_shapes=[pltpu.VMEM(piece.shape, low) for piece in pieces]
        + [pltpu.SemaphoreType.DMA((len(pieces),)), pltpu.SemaphoreType.DMA((stores,))],
        compiler_params=pltpu.CompilerParams(vmem_limit_bytes=size + (2 << 20)),
        cost_estimate=pl.CostEstimate(flops=0, bytes_accessed=2 * size, transcendentals=0),
        name="place_rows",
    )(*pieces)
    return [out.reshape(-1, out.shape[-1]) for out in outs]


def start_scatter(grad):
    x, y = lax.axis_index("dp"), lax.axis_index("cy")
    parts = grad.reshape(2, 2, 2, -1, grad.shape[-1])
    return parts, pick(parts, 1 - x)[:, 0], pick(parts, 1 - y, 1)[:, 1]


def send_scatter(parts, by_x, by_y):
    return parts, flip(by_x, "dp"), flip(by_y, "cy")


def next_scatter(parts, from_x, from_y):
    x, y = lax.axis_index("dp"), lax.axis_index("cy")
    by_y = total(pick(pick(parts, x), 1 - y)[0], pick(from_x, 1 - y)).astype(parts.dtype)
    by_x = total(pick(pick(parts, 1 - x), y)[1], pick(from_y, 1 - x)).astype(parts.dtype)
    return parts, from_x, from_y, flip(by_y, "cy"), flip(by_x, "dp")


def end_scatter(parts, from_x, from_y, last_y, last_x):
    x, y, c = lax.axis_index("dp"), lax.axis_index("cy"), lax.axis_index("core")
    own = pick(pick(parts, x), y)
    first = total(own[0], pick(from_x, y), last_y)
    second = total(own[1], pick(from_y, x), last_x)
    keep = jnp.where(c == 0, first, second)
    away = jnp.where(c == 0, second, first).astype(jnp.bfloat16)
    got = flip(away, "core").astype(jnp.float32)
    return jnp.where(c == 0, keep, got), jnp.where(c == 0, got, keep)


def gather_gains(table):
    table = ordered(lax.axis_index("core"), table, flip(table, "core"), axis=1)
    table = ordered(lax.axis_index("cy"), table, flip(table, "cy"), axis=1)
    table = ordered(lax.axis_index("dp"), table, flip(table, "dp"), axis=1)
    return table.reshape(table.shape[0], -1)


def exchange_seq(parts):
    z, size = lax.axis_index("seq"), lax.axis_size("seq")
    got = [pick(parts, z)]
    for step in range(1, size):
        ring = [(i, (i + step) % size) for i in range(size)]
        got.insert(0, lax.ppermute(pick(parts, lax.rem(z + step, size)), "seq", ring))
    got = jnp.stack(got + got[:-1])
    return lax.dynamic_slice_in_dim(got, size - 1 - z, size, 0)


def shift(value, step):
    size = lax.axis_size("seq")
    return lax.ppermute(value, "seq", [(i, (i + step) % size) for i in range(size)])


def gather_rows(local_rows):
    size = lax.axis_size("seq")
    got = {step: shift(local_rows, step) for step in (1, 3, 2)}
    pieces = [local_rows] + [got[size - ahead] for ahead in range(1, size)]
    return jnp.concatenate(pieces + [flip(piece, "core") for piece in pieces])


def join_kernel(whole, out, held, sem):
    c, z = lax.axis_index("core"), lax.axis_index("seq")
    size, rows = whole.shape[0] // 2, whole.shape[1]
    loads = []
    for i in range(2 * size):
        owner = (c if i < size else 1 - c) * size + lax.rem(z + i % size, size)
        target = held.at[pl.ds(i * rows, rows)]
        loads.append(pltpu.make_async_copy(whole.at[owner], target, sem.at[i]))
    for load in loads:
        load.start()
    for load in loads:
        load.wait()
    store = pltpu.make_async_copy(held, out, sem.at[2 * size])
    store.start()
    store.wait()


def gather_first(local_rows):
    whole = lax.all_gather(local_rows, ("core", "seq"), axis=0)
    shape, low = (whole.shape[0] * whole.shape[1], whole.shape[2]), whole.dtype
    size = whole.size * low.itemsize
    anywhere = pl.BlockSpec(memory_space=pl.ANY)
    return pl.pallas_call(
        join_kernel,
        out_shape=jax.ShapeDtypeStruct(shape, low),
        in_specs=[anywhere],
        out_specs=anywhere,
        scratch_shapes=[
            pltpu.VMEM(shape, low),
            pltpu.SemaphoreType.DMA((whole.shape[0] + 1,)),
        ],
        compiler_params=pltpu.CompilerParams(vmem_limit_bytes=size + (2 << 20)),
        cost_estimate=pl.CostEstimate(flops=0, bytes_accessed=2 * size, transcendentals=0),
        name="join_rows",
    )(whole)


def row_tokens(rows, length):
    c, z, size = lax.axis_index("core"), lax.axis_index("seq"), lax.axis_size("seq")
    shape = (2, size, 2, rows // 2)
    core = jnp.where(lax.broadcasted_iota(jnp.int32, shape, 0) == 0, c, 1 - c)
    owner = lax.rem(z + lax.broadcasted_iota(jnp.int32, shape, 1), size)
    begin = lax.broadcasted_iota(jnp.int32, shape, 2) * (length // 2)
    row = lax.broadcasted_iota(jnp.int32, shape, 3)
    return (begin + (core * size + owner) * (rows // 2) + row).reshape(-1)


def row_order(values):
    c, z, size = lax.axis_index("core"), lax.axis_index("seq"), lax.axis_size("seq")
    parts = values.reshape(2, 2, size, -1).transpose(1, 2, 0, 3)
    parts = jnp.stack([pick(parts, c), pick(parts, 1 - c)])
    parts = jnp.concatenate([parts, parts], axis=1)
    return lax.dynamic_slice_in_dim(parts, z, size, 1).reshape(-1)


def core_swap(value):
    half = value.shape[0] // 2
    got = flip(value, "core")
    return jnp.concatenate([got[half:], got[:half]])


def core_rows(left, right, dims):
    half = left.shape[0] // 2
    got = flip(dot(left[half:], right, dims).astype(jnp.bfloat16), "core")
    kept = lax.optimization_barrier(dot(left[:half], right, dims).astype(jnp.bfloat16))
    return total(kept, got).astype(jnp.bfloat16)


def core_sums(partial_rows):
    half = partial_rows.shape[0] // 2
    return total(partial_rows[:half], flip(partial_rows[half:], "core")).astype(jnp.bfloat16)


def scatter_rows(sums):
    size = lax.axis_size("seq")
    parts = sums.reshape(size, -1, sums.shape[-1])
    got = [shift(parts[step], step) for step in (3, 1, 2)]
    return total(parts[0], *got)


def chip_rows(*matrices):
    c = lax.axis_index("core")
    got = flip(core_columns(matrices, 1 - c), "core")
    return ordered(c, core_columns(matrices, c), got)


def gather_chips(rows):
    whole = lax.all_gather(rows.reshape(-1, rows.shape[-1]), ("dp", "cy"), axis=0, tiled=True)
    return whole


def scatter_chips(grad):
    sums = lax.psum_scatter(grad, ("dp", "cy"), scatter_dimension=0, tiled=True)
    return sums.reshape(2, -1, sums.shape[-1])


def both_columns(sums):
    c = lax.axis_index("core")
    keep = pick(sums, c).astype(jnp.float32)
    got = flip(pick(sums, 1 - c), "core").astype(jnp.float32)
    return jnp.where(c == 0, keep, got), jnp.where(c == 0, got, keep)


def dot(left, right, dims):
    return lax.dot_general(
        left, right, ((dims[:1], dims[1:]), ((), ())), preferred_element_type=jnp.float32
    )


def head_scores(queries, keys, visible):
    bent = jnp.tanh(dot(queries, keys, (1, 1)) * (HEAD_SIZE ** (-0.5) / CAP))
    return bent, jnp.where(visible, CAP * bent, -1e30)


def head_local(
    inputs,
    positions,
    query_weight,
    key_weight,
    value_weight,
    output_weight,
    gate_weight,
    up_weight,
    down_weight,
    pre_attn_gain,
    post_attn_gain,
    pre_ffn_gain,
    post_ffn_gain,
    cotangent,
):
    c, cy = lax.axis_index("core"), lax.axis_index("cy")
    low = jnp.bfloat16
    rows_own = query_weight.shape[0]
    ffn_cols = gate_weight.shape[1] // 2

    kv_stack = jnp.stack([key_weight, value_weight], axis=1)
    kv_stack = kv_stack.reshape(-1, 2, KEY_VALUE_HEADS, HEAD_SIZE).transpose(2, 0, 1, 3)
    kv_rows = exchange_seq(kv_stack).reshape(rows_own, 2 * HEAD_SIZE)
    x_local = after(trade_sequences(inputs), kv_rows)
    own_shape = x_local.shape
    x_local = x_local.reshape(-1, x_local.shape[-1])
    block_x = gather_first(x_local)
    x_float = x_local.astype(jnp.float32)
    gain_table = jnp.stack([pre_attn_gain, post_attn_gain, pre_ffn_gain, post_ffn_gain], axis=0)
    gain_one, gain_two, gain_three, gain_four = gather_gains(gain_table).astype(jnp.float32)

    pos_own = trade_sequences(positions)
    seq_pos = ordered(c, pos_own, flip(pos_own, "core"), axis=1).reshape(-1)
    half = HEAD_SIZE // 2
    freq = BASE ** (-jnp.arange(half, dtype=jnp.float32) * 2.0 / HEAD_SIZE)
    token = row_tokens(x_local.shape[0], seq_pos.shape[0])
    seq_pos = row_order(seq_pos)
    angle = seq_pos.astype(jnp.float32)[:, None] * freq
    cosine, sine = jnp.cos(angle), jnp.sin(angle)
    kv_cosine = jnp.where(c == 0, cosine, 1.0)
    kv_sine = jnp.where(c == 0, sine, 0.0)

    attn_begun = next_gather(
        *start_gather(
            (query_weight, 0, HEAD_SIZE), (kv_rows, 0, HEAD_SIZE), (output_weight.T, 0, HEAD_SIZE)
        )
    )
    split = 2 * HEAD_SIZE
    in_weight, out_weight = end_gather(
        [attn_begun], [((0, 0, 0, split), (1, split, 0, HEAD_SIZE))], (split, HEAD_SIZE)
    )
    gate_up_rows = chip_rows((gate_weight, 0, ffn_cols), (up_weight, 0, ffn_cols))
    gate_up_weight = gather_chips(gate_up_rows)
    down_back = gather_chips(chip_rows((down_weight.T, 0, ffn_cols)))
    grad_top = trade_sequences(after(cotangent, attn_begun))

    block_one = norm_gain(block_x.astype(jnp.float32), gain_one).astype(low)
    raw = dot(block_one, in_weight, (1, 0))
    queries = turn(raw[:, :HEAD_SIZE], cosine, sine).astype(low)
    kv_own = turn(raw[:, HEAD_SIZE:], kv_cosine, kv_sine).astype(low)
    kv_other = core_swap(kv_own)
    keys = jnp.where(c == 0, kv_own, kv_other)
    values = jnp.where(c == 0, kv_other, kv_own)
    visible = (token[None, :] <= token[:, None]) & (token[None, :] >= (token - seq_pos)[:, None])
    bent, masked = head_scores(queries, keys, visible)
    row_max = jnp.max(masked, axis=-1, keepdims=True)
    exponent = jnp.exp(masked - row_max)
    row_sum = jnp.sum(exponent, axis=-1, keepdims=True)
    heads = dot((exponent / row_sum).astype(low), values, (1, 0)).astype(low)
    log_total = row_max + jnp.log(row_sum)
    heads = after(heads, grad_top)
    grad_top = grad_top.reshape(x_local.shape).astype(jnp.float32)

    project_core = core_sums(dot(heads, out_weight, (1, 1)).astype(low))
    project = scatter_rows(project_core)
    middle = x_float + norm_gain(project, gain_two)
    normed_two = norm_gain(middle, gain_three).astype(low)
    block_two = gather_rows(normed_two)
    gate_up = dot(block_two, gate_up_weight, (1, 0))
    gate, upper = gate_up[:, :ffn_cols], gate_up[:, ffn_cols:]
    hidden = geglu(gate, upper).astype(low)
    feed = scatter_rows(core_rows(hidden, down_back, (1, 1)))
    unused, pull_four = jax.vjp(norm_gain, feed, gain_four)
    grad_feed, grad_g_four = pull_four(grad_top)
    grad_feed = grad_feed.astype(low)
    layer_output = after((middle + norm_gain(feed, gain_four)).astype(low), grad_feed)
    layer_output = trade_sequences(layer_output.reshape(own_shape))

    grad_feed_rows = after(gather_rows(grad_feed), layer_output)
    grad_hidden = dot(grad_feed_rows, down_back, (1, 0))
    unused, pull_act = jax.vjp(geglu, gate, upper)
    grad_gate_act, grad_up_act = pull_act(grad_hidden)
    grad_gate_up = jnp.concatenate([grad_gate_act.astype(low), grad_up_act.astype(low)], axis=1)
    normed_two_core = core_sums(dot(grad_gate_up, gate_up_weight, (1, 1)).astype(low))
    grad_normed_two = scatter_rows(normed_two_core)
    late = after((hidden, block_two), normed_two_core)
    grad_down = dot(grad_feed_rows, late[0], (0, 0)).astype(low)
    grad_gu = dot(late[1], grad_gate_up, (0, 0)).astype(low)
    grad_normed_two = after(grad_normed_two, grad_down, grad_gu)
    grad_down, grad_gu = scatter_chips(grad_down), scatter_chips(grad_gu)

    unused, pull_three = jax.vjp(norm_gain, middle, gain_three)
    grad_mid_norm, grad_g_three = pull_three(grad_normed_two)
    grad_middle = grad_top + grad_mid_norm
    unused, pull_two = jax.vjp(norm_gain, project, gain_two)
    grad_project, grad_g_two = pull_two(grad_middle)
    grad_project = grad_project.astype(low)
    grad_project_rows = gather_rows(grad_project)
    grad_heads = dot(grad_project_rows, out_weight, (1, 0)).astype(low)

    bent, masked = head_scores(queries, keys, visible)
    probability = jnp.exp(masked - log_total)
    grad_value = dot(probability.astype(low), grad_heads, (0, 0)).astype(low)
    grad_prob = dot(grad_heads, values, (1, 1))
    delta = jnp.sum(probability * grad_prob, axis=-1, keepdims=True)
    grad_scores = (probability * (grad_prob - delta) * (1.0 - bent * bent)).astype(low)
    scale = HEAD_SIZE ** (-0.5)
    grad_query_rot = rounded(dot(grad_scores, keys, (1, 0)) * scale)
    grad_key_rot = rounded(dot(grad_scores, queries, (0, 0)) * scale)
    grad_query_raw = turn_back(grad_query_rot, cosine, sine).astype(low)
    grad_key_raw = turn_back(grad_key_rot, cosine, sine).astype(low)
    kv_grad_own = jnp.where(c == 0, grad_key_raw, grad_value)
    kv_grad_got = core_swap(jnp.where(c == 0, grad_value, grad_key_raw))
    grad_in = jnp.concatenate([grad_query_raw, total(kv_grad_own, kv_grad_got).astype(low)], axis=1)
    normed_one_part = dot(grad_in, in_weight, (1, 1)).astype(low)
    normed_one_core = core_sums(normed_one_part)
    grad_normed_one = scatter_rows(normed_one_core)
    block_one, heads = after((block_one, heads), normed_one_core)
    grad_in_part = dot(block_one, grad_in, (0, 0)).astype(low)
    grad_output_part = dot(grad_project_rows, heads, (0, 0)).astype(low)
    attn_grad_begun = start_scatter(jnp.concatenate([grad_in_part, grad_output_part], axis=1))
    attn_grad_begun = send_scatter(*attn_grad_begun)
    grad_normed_one = after(grad_normed_one, attn_grad_begun)
    attn_grad_begun = next_scatter(*attn_grad_begun)
    attn_grads = end_scatter(*attn_grad_begun)
    grad_down, grad_gu = after((grad_down, grad_gu), attn_grad_begun)
    grad_down, grad_gu = both_columns(grad_down), both_columns(grad_gu)

    block_x = after(block_x, attn_grad_begun[0]).astype(jnp.float32)
    unused, pull_gain = jax.vjp(lambda gain: norm_gain(block_x, gain), gain_one)
    (grad_g_one,) = pull_gain(normed_one_part.astype(jnp.float32))
    everyone = ("dp", "cy", "core", "seq")
    gain_grads = jnp.stack([grad_g_one, grad_g_two, grad_g_three, grad_g_four], axis=0)
    gain_grads = after(gain_grads, grad_normed_one, attn_grad_begun)
    gain_parts = gain_grads.reshape(4, lax.axis_size(everyone), -1).transpose(1, 0, 2)
    gain_out = jnp.sum(
        lax.all_to_all(gain_parts, everyone, split_axis=0, concat_axis=0, tiled=True), axis=0
    )

    unused, pull_one = jax.vjp(lambda rows: norm_gain(rows, gain_one), x_float)
    (grad_input_norm,) = pull_one(grad_normed_one)
    input_grad = trade_sequences((grad_middle + grad_input_norm).astype(low).reshape(own_shape))

    def whole(pair, begin, cols):
        return jnp.concatenate([part[:, begin : begin + cols] for part in pair], axis=1)

    kv_back = whole(attn_grads, HEAD_SIZE, HEAD_SIZE).astype(low)
    kv_back = exchange_seq(kv_back.reshape(KEY_VALUE_HEADS, -1, 2 * HEAD_SIZE))
    kv_back = kv_back.reshape(KEY_VALUE_HEADS, -1, 2, HEAD_SIZE).transpose(2, 1, 0, 3)
    kv_back = kv_back.reshape(2, -1, KEY_VALUE_HEADS * HEAD_SIZE).astype(jnp.float32)
    return (
        layer_output,
        input_grad,
        whole(attn_grads, 0, HEAD_SIZE),
        kv_back[0],
        kv_back[1],
        whole(attn_grads, 2 * HEAD_SIZE, HEAD_SIZE).T,
        whole(grad_gu, 0, ffn_cols),
        whole(grad_gu, ffn_cols, ffn_cols),
        whole(grad_down, 0, ffn_cols).T,
        gain_out[0],
        gain_out[1],
        gain_out[2],
        gain_out[3],
    )


def one_head_each(mesh):
    sizes = mesh.shape
    return (
        sizes["dp"] == 2
        and sizes["ctx"] == 4
        and sizes["seq"] == KEY_VALUE_HEADS
        and QUERY_HEAD_COUNT == 2 * KEY_VALUE_HEADS
    )


def solution(mesh):
    if one_head_each(mesh):
        body, ctx = head_local, ("cy", "core")
        grid = jax.sharding.Mesh(
            mesh.devices.reshape(mesh.shape["dp"], -1, 2, mesh.shape["seq"]),
            ("dp", "cy", "core", "seq"),
        )
    else:
        body, ctx, grid = general_local, ("ctx",), mesh
    owners, everyone = ("dp", *ctx), ("dp", *ctx, "seq")
    rows = P("dp", (*ctx, "seq"), None)
    tall, flat, wide = P(owners, "seq"), P(everyone, None), P("seq", owners)
    gains = (P(owners),) * 4
    return jax.shard_map(
        body,
        mesh=grid,
        in_specs=(rows, P("dp", ctx), tall, flat, flat, wide, tall, tall, wide, *gains, rows),
        out_specs=(rows, rows, tall, flat, flat, wide, tall, tall, wide, *((P(everyone),) * 4)),
        check_vma=False,
    )
```
